32 devices in a mesh: ev: 4 (over x, core), gx: 2 (over y), gy: 4 (over z).
Axes of the slice: x: 2, y: 2, z: 4, core: 2. Of those that a mesh axis runs over, the one named last changes fastest.
Arguments:
- adjoint_now: float32 [8, 3, 16, 32, 128], P('ev', None, 'gx', 'gy'), may hold values from -6 to 6
- adjoint_prev: float32 [8, 3, 16, 32, 128], P('ev', None, 'gx', 'gy'), may hold values from -6 to 6
- forward: bfloat16 [8, 4, 3, 16, 32, 128], P('ev', None, None, 'gx', 'gy'), may hold values from -6 to 6
- medium: float32 [4, 16, 32, 128], P(None, 'gx', 'gy'), may hold values from 0.5 to 2
- drm_cells: int32 [2, 4, 128], P('gx', 'gy'), may hold values from 0 to 8191, as said below
- drm_force: float32 [8, 2, 3, 2, 4, 128], P('ev', None, None, 'gx', 'gy'), may hold values from -320 to 320
Outputs:
- adjoint_mid: float32 [8, 3, 16, 32, 128], P('ev', None, 'gx', 'gy')
- adjoint_next: float32 [8, 3, 16, 32, 128], P('ev', None, 'gx', 'gy')
- grad_shear: float32 [16, 32, 128], P('gx', 'gy', 'ev')
- grad_density: float32 [16, 32, 128], P('gx', 'gy', 'ev')
The draws below stay inside these ranges and needn't reach their ends.
Inputs may be any that keep to these rules, and one draw needn't show every extreme that they name: `drm_cells`: each entry is the local flat index (x * 8 + y) * 128 + z of a cell of its own tile that lies within 2 cells of the grid's bottom or of one of the grid's outer lateral faces; entries may repeat.
All inputs are finite; a program needn't handle non-finite values.
Results may differ from the reference program's by a relative error of at most 0.0011.
Values may be sent and summed in bfloat16 or wider, within the bound.
No kernel may reach another device: no remote copies, remote signals or barrier semaphores. Data moves between devices by JAX's collectives and lax.ppermute only.
A program may use at most 128 MiB of HBM per device.

```python
import math
import jax
import jax.numpy as jnp
from jax import lax

CX = 8
CY = 8
NZ = 128
LAYER = 2
NB = 128
EVENTS = 8
NX = 16
NY = 32
TILES_X = 2
TILES_Y = 4


def draw_drm_cells(key, part):
    key = jax.random.fold_in(key, 7)
    keys = jax.random.split(key, 5)
    shape = (TILES_X, TILES_Y, NB)
    tile_x = jnp.arange(TILES_X)[:, None, None]
    tile_y = jnp.arange(TILES_Y)[None, :, None]
    kind = jax.random.randint(keys[0], shape, 0, 3)
    rim_x = (tile_x == 0) | (tile_x == TILES_X - 1)
    rim_y = (tile_y == 0) | (tile_y == TILES_Y - 1)
    kind = jnp.where((kind == 1) & jnp.logical_not(rim_x), 0, kind)
    kind = jnp.where((kind == 2) & jnp.logical_not(rim_y), 0, kind)
    pos_x = jax.random.randint(keys[1], shape, 0, CX)
    pos_y = jax.random.randint(keys[2], shape, 0, CY)
    pos_z = jax.random.randint(keys[3], shape, 0, NZ)
    layer_pick = jax.random.randint(keys[4], shape, 0, LAYER)
    face_x = jnp.where(tile_x == 0, layer_pick, CX - 1 - layer_pick)
    face_y = jnp.where(tile_y == 0, layer_pick, CY - 1 - layer_pick)
    pos_x = jnp.where(kind == 1, face_x, pos_x)
    pos_y = jnp.where(kind == 2, face_y, pos_y)
    pos_z = jnp.where(kind == 0, layer_pick, pos_z)
    index = (pos_x * CY + pos_y) * NZ + pos_z
    index = index.at[:, :, 0].set(0)
    index = index.at[TILES_X - 1, TILES_Y - 1, 1].set(CX * CY * NZ - 1)
    return index.astype(jnp.int32)


def block_levels(rng, shape, cuts, low, top_value):
    factor_of, own = 1.0, jax.random.fold_in(rng, 6)
    for position, blocks in cuts:
        heights = jnp.exp(jax.random.uniform(jax.random.fold_in(own, position), (blocks,), jnp.float32, low / len(cuts), top_value / len(cuts)))
        factor_of = factor_of * jnp.repeat(heights, shape[position] // blocks).reshape([-1 if axis == position else 1 for axis in range(len(shape))])
    return factor_of


def bell_draw(key, shape, spread, reach, pieces=(), kind=jnp.bfloat16):
    entries = jax.random.normal(key, shape, jnp.float32) * spread
    if len(pieces) > 0:
        entries = block_levels(key, shape, pieces, -0.22, 0.18) * entries
    return jnp.clip(entries, min=-reach, max=reach).astype(kind)


def setup_inputs(seed: int = 0) -> dict:
    arg_keys = jax.random.split(jax.random.key(seed), 7)
    adjoint_now = bell_draw(arg_keys[0], (EVENTS, 3, NX, NY, NZ), 1.0, 6.0, ((0, 4), (2, 2), (3, 4)), jnp.float32)
    adjoint_prev = bell_draw(arg_keys[1], (EVENTS, 3, NX, NY, NZ), 1.0, 6.0, ((0, 4), (2, 2), (3, 4)), jnp.float32)
    forward = bell_draw(arg_keys[2], (EVENTS, 4, 3, NX, NY, NZ), 1.0, 6.0, ((0, 4), (3, 2), (4, 4)))
    medium = jnp.clip(jnp.exp(math.log(2.0) - 1.3862944 * jax.random.uniform(arg_keys[3], (4, NX, NY, NZ), jnp.float32) ** block_levels(arg_keys[3], (4, NX, NY, NZ), ((1, 2), (2, 4)), -0.2, 0.2)), 0.5, 2.0)
    drm_cells = draw_drm_cells(jax.random.fold_in(arg_keys[6], 71), 0)
    drm_force = bell_draw(arg_keys[5], (EVENTS, 2, 3, TILES_X, TILES_Y, NB), 50.0, 320.0, ((0, 4), (3, 2), (4, 4)), jnp.float32)
    return dict(adjoint_now=adjoint_now, adjoint_prev=adjoint_prev, forward=forward, medium=medium, drm_cells=drm_cells, drm_force=drm_force)


STEP_FACTOR = 0.01
UNITS = ((1, 0, 0), (0, 1, 0), (0, 0, 1))


def offset(array, shift_x, shift_y, shift_z):
    size_x, size_y, size_z = array.shape[-3:]
    return array[..., 1 + shift_x:size_x - 1 + shift_x, 1 + shift_y:size_y - 1 + shift_y, 1 + shift_z:size_z - 1 + shift_z]


def negate(vector):
    return tuple(-entry for entry in vector)


def operate(field, medium):
    field_pad = jnp.pad(field, ((0, 0), (0, 0), (0, 0), (0, 0), (1, 1)))
    medium_pad = jnp.pad(medium, ((0, 0), (0, 0), (0, 0), (1, 1)))
    shear = medium_pad[0]
    lame = medium_pad[1]
    inverse = medium_pad[3]
    bulk = lame + shear
    inverse_here = offset(inverse, 0, 0, 0)
    results = []
    for component in range(3):
        displaced = field_pad[:, component]
        total = jnp.zeros(displaced.shape[:1] + inverse_here.shape, jnp.float32)
        for direction in range(3):
            upper = UNITS[direction]
            lower = negate(upper)
            modulus = lame + 2.0 * shear if direction == component else shear
            here = offset(modulus, 0, 0, 0)
            face_up = 0.5 * (here + offset(modulus, *upper))
            face_down = 0.5 * (offset(modulus, *lower) + here)
            if direction == 2:
                face_up = face_up * 0.5 * (inverse_here + offset(inverse, *upper))
                face_down = face_down * 0.5 * (offset(inverse, *lower) + inverse_here)
            centre = offset(displaced, 0, 0, 0)
            term = face_up * (offset(displaced, *upper) - centre) - face_down * (centre - offset(displaced, *lower))
            if direction == 2:
                term = term * inverse_here
            total = total + term
        for other in range(3):
            if other == component:
                continue
            partner = field_pad[:, other]
            values = []
            for sign in (1, -1):
                shift = tuple(sign * entry for entry in UNITS[component])
                plus = tuple(shift[index] + UNITS[other][index] for index in range(3))
                minus = tuple(shift[index] - UNITS[other][index] for index in range(3))
                slope = 0.5 * (offset(partner, *plus) - offset(partner, *minus))
                if other == 2:
                    slope = slope * offset(inverse, *shift)
                values.append(slope * offset(bulk, *shift))
            term = 0.5 * (values[0] - values[1])
            if component == 2:
                term = term * inverse_here
            total = total + term
        results.append(total)
    return jnp.stack(results, axis=1)


def shear_term(adjoint_rim, forward_rim, inverse_own):
    adjoint_pad = jnp.pad(adjoint_rim, ((0, 0), (0, 0), (0, 0), (0, 0), (1, 1)))
    forward_pad = jnp.pad(forward_rim, ((0, 0), (0, 0), (0, 0), (0, 0), (1, 1)))
    total = jnp.zeros(inverse_own.shape, jnp.float32)
    for direction in range(3):
        upper = UNITS[direction]
        lower = negate(upper)
        slope_a = 0.5 * (offset(adjoint_pad, *upper) - offset(adjoint_pad, *lower))
        slope_f = 0.5 * (offset(forward_pad, *upper) - offset(forward_pad, *lower))
        product = jnp.sum(slope_a * slope_f, axis=(0, 1))
        if direction == 2:
            product = product * inverse_own * inverse_own
        total = total - product
    return total


def density_term(adjoint_own, newer, middle, older):
    second = newer.astype(jnp.float32) - 2.0 * middle.astype(jnp.float32) + older.astype(jnp.float32)
    return -jnp.sum(adjoint_own * second, axis=(0, 1))


def pad_lateral(array):
    widths = ((0, 0),) * (array.ndim - 3) + ((1, 1), (1, 1), (0, 0))
    return jnp.pad(array, widths)


def reference(adjoint_now, adjoint_prev, forward, medium, drm_cells, drm_force):
    local_x = drm_cells // (CY * NZ)
    local_y = (drm_cells // NZ) % CY
    local_z = drm_cells % NZ
    tile_x = jnp.arange(TILES_X, dtype=jnp.int32)[:, None, None]
    tile_y = jnp.arange(TILES_Y, dtype=jnp.int32)[None, :, None]
    global_index = ((tile_x * CX + local_x) * NY + tile_y * CY + local_y) * NZ + local_z
    global_index = global_index.reshape(-1).astype(jnp.int32)
    medium_rim = pad_lateral(medium)
    buoyancy = medium[2]
    inverse_own = medium[3]

    def per_event(inputs):
        now, prev, stored, force_values = inputs
        forces = jnp.zeros((2, 3, NX * NY * NZ), jnp.float32)
        forces = forces.at[:, :, global_index].add(force_values.reshape(2, 3, -1))
        forces = forces.reshape(2, 3, NX, NY, NZ)
        current = now[None]
        previous = prev[None]
        shear_total = jnp.zeros((NX, NY, NZ), jnp.float32)
        density_total = jnp.zeros((NX, NY, NZ), jnp.float32)
        for step in range(2):
            current_rim = pad_lateral(current)
            forward_rim = pad_lateral(stored[step + 1][None].astype(jnp.float32))
            shear_total = shear_total + shear_term(current_rim, forward_rim, inverse_own)
            density_total = density_total + density_term(current, stored[step][None], stored[step + 1][None], stored[step + 2][None])
            applied = operate(current_rim, medium_rim)
            following = 2.0 * current - previous + STEP_FACTOR * buoyancy * (applied + forces[step][None])
            previous, current = current, following
        return previous[0], current[0], shear_total, density_total

    middle, latest, shear_all, density_all = lax.map(per_event, (adjoint_now, adjoint_prev, forward, drm_force))
    grad_shear = jnp.sum(shear_all, axis=0) * (1.0 / EVENTS)
    grad_density = jnp.sum(density_all, axis=0) * (1.0 / EVENTS)
    return middle, latest, grad_shear, grad_density
```

```python
import functools

import jax
import jax.numpy as jnp
from jax import lax
from jax.experimental import pallas as pl
from jax.experimental.pallas import tpu as pltpu
from jax.sharding import PartitionSpec as P

STEP_FACTOR = 0.01
F32, BF16 = jnp.float32, jnp.bfloat16
SHEAR, LAME, BUOY, INV = range(4)
ROWS = 16
FULL = pl.BlockSpec(memory_space=pltpu.VMEM)
VMEM_LIMIT = 40 * 1024 * 1024
PACK_LIMIT = 60 * 1024 * 1024


def rounds_of(count):
    return "AB"[: max(0, min(2, count - 1))]


def swap(values, axis, name):
    count = lax.axis_size(axis)
    first = "AB".index(name)
    pairs = []
    for low in range(first, count - 1, 2):
        pairs += [(low, low + 1), (low + 1, low)]
    return lax.ppermute(values, axis, pairs)


def upward(axis, name):
    even = lax.rem(lax.axis_index(axis), 2) == 0
    return even if name == "A" else jnp.logical_not(even)


def split(values):
    high = values.astype(BF16)
    low = (values - high.astype(F32)).astype(BF16)
    return jnp.concatenate([high, low], axis=0)


def join(tile):
    tile = tile.astype(F32)
    return tile[:8] + tile[8:]


def force_field(cells, force_rows, width):
    depth = 128
    count = cells.shape[1]
    place = lax.broadcasted_iota(jnp.int32, (width, count), 0)
    mask = place == cells // depth
    level = lax.broadcasted_iota(jnp.int32, (depth, count), 0)
    hot = jnp.where(level == lax.rem(cells, depth), 1.0, 0.0).astype(BF16)
    left = jnp.concatenate([jnp.where(mask, row, 0.0) for row in force_rows], axis=0)
    total = None
    for _ in range(3):
        part = left.astype(BF16)
        left = left - part.astype(F32)
        term = lax.dot_general(part, hot, (((1,), (1,)), ((), ())), preferred_element_type=F32)
        total = term if total is None else total + term
    return total


def pack_kernel(events, x_rounds, y_rounds, now_in, prev_in, fwd_in, med_in, cells, force, *refs):
    fields = 3 * events
    outs, (now, prev, fwd, med, stored, arrived) = refs[:-6], refs[-6:]
    base = outs[0]
    messages = outs[1:]
    copies = [(now_in, now), (prev_in, prev), (med_in, med)]
    for e in range(events):
        copies.append((fwd_in.at[pl.ds(e * 12 + 3, 6)], fwd.at[pl.ds(e * 6, 6)]))
    copies = [
        pltpu.make_async_copy(source, target, arrived.at[k])
        for k, (source, target) in enumerate(copies)
    ]
    for copy in copies:
        copy.start()
    rows = [force[e, 0, c, 0] for e in range(events) for c in range(3)]
    pushed = force_field(cells[...], rows, 64)
    for copy in copies:
        copy.wait()
    for f in range(fields):
        base[f] = (
            2.0 * now[f] - prev[f] + STEP_FACTOR * med[BUOY] * pushed[f * 64 : (f + 1) * 64]
        )
        e, c = f // 3, f % 3
        for t in range(2):
            stored[f * 2 + t] = fwd[(e * 2 + t) * 3 + c].astype(F32).reshape(64, 128)

    def fill(message, pick):
        for f in range(fields):
            message[2 * f] = split(pick(now, f, 1))
            message[2 * f + 1] = split(pick(now, f, 2))
            message[2 * fields + f] = split(pick(base, f, 1))
            message[3 * fields + f] = jnp.concatenate(
                [pick(stored, 2 * f, 1), pick(stored, 2 * f + 1, 1)], axis=0
            ).astype(BF16)
        for k, m in enumerate((SHEAR, LAME, INV)):
            message[4 * fields + k] = jnp.concatenate(
                [pick(med, m, 1), pick(med, m, 2)], axis=0
            ).astype(BF16)
        edge = pick(med, BUOY, 1)
        message[4 * fields + 3] = jnp.concatenate([edge, edge], axis=0).astype(BF16)

    for k, name in enumerate(x_rounds):
        up = upward("gx", name)

        def pick_x(ref, index, ring, up=up):
            row = jnp.where(up, 8 - ring, ring - 1)
            return ref[index, pl.ds(pl.multiple_of(row * 8, 8), 8), :]

        fill(messages[k], pick_x)
    for k, name in enumerate(y_rounds):
        up = upward("gy", name)

        def pick_y(ref, index, ring, up=up):
            row = jnp.where(up, 8 - ring, ring - 1)
            return ref[index, pl.ds(row, 8, stride=8), :]

        fill(messages[len(x_rounds) + k], pick_y)


def corner_kernel(fields, x_rounds, y_rounds, *refs):
    sides = refs[: len(y_rounds)]
    outs = refs[len(y_rounds) : len(y_rounds) + len(x_rounds)]
    rows = refs[-1]
    for s, side in enumerate(sides):
        for k in range(3 * fields):
            rows[s, pl.ds(k * 8, 8), :] = join(side[k])
        for k in range(3):
            tile = side[4 * fields + k].astype(F32)
            rows[s, pl.ds((3 * fields + 2 * k) * 8, 16), :] = tile
        tile = side[4 * fields + 3].astype(F32)
        rows[s, pl.ds((3 * fields + 6) * 8, 16), :] = tile
        for k in range(3 * fields + 8, 32):
            rows[s, pl.ds(k * 8, 8), :] = jnp.zeros((8, 128), F32)
    for k, name in enumerate(x_rounds):
        up = upward("gx", name)
        for s in range(len(sides)):
            for ring in (1, 2):
                row = jnp.where(up, 8 - ring, ring - 1)
                outs[k][s, ring - 1] = rows[s, pl.ds(row, 32, stride=8), :]


def shift_z(values, step, lane, beyond=0.0):
    depth = values.shape[-1]
    moved = pltpu.roll(values, (-step) % depth, axis=values.ndim - 1)
    edge = depth - 1 if step > 0 else 0
    return jnp.where(lane == edge, beyond, moved)


def shift_y(values, step):
    return pltpu.roll(values, (-step) % ROWS, axis=0)


def row_of(ref, index, row):
    return ref[index, pl.ds(row * ROWS, ROWS), :]


def time_step(field, faces, first, last, emit):
    lane = lax.broadcasted_iota(jnp.int32, (ROWS, 128), 1)
    value = functools.cache(field)

    @functools.cache
    def ahead_y(c, row):
        return shift_y(value(c, row), 1)

    @functools.cache
    def ahead_z(c, row):
        return shift_z(value(c, row), 1, lane)

    @functools.cache
    def slope(d, row):
        if d == 0:
            return faces("cross", row) * (value(0, row + 1) - value(0, row - 1))
        if d == 1:
            return faces("cross", row) * (ahead_y(1, row) - shift_y(value(1, row), -1))
        return faces("cross_z", row) * (ahead_z(2, row) - shift_z(value(2, row), -1, lane))

    @functools.cache
    def flux_x(c, row):
        kind = "own_x" if c == 0 else "other_x"
        return faces(kind, row) * (value(c, row + 1) - value(c, row))

    for row in range(first, last + 1):
        results = []
        for c in range(3):
            total = flux_x(c, row) - flux_x(c, row - 1)
            flux = faces("own_y" if c == 1 else "other_y", row) * (ahead_y(c, row) - value(c, row))
            total = total + (flux - shift_y(flux, -1))
            flux = faces("own_z" if c == 2 else "other_z", row) * (ahead_z(c, row) - value(c, row))
            below = faces("own_low" if c == 2 else "other_low", row) * value(c, row)
            upright = flux - shift_z(flux, -1, lane, below)
            if c == 0:
                total = total + (
                    (slope(1, row + 1) + slope(2, row + 1))
                    - (slope(1, row - 1) + slope(2, row - 1))
                )
            elif c == 1:
                mixed = slope(0, row) + slope(2, row)
                total = total + (shift_y(mixed, 1) - shift_y(mixed, -1))
            else:
                mixed = slope(0, row) + slope(1, row)
                upright = upright + (shift_z(mixed, 1, lane) - shift_z(mixed, -1, lane))
            results.append(total + faces("inverse", row) * upright)
        emit(row, results)


def main_kernel(events, x_rounds, y_rounds, shares, *refs):
    fields = 3 * events
    now, base, fwd, med, cells, force = refs[:6]
    at = 6
    x_messages = refs[at : at + len(x_rounds)]
    at += len(x_rounds)
    y_messages = refs[at : at + len(y_rounds)]
    at += len(y_rounds)
    corners = refs[at : at + len(x_rounds)] if y_rounds else ()
    at += len(corners)
    mid, after, own_share = refs[at : at + 3]
    at += 3
    sent = refs[at : at + shares - 1]
    at += shares - 1
    here, then, start, stored, medium, coef, slabs = refs[at:]

    for f in range(fields):
        e, c = f // 3, f % 3
        for x in range(8):
            spot = pl.ds((x + 2) * ROWS, 8)
            here[f, spot, :] = now[f, pl.ds(x * 8, 8), :]
            start[f, spot, :] = base[f, pl.ds(x * 8, 8), :]
            for t in range(2):
                stored[2 * f + t, spot, :] = fwd[(e * 4 + t + 1) * 3 + c, x].astype(F32)
    for m in range(4):
        for x in range(8):
            medium[m, pl.ds((x + 2) * ROWS, 8), :] = med[m, pl.ds(x * 8, 8), :]

    def place(tile, put):
        for f in range(fields):
            put(here, f, 1, join(tile(2 * f)))
            put(here, f, 2, join(tile(2 * f + 1)))
            put(start, f, 1, join(tile(2 * fields + f)))
            both = tile(3 * fields + f).astype(F32)
            put(stored, 2 * f, 1, both[:8])
            put(stored, 2 * f + 1, 1, both[8:])
        for k, m in enumerate((SHEAR, LAME, INV)):
            both = tile(4 * fields + k).astype(F32)
            put(medium, m, 1, both[:8])
            put(medium, m, 2, both[8:])
        put(medium, BUOY, 1, tile(4 * fields + 3).astype(F32)[:8])

    def nothing(_):
        return jnp.zeros((16, 128), BF16)

    def x_row(up, ring):
        return jnp.where(up, 9 + ring, 2 - ring)

    def y_place(up, ring):
        return jnp.where(up, 7 + ring, ROWS - ring)

    for k, name in enumerate("AB"):
        up = upward("gx", name)

        def put_x(ref, index, ring, values, up=up):
            row = pl.multiple_of(x_row(up, ring) * ROWS, ROWS)
            ref[index, pl.ds(row, 8), :] = values

        if k < len(x_rounds):
            place(lambda i, k=k: x_messages[k][i], put_x)
        else:
            place(nothing, put_x)
    for k, name in enumerate("AB"):
        up = upward("gy", name)

        def put_y(ref, index, ring, values, up=up):
            ref[index, pl.ds(2 * ROWS + y_place(up, ring), 8, stride=ROWS), :] = values

        if k < len(y_rounds):
            place(lambda i, k=k: y_messages[k][i], put_y)
        else:
            place(nothing, put_y)
    for kx, name_x in enumerate("AB"):
        for ky, name_y in enumerate("AB"):
            up_x, up_y = upward("gx", name_x), upward("gy", name_y)
            for ring_x in (1, 2):
                for ring_y in (1, 2):
                    spot = x_row(up_x, ring_x) * ROWS + y_place(up_y, ring_y)

                    def move(ref, index, k):
                        if kx < len(x_rounds) and ky < len(y_rounds):
                            values = corners[kx][ky, ring_x - 1, pl.ds(k, 1), :]
                        else:
                            values = jnp.zeros((1, 128), F32)
                        ref[index, pl.ds(spot, 1), :] = values

                    for f in range(fields):
                        move(here, f, 2 * f + ring_y - 1)
                        if ring_x == 1 and ring_y == 1:
                            move(start, f, 2 * fields + f)
                    for k, m in enumerate((SHEAR, LAME, INV)):
                        move(medium, m, 3 * fields + 2 * k + ring_y - 1)
                    if ring_x == 1 and ring_y == 1:
                        move(medium, BUOY, 3 * fields + 6)

    names = (
        ("own_x", "other_x", "own_y", "other_y", "own_z", "other_z")
        + ("own_low", "other_low", "cross", "cross_z")
    )
    lane = lax.broadcasted_iota(jnp.int32, (ROWS, 128), 1)

    def wide(row):
        return row_of(medium, LAME, row) + 2.0 * row_of(medium, SHEAR, row)

    for row in range(12):
        shear, lame, inverse = (row_of(medium, m, row) for m in (SHEAR, LAME, INV))
        both = lame + 2.0 * shear
        values = {}
        if row < 11:
            values["own_x"] = 0.5 * (both + wide(row + 1))
            values["other_x"] = 0.5 * (shear + row_of(medium, SHEAR, row + 1))
        values["own_y"] = 0.5 * (both + shift_y(both, 1))
        values["other_y"] = 0.5 * (shear + shift_y(shear, 1))
        spacing = 0.25 * (inverse + shift_z(inverse, 1, lane))
        values["own_z"] = spacing * (both + shift_z(both, 1, lane))
        values["other_z"] = spacing * (shear + shift_z(shear, 1, lane))
        values["own_low"] = 0.25 * inverse * both
        values["other_low"] = 0.25 * inverse * shear
        values["cross"] = 0.25 * (lame + shear)
        values["cross_z"] = values["cross"] * inverse
        for name, value in values.items():
            coef[names.index(name), pl.ds(row * ROWS, ROWS), :] = value

    def faces(name, row):
        if name == "inverse":
            return row_of(medium, INV, row)
        return row_of(coef, names.index(name), row)

    for e in range(events):

        def emit(row, results, e=e):
            scale = STEP_FACTOR * row_of(medium, BUOY, row)
            for c in range(3):
                f = 3 * e + c
                value = row_of(start, f, row) + scale * results[c]
                then[f, pl.ds(row * ROWS, ROWS), :] = value
                if 2 <= row <= 9:
                    mid[f, pl.ds((row - 2) * 8, 8), :] = value[:8]

        time_step(lambda c, row, e=e: row_of(here, 3 * e + c, row), faces, 1, 10, emit)

    lane8 = lane[:8]
    grads = [[], []]
    for x in range(8):
        row = x + 2
        lateral = upright = density = None
        for t, ref in ((0, here), (1, then)):
            for f in range(fields):
                e, c = f // 3, f % 3

                def slopes(source, index):
                    mine = row_of(source, index, row)
                    along_x = row_of(source, index, row + 1) - row_of(source, index, row - 1)
                    along_y = shift_y(mine, 1) - shift_y(mine, -1)
                    own = mine[:8]
                    along_z = shift_z(own, 1, lane8) - shift_z(own, -1, lane8)
                    return own, along_x[:8], along_y[:8], along_z

                own, ax, ay, az = slopes(ref, f)
                middle, ux, uy, uz = slopes(stored, 2 * f + t)
                newer = fwd[(e * 4 + t) * 3 + c, x].astype(F32)
                older = fwd[(e * 4 + t + 2) * 3 + c, x].astype(F32)
                terms = (ax * ux + ay * uy, az * uz, own * (newer - 2.0 * middle + older))
                if lateral is None:
                    lateral, upright, density = terms
                else:
                    lateral, upright, density = (
                        lateral + terms[0],
                        upright + terms[1],
                        density + terms[2],
                    )
        inverse = med[INV, pl.ds(x * 8, 8), :]
        grads[0].append(-0.25 * (lateral + inverse * inverse * upright))
        grads[1].append(-density)
    grads = grads[0] + grads[1]
    piece = 128 // shares
    quarter = lane8 // piece
    per = len(grads) // shares
    for j in range(shares):
        for r in range(per):
            tile = None
            for g in range(shares):
                source = grads[r * shares + g]
                moved = pltpu.roll(source, ((g - j) * piece) % 128, axis=1) if g != j else source
                tile = moved if tile is None else jnp.where(quarter == g, moved, tile)
            slabs[j, pl.ds(r * 8, 8), :] = tile
    me = lax.axis_index("ev")
    own_share[...] = slabs[me]
    for m in range(1, shares):
        sent[m - 1][...] = slabs[me ^ m]

    rows = [force[e, 1, c, 0] for e in range(events) for c in range(3)]
    pushed = force_field(cells[...], rows, 64)
    for e in range(events):

        def emit(row, results, e=e):
            x = row - 2
            scale = STEP_FACTOR * med[BUOY, pl.ds(x * 8, 8), :]
            for c in range(3):
                f = 3 * e + c
                current = then[f, pl.ds(row * ROWS, 8), :]
                previous = now[f, pl.ds(x * 8, 8), :]
                extra = pushed[f * 64 + x * 8 : f * 64 + x * 8 + 8]
                after[f, pl.ds(x * 8, 8), :] = (
                    2.0 * current - previous + scale * (results[c][:8] + extra)
                )

        time_step(lambda c, row, e=e: row_of(then, 3 * e + c, row), faces, 2, 9, emit)


def finish_kernel(shares, scale, *refs):
    pieces, (shear, density) = refs[:shares], refs[shares:]
    total = pieces[0][...]
    for piece in pieces[1:]:
        total = total + piece[...]
    width = 128 // shares
    for v in range(16):
        g, r = v % shares, v // shares
        tile = total[r * 8 : (r + 1) * 8]
        if g:
            tile = pltpu.roll(tile, (-g * width) % 128, axis=1)
        out = shear if v < 8 else density
        out[pl.ds((v % 8) * 8, 8), :] = tile[:, :width] * scale


def call(kernel, outs, ins, scratch=(), name=None, limit=VMEM_LIMIT):
    return pl.pallas_call(
        kernel,
        out_shape=[jax.ShapeDtypeStruct(s, d) for s, d in outs],
        in_specs=[pl.BlockSpec(memory_space=m) for m in ins],
        scratch_shapes=[s if not isinstance(s, tuple) else pltpu.VMEM(*s) for s in scratch],
        compiler_params=pltpu.CompilerParams(vmem_limit_bytes=limit),
        name=name,
    )


def body(adjoint_now, adjoint_prev, forward, medium, drm_cells, drm_force):
    events, _, width_x, width_y, depth = adjoint_now.shape
    fields = 3 * events
    tile = width_x * width_y
    shares = lax.axis_size("ev")
    x_rounds, y_rounds = rounds_of(lax.axis_size("gx")), rounds_of(lax.axis_size("gy"))
    now = adjoint_now.reshape(fields, tile, depth)
    prev = adjoint_prev.reshape(fields, tile, depth)
    fwd = forward.reshape(events * 12, width_x, width_y, depth)
    med = medium.reshape(4, tile, depth)
    cells = drm_cells.reshape(1, -1)
    force = drm_force

    message = ((4 * fields + 4, 16, depth), BF16)
    base, *messages = call(
        functools.partial(pack_kernel, events, x_rounds, y_rounds),
        [((fields, tile, depth), F32)] + [message] * (len(x_rounds) + len(y_rounds)),
        [pltpu.HBM] * 4 + [pltpu.VMEM] * 2,
        [
            ((fields, tile, depth), F32),
            ((fields, tile, depth), F32),
            ((2 * fields, width_x, width_y, depth), BF16),
            ((4, tile, depth), F32),
            ((2 * fields, tile, depth), F32),
            pltpu.SemaphoreType.DMA((3 + events,)),
        ],
        "pack",
        PACK_LIMIT,
    )(now, prev, fwd, med, cells, force)
    y_messages = [swap(m, "gy", r) for m, r in zip(messages[len(x_rounds) :], y_rounds)]
    x_messages = [swap(m, "gx", r) for m, r in zip(messages, x_rounds)]
    corners = []
    if x_rounds and y_rounds:
        corners = call(
            functools.partial(corner_kernel, fields, x_rounds, y_rounds),
            [((len(y_rounds), 2, 32, depth), F32)] * len(x_rounds),
            [pltpu.VMEM] * len(y_rounds),
            [((len(y_rounds), 32 * 8, depth), F32)],
            "corners",
        )(*y_messages)
        corners = [swap(m, "gx", r) for m, r in zip(corners, x_rounds)]

    slab = ((16 // shares * 8, depth), F32)
    wide = ((fields, 12 * ROWS, depth), F32)
    mid, after, own_share, *sent = call(
        functools.partial(main_kernel, events, x_rounds, y_rounds, shares),
        [((fields, tile, depth), F32)] * 2 + [slab] * shares,
        [pltpu.VMEM] * (6 + len(x_messages) + len(y_messages) + len(corners)),
        [
            wide,
            wide,
            wide,
            ((2 * fields, 12 * ROWS, depth), F32),
            ((4, 12 * ROWS, depth), F32),
            ((10, 12 * ROWS, depth), F32),
            ((shares,) + slab[0], F32),
        ],
        "steps",
    )(now, base, fwd, med, cells, force, *x_messages, *y_messages, *corners)
    pieces = [own_share]
    for m in reversed(range(1, shares)):
        pairs = [(i, i ^ m) for i in range(shares)]
        pieces.append(lax.ppermute(sent[m - 1], "ev", pairs))
    shear, density = call(
        functools.partial(finish_kernel, shares, 1.0 / (events * shares)),
        [((tile, depth // shares), F32)] * 2,
        [pltpu.VMEM] * shares,
        name="finish",
    )(*pieces)
    shape = adjoint_now.shape
    grad = (width_x, width_y, depth // shares)
    return mid.reshape(shape), after.reshape(shape), shear.reshape(grad), density.reshape(grad)


def solution(mesh):
    in_specs = (
        P("ev", None, "gx", "gy", None),
        P("ev", None, "gx", "gy", None),
        P("ev", None, None, "gx", "gy", None),
        P(None, "gx", "gy", None),
        P("gx", "gy", None),
        P("ev", None, None, "gx", "gy", None),
    )
    out_specs = (
        P("ev", None, "gx", "gy", None),
        P("ev", None, "gx", "gy", None),
        P("gx", "gy", "ev"),
        P("gx", "gy", "ev"),
    )
    return jax.shard_map(body, mesh=mesh, in_specs=in_specs, out_specs=out_specs, check_vma=False)
```

```python
import functools

import jax
import jax.numpy as jnp
from jax import lax
from jax.experimental import pallas as pl
from jax.experimental.pallas import tpu as pltpu
from jax.sharding import PartitionSpec as P

STEP_FACTOR = 0.01
F32, BF16 = jnp.float32, jnp.bfloat16
SHEAR, LAME, BUOY, INV = range(4)
ROWS = 16
FULL = pl.BlockSpec(memory_space=pltpu.VMEM)
VMEM_LIMIT = 40 * 1024 * 1024
PACK_LIMIT = 60 * 1024 * 1024


def rounds_of(count):
    return "AB"[: max(0, min(2, count - 1))]


def swap(values, axis, name):
    count = lax.axis_size(axis)
    first = "AB".index(name)
    pairs = []
    for low in range(first, count - 1, 2):
        pairs += [(low, low + 1), (low + 1, low)]
    return lax.ppermute(values, axis, pairs)


def upward(axis, name):
    even = lax.rem(lax.axis_index(axis), 2) == 0
    return even if name == "A" else jnp.logical_not(even)


def split(values):
    high = values.astype(BF16)
    low = (values - high.astype(F32)).astype(BF16)
    return jnp.concatenate([high, low], axis=0)


def join(tile):
    tile = tile.astype(F32)
    return tile[:8] + tile[8:]


def force_field(cells, force_rows, width):
    depth = 128
    count = cells.shape[1]
    place = lax.broadcasted_iota(jnp.int32, (width, count), 0)
    mask = place == cells // depth
    level = lax.broadcasted_iota(jnp.int32, (depth, count), 0)
    hot = jnp.where(level == lax.rem(cells, depth), 1.0, 0.0).astype(BF16)
    left = jnp.concatenate([jnp.where(mask, row, 0.0) for row in force_rows], axis=0)
    total = None
    for _ in range(3):
        part = left.astype(BF16)
        left = left - part.astype(F32)
        term = lax.dot_general(part, hot, (((1,), (1,)), ((), ())), preferred_element_type=F32)
        total = term if total is None else total + term
    return total


def pack_kernel(events, x_rounds, y_rounds, *refs):
    fields = 3 * events
    count = 6
    sources = refs[:count]
    messages = refs[count : count + len(x_rounds) + len(y_rounds)]
    now, prev, fwd, med, cells, force, base, stored, arrived = refs[count + len(messages) :]
    now_in, prev_in, fwd_in, med_in, cells_in, force_in = sources
    pairs = [(cells_in, cells), (force_in, force), (now_in, now), (prev_in, prev), (med_in, med)]
    for e in range(events):
        pairs.append((fwd_in.at[pl.ds(e * 12 + 3, 6)], fwd.at[pl.ds(e * 6, 6)]))
    copies = [
        pltpu.make_async_copy(source, target, arrived.at[k])
        for k, (source, target) in enumerate(pairs)
    ]
    for copy in copies:
        copy.start()
    for copy in copies[:2]:
        copy.wait()
    rows = [force[e, 0, c, 0] for e in range(events) for c in range(3)]
    pushed = force_field(cells[0], rows, 64)
    for copy in copies[2:]:
        copy.wait()
    for f in range(fields):
        base[f] = (
            2.0 * now[f] - prev[f] + STEP_FACTOR * med[BUOY] * pushed[f * 64 : (f + 1) * 64]
        )
        e, c = f // 3, f % 3
        for t in range(2):
            stored[f * 2 + t] = fwd[(e * 2 + t) * 3 + c].astype(F32).reshape(64, 128)

    def fill(message, pick):
        for f in range(fields):
            message[2 * f] = split(pick(now, f, 1))
            message[2 * f + 1] = split(pick(now, f, 2))
            message[2 * fields + f] = split(pick(base, f, 1))
            message[3 * fields + f] = jnp.concatenate(
                [pick(stored, 2 * f, 1), pick(stored, 2 * f + 1, 1)], axis=0
            ).astype(BF16)
        for k, m in enumerate((SHEAR, LAME, INV)):
            message[4 * fields + k] = jnp.concatenate(
                [pick(med, m, 1), pick(med, m, 2)], axis=0
            ).astype(BF16)
        edge = pick(med, BUOY, 1)
        message[4 * fields + 3] = jnp.concatenate([edge, edge], axis=0).astype(BF16)

    for k, name in enumerate(x_rounds):
        up = upward("gx", name)

        def pick_x(ref, index, ring, up=up):
            row = jnp.where(up, 8 - ring, ring - 1)
            return ref[index, pl.ds(pl.multiple_of(row * 8, 8), 8), :]

        fill(messages[k], pick_x)
    for k, name in enumerate(y_rounds):
        up = upward("gy", name)

        def pick_y(ref, index, ring, up=up):
            row = jnp.where(up, 8 - ring, ring - 1)
            return ref[index, pl.ds(row, 8, stride=8), :]

        fill(messages[len(x_rounds) + k], pick_y)


def corner_kernel(fields, x_rounds, y_rounds, *refs):
    sides = refs[: len(y_rounds)]
    outs = refs[len(y_rounds) : len(y_rounds) + len(x_rounds)]
    rows = refs[-1]
    for s, side in enumerate(sides):
        for k in range(3 * fields):
            rows[s, pl.ds(k * 8, 8), :] = join(side[k])
        for k in range(3):
            tile = side[4 * fields + k].astype(F32)
            rows[s, pl.ds((3 * fields + 2 * k) * 8, 16), :] = tile
        tile = side[4 * fields + 3].astype(F32)
        rows[s, pl.ds((3 * fields + 6) * 8, 16), :] = tile
        for k in range(3 * fields + 8, 32):
            rows[s, pl.ds(k * 8, 8), :] = jnp.zeros((8, 128), F32)
    for k, name in enumerate(x_rounds):
        up = upward("gx", name)
        for s in range(len(sides)):
            for ring in (1, 2):
                row = jnp.where(up, 8 - ring, ring - 1)
                outs[k][s, ring - 1] = rows[s, pl.ds(row, 32, stride=8), :]


def shift_z(values, step):
    depth = values.shape[-1]
    lane = lax.broadcasted_iota(jnp.int32, values.shape, values.ndim - 1)
    moved = pltpu.roll(values, (-step) % depth, axis=values.ndim - 1)
    return jnp.where(lane == (depth - 1 if step > 0 else 0), 0.0, moved)


def shift_y(values, step):
    return pltpu.roll(values, (-step) % ROWS, axis=0)


def row_of(ref, index, row):
    return ref[index, pl.ds(row * ROWS, ROWS), :]


COEFFICIENTS = (
    ("own_x", "other_x", "own_y", "other_y", "own_z", "other_z", "cross", "cross_z")
    + ("own_y_down", "other_y_down", "own_z_down", "other_z_down")
)


def coefficients(medium, row, ahead=True):
    def both_of(row):
        return medium(LAME, row) + 2.0 * medium(SHEAR, row)

    shear, lame, inverse = (medium(m, row) for m in (SHEAR, LAME, INV))
    both = both_of(row)
    values = {}
    if ahead:
        values["own_x"] = 0.5 * (both + both_of(row + 1))
        values["other_x"] = 0.5 * (shear + medium(SHEAR, row + 1))
    for tail, step in (("", 1), ("_down", -1)):
        values["own_y" + tail] = 0.5 * (both + shift_y(both, step))
        values["other_y" + tail] = 0.5 * (shear + shift_y(shear, step))
        spacing = 0.25 * (inverse + shift_z(inverse, step))
        values["own_z" + tail] = spacing * (both + shift_z(both, step))
        values["other_z" + tail] = spacing * (shear + shift_z(shear, step))
    values["cross"] = 0.25 * (lame + shear)
    values["cross_z"] = values["cross"] * inverse
    return values


class Event:
    def __init__(self, value):
        self.value = functools.cache(value)
        self.y = functools.cache(lambda c, row, step: shift_y(self.value(c, row), step))
        self.z = functools.cache(lambda c, row, step: shift_z(self.value(c, row), step))

    def slopes(self, c, row):
        return (
            (self.value(c, row + 1) - self.value(c, row - 1))[:8],
            (self.y(c, row, 1) - self.y(c, row, -1))[:8],
            (self.z(c, row, 1) - self.z(c, row, -1))[:8],
        )

    def operator(self, faces):
        value = self.value

        @functools.cache
        def slope(d, row):
            if d == 0:
                return faces("cross", row) * (value(0, row + 1) - value(0, row - 1))
            if d == 1:
                return faces("cross", row) * (self.y(1, row, 1) - self.y(1, row, -1))
            return faces("cross_z", row) * (self.z(2, row, 1) - self.z(2, row, -1))

        @functools.cache
        def flux_x(c, row):
            kind = "own_x" if c == 0 else "other_x"
            return faces(kind, row) * (value(c, row + 1) - value(c, row))

        def apply(row):
            results = []
            for c in range(3):
                here = value(c, row)
                total = flux_x(c, row) - flux_x(c, row - 1)
                kind = "own_y" if c == 1 else "other_y"
                total = total + (
                    faces(kind, row) * (self.y(c, row, 1) - here)
                    - faces(kind + "_down", row) * (here - self.y(c, row, -1))
                )
                kind = "own_z" if c == 2 else "other_z"
                upright = faces(kind, row) * (self.z(c, row, 1) - here) - faces(
                    kind + "_down", row
                ) * (here - self.z(c, row, -1))
                if c == 0:
                    total = total + (
                        (slope(1, row + 1) + slope(2, row + 1))
                        - (slope(1, row - 1) + slope(2, row - 1))
                    )
                elif c == 1:
                    mixed = slope(0, row) + slope(2, row)
                    total = total + (shift_y(mixed, 1) - shift_y(mixed, -1))
                else:
                    mixed = slope(0, row) + slope(1, row)
                    upright = upright + (shift_z(mixed, 1) - shift_z(mixed, -1))
                results.append(total + faces("inverse", row) * upright)
            return results

        return apply


def x_row(up, ring):
    return jnp.where(up, 9 + ring, 2 - ring)


def y_place(up, ring):
    return jnp.where(up, 7 + ring, ROWS - ring)


def tile_row(ref, index, row):
    return ref[index, pl.ds((row - 2) * 8, 8), :]


def own_kernel(events, now, prev, med, cells, force, base, extra):
    fields = 3 * events
    rows = [force[e, s, c, 0] for s in range(2) for e in range(events) for c in range(3)]
    pushed = force_field(cells[0], rows, 64)
    scale = STEP_FACTOR * med[BUOY]
    for f in range(fields):
        base[f] = 2.0 * now[f] - prev[f] + scale * pushed[f * 64 : (f + 1) * 64]
        extra[f] = scale * pushed[(fields + f) * 64 : (fields + f + 1) * 64]


def add_to(sums, key, value):
    sums[key] = sums[key] + value if key in sums else value


def inner_kernel(events, x_rounds, y_rounds, now, base, fwd, med, *refs):
    fields = 3 * events
    x_messages, refs = refs[: len(x_rounds)], refs[len(x_rounds) :]
    y_messages, refs = refs[: len(y_rounds)], refs[len(y_rounds) :]
    here, start, stored, medium, coef, then, part = refs

    for f in range(fields):
        e, c = f // 3, f % 3
        for x in range(8):
            spot = pl.ds((x + 2) * ROWS, 8)
            here[f, spot, :] = now[f, pl.ds(x * 8, 8), :]
            start[f, spot, :] = base[f, pl.ds(x * 8, 8), :]
            for t in range(2):
                stored[2 * f + t, spot, :] = fwd[(e * 4 + t + 1) * 3 + c, x].astype(F32)
    for m in range(4):
        for x in range(8):
            medium[m, pl.ds((x + 2) * ROWS, 8), :] = med[m, pl.ds(x * 8, 8), :]

    def place(tile, put):
        for f in range(fields):
            put(here, f, 1, join(tile(2 * f)))
            put(here, f, 2, join(tile(2 * f + 1)))
            put(start, f, 1, join(tile(2 * fields + f)))
            both = tile(3 * fields + f).astype(F32)
            put(stored, 2 * f, 1, both[:8])
            put(stored, 2 * f + 1, 1, both[8:])
        for k, m in enumerate((SHEAR, LAME, INV)):
            both = tile(4 * fields + k).astype(F32)
            put(medium, m, 1, both[:8])
            put(medium, m, 2, both[8:])
        put(medium, BUOY, 1, tile(4 * fields + 3).astype(F32)[:8])

    def nothing(_):
        return jnp.zeros((16, 128), BF16)

    for k, name in enumerate("AB"):
        up = upward("gx", name)

        def put_x(ref, index, ring, values, up=up):
            row = pl.multiple_of(x_row(up, ring) * ROWS, ROWS)
            ref[index, pl.ds(row, 8), :] = values

        place((lambda i, k=k: x_messages[k][i]) if k < len(x_rounds) else nothing, put_x)
    for k, name in enumerate("AB"):
        up = upward("gy", name)

        def put_y(ref, index, ring, values, up=up):
            ref[index, pl.ds(2 * ROWS + y_place(up, ring), 8, stride=ROWS), :] = values

        place((lambda i, k=k: y_messages[k][i]) if k < len(y_rounds) else nothing, put_y)

    for row in range(1, 11):
        values = coefficients(lambda m, r: row_of(medium, m, r), row, row < 10)
        for name, value in values.items():
            coef[COEFFICIENTS.index(name), pl.ds(row * ROWS, ROWS), :] = value

    def faces(name, row):
        if name == "inverse":
            return row_of(medium, INV, row)
        return row_of(coef, COEFFICIENTS.index(name), row)

    sums = {}
    for e in range(events):
        first = Event(lambda c, row, e=e: row_of(here, 3 * e + c, row))
        apply = first.operator(faces)
        waves = [
            Event(lambda c, row, e=e, t=t: row_of(stored, 2 * (3 * e + c) + t, row))
            for t in range(2)
        ]
        for row in range(2, 10):
            if 3 <= row <= 8:
                scale = STEP_FACTOR * row_of(medium, BUOY, row)
                for c, result in enumerate(apply(row)):
                    f = 3 * e + c
                    then[f, pl.ds(row * ROWS, ROWS), :] = row_of(start, f, row) + scale * result
            gather(sums, first, waves[0], fwd, e, 0, row)
        second = Event(lambda c, row, e=e: row_of(then, 3 * e + c, row))
        for row in range(4, 8):
            gather(sums, second, waves[1], fwd, e, 1, row)
    for row in range(2, 10):
        inverse = tile_row(med, INV, row)
        shear = sums["lateral", row] + inverse * inverse * sums["upright", row]
        part[0, pl.ds((row - 2) * 8, 8), :] = -0.25 * shear
        part[1, pl.ds((row - 2) * 8, 8), :] = -sums["density", row]


def gather(sums, field, wave, fwd, e, t, row):
    for c in range(3):
        ax, ay, az = field.slopes(c, row)
        ux, uy, uz = wave.slopes(c, row)
        newer = fwd[(e * 4 + t) * 3 + c, row - 2].astype(F32)
        older = fwd[(e * 4 + t + 2) * 3 + c, row - 2].astype(F32)
        bend = newer - 2.0 * wave.value(c, row)[:8] + older
        add_to(sums, ("lateral", row), ax * ux + ay * uy)
        add_to(sums, ("upright", row), az * uz)
        add_to(sums, ("density", row), field.value(c, row)[:8] * bend)


OUTER = (0, 1, 10, 11)
EDGES = (1, 2, 9, 10)


def edge_kernel(events, x_rounds, y_rounds, shares, *refs):
    fields = 3 * events
    corners, refs = refs[: len(x_rounds)], refs[len(x_rounds) :]
    (here, start, stored, medium, coef, then, part, fwd, med), refs = refs[:9], refs[9:]
    edge, own_share, *sent = refs[: 1 + shares]
    outer, outer_start, outer_medium, outer_coef, slabs = refs[1 + shares :]

    for k, row in enumerate(OUTER):
        spot = pl.ds(k * ROWS, ROWS)
        for f in range(fields):
            outer[f, spot, :] = row_of(here, f, row)
            if row in EDGES:
                outer_start[f, spot, :] = row_of(start, f, row)
        for m in range(4):
            outer_medium[m, spot, :] = row_of(medium, m, row)
    for kx, name_x in enumerate("AB"):
        for ky, name_y in enumerate("AB"):
            up_x, up_y = upward("gx", name_x), upward("gy", name_y)
            for ring_x in (1, 2):
                for ring_y in (1, 2):
                    place = jnp.where(up_x, 1 + ring_x, 2 - ring_x)
                    spot = place * ROWS + y_place(up_y, ring_y)

                    def move(ref, index, k):
                        if kx < len(x_rounds) and ky < len(y_rounds):
                            values = corners[kx][ky, ring_x - 1, pl.ds(k, 1), :]
                        else:
                            values = jnp.zeros((1, 128), F32)
                        ref[index, pl.ds(spot, 1), :] = values

                    for f in range(fields):
                        move(outer, f, 2 * f + ring_y - 1)
                        if ring_x == 1 and ring_y == 1:
                            move(outer_start, f, 2 * fields + f)
                    for k, m in enumerate((SHEAR, LAME, INV)):
                        move(outer_medium, m, 3 * fields + 2 * k + ring_y - 1)
                    if ring_x == 1 and ring_y == 1:
                        move(outer_medium, BUOY, 3 * fields + 6)

    def outer_or(ref, full):
        def pick(index, row):
            if row in OUTER:
                return row_of(ref, index, OUTER.index(row))
            return row_of(full, index, row)

        return pick

    field_row, start_row = outer_or(outer, here), outer_or(outer_start, start)
    medium_row = outer_or(outer_medium, medium)
    fresh = (0, 1, 9, 10, 11)
    for k, row in enumerate(fresh):
        for name, value in coefficients(medium_row, row, row < 11).items():
            outer_coef[COEFFICIENTS.index(name), pl.ds(k * ROWS, ROWS), :] = value

    def faces(name, row):
        if name == "inverse":
            return medium_row(INV, row)
        index = COEFFICIENTS.index(name)
        if row in fresh:
            return row_of(outer_coef, index, fresh.index(row))
        return row_of(coef, index, row)

    def then_row(f, row):
        if row in EDGES:
            return row_of(edge, f, EDGES.index(row))
        return row_of(then, f, row)

    sums = {}
    for e in range(events):
        apply = Event(lambda c, row, e=e: field_row(3 * e + c, row)).operator(faces)
        for k, row in enumerate(EDGES):
            scale = STEP_FACTOR * medium_row(BUOY, row)
            for c, result in enumerate(apply(row)):
                f = 3 * e + c
                edge[f, pl.ds(k * ROWS, ROWS), :] = start_row(f, row) + scale * result
        second = Event(lambda c, row, e=e: then_row(3 * e + c, row))
        wave = Event(lambda c, row, e=e: row_of(stored, 2 * (3 * e + c) + 1, row))
        for row in (2, 3, 8, 9):
            gather(sums, second, wave, fwd, e, 1, row)
    grads = [[], []]
    for row in range(2, 10):
        shear, density = tile_row(part, 0, row), tile_row(part, 1, row)
        if row in (2, 3, 8, 9):
            inverse = tile_row(med, INV, row)
            more = sums["lateral", row] + inverse * inverse * sums["upright", row]
            shear = shear - 0.25 * more
            density = density - sums["density", row]
        grads[0].append(shear)
        grads[1].append(density)
    grads = grads[0] + grads[1]
    piece = 128 // shares
    quarter = lax.broadcasted_iota(jnp.int32, (8, 128), 1) // piece
    per = len(grads) // shares
    for j in range(shares):
        for r in range(per):
            tile = None
            for g in range(shares):
                source = grads[r * shares + g]
                moved = pltpu.roll(source, ((g - j) * piece) % 128, axis=1) if g != j else source
                tile = moved if tile is None else jnp.where(quarter == g, moved, tile)
            slabs[j, pl.ds(r * 8, 8), :] = tile
    me = lax.axis_index("ev")
    own_share[...] = slabs[me]
    for m in range(1, shares):
        sent[m - 1][...] = slabs[me ^ m]


def second_kernel(events, now, extra, med, medium, coef, then, edge, mid, after):
    def faces(name, row):
        if name == "inverse":
            return row_of(medium, INV, row)
        return row_of(coef, COEFFICIENTS.index(name), row)

    def then_row(f, row):
        if row in EDGES:
            return row_of(edge, f, EDGES.index(row))
        return row_of(then, f, row)

    for e in range(events):
        apply = Event(lambda c, row, e=e: then_row(3 * e + c, row)).operator(faces)
        for row in range(2, 10):
            spot = pl.ds((row - 2) * 8, 8)
            scale = STEP_FACTOR * tile_row(med, BUOY, row)
            for c, result in enumerate(apply(row)):
                f = 3 * e + c
                current = then_row(f, row)[:8]
                mid[f, spot, :] = current
                after[f, spot, :] = (
                    2.0 * current - now[f, spot, :] + extra[f, spot, :] + scale * result[:8]
                )


def finish_kernel(shares, scale, *refs):
    pieces, (shear, density) = refs[:shares], refs[shares:]
    total = pieces[0][...]
    for piece in pieces[1:]:
        total = total + piece[...]
    width = 128 // shares
    for v in range(16):
        g, r = v % shares, v // shares
        tile = total[r * 8 : (r + 1) * 8]
        if g:
            tile = pltpu.roll(tile, (-g * width) % 128, axis=1)
        out = shear if v < 8 else density
        out[pl.ds((v % 8) * 8, 8), :] = tile[:, :width] * scale


def call(kernel, outs, ins, scratch=(), name=None, limit=VMEM_LIMIT, cost=1000):
    return pl.pallas_call(
        kernel,
        out_shape=[jax.ShapeDtypeStruct(s, d) for s, d in outs],
        in_specs=[pl.BlockSpec(memory_space=m) for m in ins],
        scratch_shapes=[s if not isinstance(s, tuple) else pltpu.VMEM(*s) for s in scratch],
        compiler_params=pltpu.CompilerParams(vmem_limit_bytes=limit),
        cost_estimate=pl.CostEstimate(
            flops=cost * 1024, bytes_accessed=cost * 1024, transcendentals=0
        ),
        name=name,
    )


def body(adjoint_now, adjoint_prev, forward, medium, drm_cells, drm_force):
    events, _, width_x, width_y, depth = adjoint_now.shape
    fields = 3 * events
    tile = width_x * width_y
    shares = lax.axis_size("ev")
    x_rounds, y_rounds = rounds_of(lax.axis_size("gx")), rounds_of(lax.axis_size("gy"))
    now = adjoint_now.reshape(fields, tile, depth)
    prev = adjoint_prev.reshape(fields, tile, depth)
    fwd = forward.reshape(events * 12, width_x, width_y, depth)
    med = medium.reshape(4, tile, depth)
    own = ((fields, tile, depth), F32)
    tall = 12 * ROWS

    messages = call(
        functools.partial(pack_kernel, events, x_rounds, y_rounds),
        [((4 * fields + 4, 16, depth), BF16)] * (len(x_rounds) + len(y_rounds)),
        [pltpu.HBM] * 6,
        [
            own,
            own,
            ((2 * fields, width_x, width_y, depth), BF16),
            ((4, tile, depth), F32),
            (drm_cells.shape, drm_cells.dtype),
            (drm_force.shape, F32),
            own,
            ((2 * fields, tile, depth), F32),
            pltpu.SemaphoreType.DMA((5 + events,)),
        ],
        "pack",
        PACK_LIMIT,
    )(now, prev, fwd, med, drm_cells, drm_force)
    y_messages = [swap(m, "gy", r) for m, r in zip(messages[len(x_rounds) :], y_rounds)]
    x_messages = [swap(m, "gx", r) for m, r in zip(messages, x_rounds)]
    base, extra = call(
        functools.partial(own_kernel, events),
        [own, own],
        [pltpu.VMEM] * 5,
        name="own",
    )(now, prev, med, drm_cells, drm_force)
    corners = []
    if x_rounds and y_rounds:
        corners = call(
            functools.partial(corner_kernel, fields, x_rounds, y_rounds),
            [((len(y_rounds), 2, 32, depth), F32)] * len(x_rounds),
            [pltpu.VMEM] * len(y_rounds),
            [((len(y_rounds), 32 * 8, depth), F32)],
            "corners",
        )(*y_messages)
        corners = [swap(m, "gx", r) for m, r in zip(corners, x_rounds)]

    wide = ((fields, tall, depth), F32)
    here, start, stored, tall_medium, coef, then, part = call(
        functools.partial(inner_kernel, events, x_rounds, y_rounds),
        [
            wide,
            wide,
            ((2 * fields, tall, depth), F32),
            ((4, tall, depth), F32),
            ((len(COEFFICIENTS), tall, depth), F32),
            wide,
            ((2, tile, depth), F32),
        ],
        [pltpu.VMEM] * (4 + len(x_messages) + len(y_messages)),
        name="inner",
        cost=3000,
    )(now, base, fwd, med, *x_messages, *y_messages)
    slab = ((16 // shares * 8, depth), F32)
    outer = ((fields, len(OUTER) * ROWS, depth), F32)
    if not corners:
        corners = [jnp.zeros((2, 2, 32, depth), F32)] * len(x_rounds)
    edge, own_share, *sent = call(
        functools.partial(edge_kernel, events, x_rounds, y_rounds, shares),
        [outer] + [slab] * shares,
        [pltpu.VMEM] * (9 + len(corners)),
        [
            outer,
            outer,
            ((4, len(OUTER) * ROWS, depth), F32),
            ((len(COEFFICIENTS), 5 * ROWS, depth), F32),
            ((shares,) + slab[0], F32),
        ],
        "edges",
    )(*corners, here, start, stored, tall_medium, coef, then, part, fwd, med)
    pieces = [own_share]
    for m in reversed(range(1, shares)):
        pairs = [(i, i ^ m) for i in range(shares)]
        pieces.append(lax.ppermute(sent[m - 1], "ev", pairs))
    mid, after = call(
        functools.partial(second_kernel, events),
        [own, own],
        [pltpu.VMEM] * 7,
        name="second",
    )(now, extra, med, tall_medium, coef, then, edge)
    shear, density = call(
        functools.partial(finish_kernel, shares, 1.0 / (events * shares)),
        [((tile, depth // shares), F32)] * 2,
        [pltpu.VMEM] * shares,
        name="finish",
    )(*pieces)
    shape = adjoint_now.shape
    grad = (width_x, width_y, depth // shares)
    return mid.reshape(shape), after.reshape(shape), shear.reshape(grad), density.reshape(grad)


def solution(mesh):
    in_specs = (
        P("ev", None, "gx", "gy", None),
        P("ev", None, "gx", "gy", None),
        P("ev", None, None, "gx", "gy", None),
        P(None, "gx", "gy", None),
        P("gx", "gy", None),
        P("ev", None, None, "gx", "gy", None),
    )
    out_specs = (
        P("ev", None, "gx", "gy", None),
        P("ev", None, "gx", "gy", None),
        P("gx", "gy", "ev"),
        P("gx", "gy", "ev"),
    )
    return jax.shard_map(body, mesh=mesh, in_specs=in_specs, out_specs=out_specs, check_vma=False)
```

```python
import functools
import itertools

import jax
import jax.numpy as jnp
from jax import lax
from jax.experimental import pallas as pl
from jax.experimental.pallas import tpu as pltpu
from jax.sharding import PartitionSpec as P

STEP_FACTOR = 0.01
F32, BF16 = jnp.float32, jnp.bfloat16
SHEAR, LAME, BUOY, INV = range(4)
ROWS = 16
FULL = pl.BlockSpec(memory_space=pltpu.VMEM)
VMEM_LIMIT = 40 * 1024 * 1024
PACK_LIMIT = 60 * 1024 * 1024


def rounds_of(count):
    return "AB"[: max(0, min(2, count - 1))]


def swap(values, axis, name):
    names = ("ev", "gx", "gy")
    sizes = [lax.axis_size(a) for a in names]
    along = names.index(axis)
    pairs = []
    for source in itertools.product(*map(range, sizes)):
        target = list(source)
        up = (source[along] % 2 == 0) == (name == "A")
        target[along] += 1 if up else -1
        if not 0 <= target[along] < sizes[along]:
            target = [source[0] ^ 1, *source[1:]]
        flat = [(s[0] * sizes[1] + s[1]) * sizes[2] + s[2] for s in (source, target)]
        pairs.append(tuple(flat))
    return lax.ppermute(values, names, pairs)


def linked(axis, name):
    other = lax.axis_index(axis) + jnp.where(upward(axis, name), 1, -1)
    return jnp.logical_and(other >= 0, other < lax.axis_size(axis))


def upward(axis, name):
    even = lax.rem(lax.axis_index(axis), 2) == 0
    return even if name == "A" else jnp.logical_not(even)


def split(values):
    high = values.astype(BF16)
    low = (values - high.astype(F32)).astype(BF16)
    return jnp.concatenate([high, low], axis=0)


def join(tile):
    tile = tile.astype(F32)
    return tile[:8] + tile[8:]


def force_field(cells, force_rows, width):
    depth = 128
    count = cells.shape[1]
    place = lax.broadcasted_iota(jnp.int32, (width, count), 0)
    mask = place == cells // depth
    level = lax.broadcasted_iota(jnp.int32, (depth, count), 0)
    hot = jnp.where(level == lax.rem(cells, depth), 1.0, 0.0).astype(BF16)
    left = jnp.concatenate([jnp.where(mask, row, 0.0) for row in force_rows], axis=0)
    total = None
    for _ in range(3):
        part = left.astype(BF16)
        left = left - part.astype(F32)
        term = lax.dot_general(part, hot, (((1,), (1,)), ((), ())), preferred_element_type=F32)
        total = term if total is None else total + term
    return total


def pack_kernel(events, x_rounds, y_rounds, *refs):
    fields = 3 * events
    count = 6
    sources = refs[:count]
    messages = refs[count : count + len(x_rounds) + len(y_rounds)]
    now, prev, fwd, med, cells, force, base, stored, arrived = refs[count + len(messages) :]
    now_in, prev_in, fwd_in, med_in, cells_in, force_in = sources
    pairs = [(cells_in, cells), (force_in, force), (now_in, now), (prev_in, prev), (med_in, med)]
    for e in range(events):
        pairs.append((fwd_in.at[pl.ds(e * 12 + 3, 6)], fwd.at[pl.ds(e * 6, 6)]))
    copies = [
        pltpu.make_async_copy(source, target, arrived.at[k])
        for k, (source, target) in enumerate(pairs)
    ]
    for copy in copies:
        copy.start()
    for copy in copies[:2]:
        copy.wait()
    rows = [force[e, 0, c, 0] for e in range(events) for c in range(3)]
    pushed = force_field(cells[0], rows, 64)
    for copy in copies[2:]:
        copy.wait()
    for f in range(fields):
        base[f] = (
            2.0 * now[f] - prev[f] + STEP_FACTOR * med[BUOY] * pushed[f * 64 : (f + 1) * 64]
        )
        e, c = f // 3, f % 3
        for t in range(2):
            stored[f * 2 + t] = fwd[(e * 2 + t) * 3 + c].astype(F32).reshape(64, 128)

    def fill(message, pick):
        for f in range(fields):
            message[2 * f] = split(pick(now, f, 1))
            message[2 * f + 1] = split(pick(now, f, 2))
            message[2 * fields + f] = split(pick(base, f, 1))
            message[3 * fields + f] = jnp.concatenate(
                [pick(stored, 2 * f, 1), pick(stored, 2 * f + 1, 1)], axis=0
            ).astype(BF16)
        for k, m in enumerate((SHEAR, LAME, INV)):
            message[4 * fields + k] = jnp.concatenate(
                [pick(med, m, 1), pick(med, m, 2)], axis=0
            ).astype(BF16)
        edge = pick(med, BUOY, 1)
        message[4 * fields + 3] = jnp.concatenate([edge, edge], axis=0).astype(BF16)

    for k, name in enumerate(x_rounds):
        up = upward("gx", name)

        def pick_x(ref, index, ring, up=up):
            row = jnp.where(up, 8 - ring, ring - 1)
            return ref[index, pl.ds(pl.multiple_of(row * 8, 8), 8), :]

        fill(messages[k], pick_x)
    for k, name in enumerate(y_rounds):
        up = upward("gy", name)

        def pick_y(ref, index, ring, up=up):
            row = jnp.where(up, 8 - ring, ring - 1)
            return ref[index, pl.ds(row, 8, stride=8), :]

        fill(messages[len(x_rounds) + k], pick_y)


def masked(message, axis, name):
    if name == "A" and lax.axis_size(axis) % 2 == 0:
        return lambda index: message[index]
    real = linked(axis, name)
    return lambda index: jnp.where(real, message[index].astype(F32), 0.0).astype(BF16)


def corner_kernel(fields, x_rounds, y_rounds, *refs):
    sides = refs[: len(y_rounds)]
    outs = refs[len(y_rounds) : len(y_rounds) + len(x_rounds)]
    rows = refs[-1]
    for s, name in enumerate(y_rounds):
        side = masked(sides[s], "gy", name)
        for k in range(3 * fields):
            rows[s, pl.ds(k * 8, 8), :] = join(side(k))
        for k in range(3):
            tile = side(4 * fields + k).astype(F32)
            rows[s, pl.ds((3 * fields + 2 * k) * 8, 16), :] = tile
        tile = side(4 * fields + 3).astype(F32)
        rows[s, pl.ds((3 * fields + 6) * 8, 16), :] = tile
        for k in range(3 * fields + 8, 32):
            rows[s, pl.ds(k * 8, 8), :] = jnp.zeros((8, 128), F32)
    for k, name in enumerate(x_rounds):
        up = upward("gx", name)
        for s in range(len(y_rounds)):
            for ring in (1, 2):
                row = jnp.where(up, 8 - ring, ring - 1)
                outs[k][s, ring - 1] = rows[s, pl.ds(row, 32, stride=8), :]


def shift_z(values, step):
    depth = values.shape[-1]
    lane = lax.broadcasted_iota(jnp.int32, values.shape, values.ndim - 1)
    moved = pltpu.roll(values, (-step) % depth, axis=values.ndim - 1)
    return jnp.where(lane == (depth - 1 if step > 0 else 0), 0.0, moved)


def shift_y(values, step):
    return pltpu.roll(values, (-step) % ROWS, axis=0)


def row_of(ref, index, row):
    return ref[index, pl.ds(row * ROWS, ROWS), :]


COEFFICIENTS = (
    ("own_x", "other_x", "own_y", "other_y", "own_z", "other_z", "cross", "cross_z")
    + ("own_y_down", "other_y_down", "own_z_down", "other_z_down")
)


def coefficients(medium, row, ahead=True):
    def both_of(row):
        return medium(LAME, row) + 2.0 * medium(SHEAR, row)

    shear, lame, inverse = (medium(m, row) for m in (SHEAR, LAME, INV))
    both = both_of(row)
    values = {}
    if ahead:
        values["own_x"] = 0.5 * (both + both_of(row + 1))
        values["other_x"] = 0.5 * (shear + medium(SHEAR, row + 1))
    for tail, step in (("", 1), ("_down", -1)):
        values["own_y" + tail] = 0.5 * (both + shift_y(both, step))
        values["other_y" + tail] = 0.5 * (shear + shift_y(shear, step))
        spacing = 0.25 * (inverse + shift_z(inverse, step))
        values["own_z" + tail] = spacing * (both + shift_z(both, step))
        values["other_z" + tail] = spacing * (shear + shift_z(shear, step))
    values["cross"] = 0.25 * (lame + shear)
    values["cross_z"] = values["cross"] * inverse
    return values


class Event:
    def __init__(self, value):
        self.value = functools.cache(value)
        self.y = functools.cache(lambda c, row, step: shift_y(self.value(c, row), step))
        self.z = functools.cache(lambda c, row, step: shift_z(self.value(c, row), step))

    def slopes(self, c, row):
        return (
            (self.value(c, row + 1) - self.value(c, row - 1))[:8],
            (self.y(c, row, 1) - self.y(c, row, -1))[:8],
            (self.z(c, row, 1) - self.z(c, row, -1))[:8],
        )

    def operator(self, faces):
        value = self.value

        @functools.cache
        def slope(d, row):
            if d == 0:
                return faces("cross", row) * (value(0, row + 1) - value(0, row - 1))
            if d == 1:
                return faces("cross", row) * (self.y(1, row, 1) - self.y(1, row, -1))
            return faces("cross_z", row) * (self.z(2, row, 1) - self.z(2, row, -1))

        @functools.cache
        def flux_x(c, row):
            kind = "own_x" if c == 0 else "other_x"
            return faces(kind, row) * (value(c, row + 1) - value(c, row))

        def apply(row):
            results = []
            for c in range(3):
                here = value(c, row)
                total = flux_x(c, row) - flux_x(c, row - 1)
                kind = "own_y" if c == 1 else "other_y"
                total = total + (
                    faces(kind, row) * (self.y(c, row, 1) - here)
                    - faces(kind + "_down", row) * (here - self.y(c, row, -1))
                )
                kind = "own_z" if c == 2 else "other_z"
                upright = faces(kind, row) * (self.z(c, row, 1) - here) - faces(
                    kind + "_down", row
                ) * (here - self.z(c, row, -1))
                if c == 0:
                    total = total + (
                        (slope(1, row + 1) + slope(2, row + 1))
                        - (slope(1, row - 1) + slope(2, row - 1))
                    )
                elif c == 1:
                    mixed = slope(0, row) + slope(2, row)
                    total = total + (shift_y(mixed, 1) - shift_y(mixed, -1))
                else:
                    mixed = slope(0, row) + slope(1, row)
                    upright = upright + (shift_z(mixed, 1) - shift_z(mixed, -1))
                results.append(total + faces("inverse", row) * upright)
            return results

        return apply


def x_row(up, ring):
    return jnp.where(up, 9 + ring, 2 - ring)


def y_place(up, ring):
    return jnp.where(up, 7 + ring, ROWS - ring)


def tile_row(ref, index, row):
    return ref[index, pl.ds((row - 2) * 8, 8), :]


def own_kernel(events, now, prev, med, cells, force, base, extra):
    fields = 3 * events
    rows = [force[e, s, c, 0] for s in range(2) for e in range(events) for c in range(3)]
    pushed = force_field(cells[0], rows, 64)
    scale = STEP_FACTOR * med[BUOY]
    for f in range(fields):
        base[f] = 2.0 * now[f] - prev[f] + scale * pushed[f * 64 : (f + 1) * 64]
        extra[f] = scale * pushed[(fields + f) * 64 : (fields + f + 1) * 64]


def add_to(sums, key, value):
    sums[key] = sums[key] + value if key in sums else value


def inner_kernel(events, x_rounds, y_rounds, now, base, fwd, med, *refs):
    fields = 3 * events
    x_messages, refs = refs[: len(x_rounds)], refs[len(x_rounds) :]
    y_messages, refs = refs[: len(y_rounds)], refs[len(y_rounds) :]
    here, start, stored, medium, coef, then, part = refs

    for f in range(fields):
        e, c = f // 3, f % 3
        for x in range(8):
            spot = pl.ds((x + 2) * ROWS, 8)
            here[f, spot, :] = now[f, pl.ds(x * 8, 8), :]
            start[f, spot, :] = base[f, pl.ds(x * 8, 8), :]
            for t in range(2):
                stored[2 * f + t, spot, :] = fwd[(e * 4 + t + 1) * 3 + c, x].astype(F32)
    for m in range(4):
        for x in range(8):
            medium[m, pl.ds((x + 2) * ROWS, 8), :] = med[m, pl.ds(x * 8, 8), :]

    def place(tile, put):
        for f in range(fields):
            put(here, f, 1, join(tile(2 * f)))
            put(here, f, 2, join(tile(2 * f + 1)))
            put(start, f, 1, join(tile(2 * fields + f)))
            both = tile(3 * fields + f).astype(F32)
            put(stored, 2 * f, 1, both[:8])
            put(stored, 2 * f + 1, 1, both[8:])
        for k, m in enumerate((SHEAR, LAME, INV)):
            both = tile(4 * fields + k).astype(F32)
            put(medium, m, 1, both[:8])
            put(medium, m, 2, both[8:])
        put(medium, BUOY, 1, tile(4 * fields + 3).astype(F32)[:8])

    def nothing(_):
        return jnp.zeros((16, 128), BF16)

    for k, name in enumerate("AB"):
        up = upward("gx", name)

        def put_x(ref, index, ring, values, up=up):
            row = pl.multiple_of(x_row(up, ring) * ROWS, ROWS)
            ref[index, pl.ds(row, 8), :] = values

        place(masked(x_messages[k], "gx", name) if k < len(x_rounds) else nothing, put_x)
    for k, name in enumerate("AB"):
        up = upward("gy", name)

        def put_y(ref, index, ring, values, up=up):
            ref[index, pl.ds(2 * ROWS + y_place(up, ring), 8, stride=ROWS), :] = values

        place(masked(y_messages[k], "gy", name) if k < len(y_rounds) else nothing, put_y)

    for row in range(1, 11):
        values = coefficients(lambda m, r: row_of(medium, m, r), row, row < 10)
        for name, value in values.items():
            coef[COEFFICIENTS.index(name), pl.ds(row * ROWS, ROWS), :] = value

    def faces(name, row):
        if name == "inverse":
            return row_of(medium, INV, row)
        return row_of(coef, COEFFICIENTS.index(name), row)

    sums = {}
    for e in range(events):
        first = Event(lambda c, row, e=e: row_of(here, 3 * e + c, row))
        apply = first.operator(faces)
        waves = [
            Event(lambda c, row, e=e, t=t: row_of(stored, 2 * (3 * e + c) + t, row))
            for t in range(2)
        ]
        for row in range(2, 10):
            if 3 <= row <= 8:
                scale = STEP_FACTOR * row_of(medium, BUOY, row)
                for c, result in enumerate(apply(row)):
                    f = 3 * e + c
                    then[f, pl.ds(row * ROWS, ROWS), :] = row_of(start, f, row) + scale * result
            gather(sums, first, waves[0], fwd, e, 0, row)
        second = Event(lambda c, row, e=e: row_of(then, 3 * e + c, row))
        for row in range(4, 8):
            gather(sums, second, waves[1], fwd, e, 1, row)
    for row in range(2, 10):
        inverse = tile_row(med, INV, row)
        shear = sums["lateral", row] + inverse * inverse * sums["upright", row]
        part[0, pl.ds((row - 2) * 8, 8), :] = -0.25 * shear
        part[1, pl.ds((row - 2) * 8, 8), :] = -sums["density", row]


def gather(sums, field, wave, fwd, e, t, row):
    for c in range(3):
        ax, ay, az = field.slopes(c, row)
        ux, uy, uz = wave.slopes(c, row)
        newer = fwd[(e * 4 + t) * 3 + c, row - 2].astype(F32)
        older = fwd[(e * 4 + t + 2) * 3 + c, row - 2].astype(F32)
        bend = newer - 2.0 * wave.value(c, row)[:8] + older
        add_to(sums, ("lateral", row), ax * ux + ay * uy)
        add_to(sums, ("upright", row), az * uz)
        add_to(sums, ("density", row), field.value(c, row)[:8] * bend)


OUTER = (0, 1, 10, 11)
EDGES = (1, 2, 9, 10)


def edge_kernel(events, x_rounds, y_rounds, shares, *refs):
    fields = 3 * events
    corners, refs = refs[: len(x_rounds)], refs[len(x_rounds) :]
    (here, start, stored, medium, coef, then, part, fwd, med), refs = refs[:9], refs[9:]
    edge, own_share, *sent = refs[: 1 + shares]
    outer, outer_start, outer_medium, outer_coef, slabs = refs[1 + shares :]

    for k, row in enumerate(OUTER):
        spot = pl.ds(k * ROWS, ROWS)
        for f in range(fields):
            outer[f, spot, :] = row_of(here, f, row)
            if row in EDGES:
                outer_start[f, spot, :] = row_of(start, f, row)
        for m in range(4):
            outer_medium[m, spot, :] = row_of(medium, m, row)
    for kx, name_x in enumerate("AB"):
        for ky, name_y in enumerate("AB"):
            up_x, up_y = upward("gx", name_x), upward("gy", name_y)
            for ring_x in (1, 2):
                for ring_y in (1, 2):
                    place = jnp.where(up_x, 1 + ring_x, 2 - ring_x)
                    spot = place * ROWS + y_place(up_y, ring_y)

                    def move(ref, index, k):
                        if kx < len(x_rounds) and ky < len(y_rounds):
                            values = corners[kx][ky, ring_x - 1, pl.ds(k, 1), :]
                            if name_x == "B" or lax.axis_size("gx") % 2:
                                values = jnp.where(linked("gx", name_x), values, 0.0)
                        else:
                            values = jnp.zeros((1, 128), F32)
                        ref[index, pl.ds(spot, 1), :] = values

                    for f in range(fields):
                        move(outer, f, 2 * f + ring_y - 1)
                        if ring_x == 1 and ring_y == 1:
                            move(outer_start, f, 2 * fields + f)
                    for k, m in enumerate((SHEAR, LAME, INV)):
                        move(outer_medium, m, 3 * fields + 2 * k + ring_y - 1)
                    if ring_x == 1 and ring_y == 1:
                        move(outer_medium, BUOY, 3 * fields + 6)

    def outer_or(ref, full):
        def pick(index, row):
            if row in OUTER:
                return row_of(ref, index, OUTER.index(row))
            return row_of(full, index, row)

        return pick

    field_row, start_row = outer_or(outer, here), outer_or(outer_start, start)
    medium_row = outer_or(outer_medium, medium)
    fresh = (0, 1, 9, 10, 11)
    for k, row in enumerate(fresh):
        for name, value in coefficients(medium_row, row, row < 11).items():
            outer_coef[COEFFICIENTS.index(name), pl.ds(k * ROWS, ROWS), :] = value

    def faces(name, row):
        if name == "inverse":
            return medium_row(INV, row)
        index = COEFFICIENTS.index(name)
        if row in fresh:
            return row_of(outer_coef, index, fresh.index(row))
        return row_of(coef, index, row)

    def then_row(f, row):
        if row in EDGES:
            return row_of(edge, f, EDGES.index(row))
        return row_of(then, f, row)

    sums = {}
    for e in range(events):
        apply = Event(lambda c, row, e=e: field_row(3 * e + c, row)).operator(faces)
        for k, row in enumerate(EDGES):
            scale = STEP_FACTOR * medium_row(BUOY, row)
            for c, result in enumerate(apply(row)):
                f = 3 * e + c
                edge[f, pl.ds(k * ROWS, ROWS), :] = start_row(f, row) + scale * result
        second = Event(lambda c, row, e=e: then_row(3 * e + c, row))
        wave = Event(lambda c, row, e=e: row_of(stored, 2 * (3 * e + c) + 1, row))
        for row in (2, 3, 8, 9):
            gather(sums, second, wave, fwd, e, 1, row)
    grads = [[], []]
    for row in range(2, 10):
        shear, density = tile_row(part, 0, row), tile_row(part, 1, row)
        if row in (2, 3, 8, 9):
            inverse = tile_row(med, INV, row)
            more = sums["lateral", row] + inverse * inverse * sums["upright", row]
            shear = shear - 0.25 * more
            density = density - sums["density", row]
        grads[0].append(shear)
        grads[1].append(density)
    grads = grads[0] + grads[1]
    piece = 128 // shares
    quarter = lax.broadcasted_iota(jnp.int32, (8, 128), 1) // piece
    per = len(grads) // shares
    for j in range(shares):
        for r in range(per):
            tile = None
            for g in range(shares):
                source = grads[r * shares + g]
                moved = pltpu.roll(source, ((g - j) * piece) % 128, axis=1) if g != j else source
                tile = moved if tile is None else jnp.where(quarter == g, moved, tile)
            slabs[j, pl.ds(r * 8, 8), :] = tile
    me = lax.axis_index("ev")
    own_share[...] = slabs[me]
    for m in range(1, shares):
        sent[m - 1][...] = slabs[me ^ m]


def second_kernel(events, now, extra, med, medium, coef, then, edge, mid, after):
    def faces(name, row):
        if name == "inverse":
            return row_of(medium, INV, row)
        return row_of(coef, COEFFICIENTS.index(name), row)

    def then_row(f, row):
        if row in EDGES:
            return row_of(edge, f, EDGES.index(row))
        return row_of(then, f, row)

    for e in range(events):
        apply = Event(lambda c, row, e=e: then_row(3 * e + c, row)).operator(faces)
        for row in range(2, 10):
            spot = pl.ds((row - 2) * 8, 8)
            scale = STEP_FACTOR * tile_row(med, BUOY, row)
            for c, result in enumerate(apply(row)):
                f = 3 * e + c
                current = then_row(f, row)[:8]
                mid[f, spot, :] = current
                after[f, spot, :] = (
                    2.0 * current - now[f, spot, :] + extra[f, spot, :] + scale * result[:8]
                )


def finish_kernel(shares, scale, *refs):
    pieces, (shear, density) = refs[:shares], refs[shares:]
    total = pieces[0][...]
    for piece in pieces[1:]:
        total = total + piece[...]
    width = 128 // shares
    for v in range(16):
        g, r = v % shares, v // shares
        tile = total[r * 8 : (r + 1) * 8]
        if g:
            tile = pltpu.roll(tile, (-g * width) % 128, axis=1)
        out = shear if v < 8 else density
        out[pl.ds((v % 8) * 8, 8), :] = tile[:, :width] * scale


def call(kernel, outs, ins, scratch=(), name=None, limit=VMEM_LIMIT, cost=1000):
    return pl.pallas_call(
        kernel,
        out_shape=[jax.ShapeDtypeStruct(s, d) for s, d in outs],
        in_specs=[pl.BlockSpec(memory_space=m) for m in ins],
        scratch_shapes=[s if not isinstance(s, tuple) else pltpu.VMEM(*s) for s in scratch],
        compiler_params=pltpu.CompilerParams(vmem_limit_bytes=limit),
        cost_estimate=pl.CostEstimate(
            flops=cost * 1024, bytes_accessed=cost * 1024, transcendentals=0
        ),
        name=name,
    )


def body(adjoint_now, adjoint_prev, forward, medium, drm_cells, drm_force):
    events, _, width_x, width_y, depth = adjoint_now.shape
    fields = 3 * events
    tile = width_x * width_y
    shares = lax.axis_size("ev")
    x_rounds, y_rounds = rounds_of(lax.axis_size("gx")), rounds_of(lax.axis_size("gy"))
    now = adjoint_now.reshape(fields, tile, depth)
    prev = adjoint_prev.reshape(fields, tile, depth)
    fwd = forward.reshape(events * 12, width_x, width_y, depth)
    med = medium.reshape(4, tile, depth)
    own = ((fields, tile, depth), F32)
    tall = 12 * ROWS

    messages = call(
        functools.partial(pack_kernel, events, x_rounds, y_rounds),
        [((4 * fields + 4, 16, depth), BF16)] * (len(x_rounds) + len(y_rounds)),
        [pltpu.HBM] * 6,
        [
            own,
            own,
            ((2 * fields, width_x, width_y, depth), BF16),
            ((4, tile, depth), F32),
            (drm_cells.shape, drm_cells.dtype),
            (drm_force.shape, F32),
            own,
            ((2 * fields, tile, depth), F32),
            pltpu.SemaphoreType.DMA((5 + events,)),
        ],
        "pack",
        PACK_LIMIT,
    )(now, prev, fwd, med, drm_cells, drm_force)
    y_messages = [swap(m, "gy", r) for m, r in zip(messages[len(x_rounds) :], y_rounds)]
    x_messages = [swap(m, "gx", r) for m, r in zip(messages, x_rounds)]
    base, extra = call(
        functools.partial(own_kernel, events),
        [own, own],
        [pltpu.VMEM] * 5,
        name="own",
    )(now, prev, med, drm_cells, drm_force)
    corners = []
    if x_rounds and y_rounds:
        corners = call(
            functools.partial(corner_kernel, fields, x_rounds, y_rounds),
            [((len(y_rounds), 2, 32, depth), F32)] * len(x_rounds),
            [pltpu.VMEM] * len(y_rounds),
            [((len(y_rounds), 32 * 8, depth), F32)],
            "corners",
        )(*y_messages)
        corners = [swap(m, "gx", r) for m, r in zip(corners, x_rounds)]

    wide = ((fields, tall, depth), F32)
    here, start, stored, tall_medium, coef, then, part = call(
        functools.partial(inner_kernel, events, x_rounds, y_rounds),
        [
            wide,
            wide,
            ((2 * fields, tall, depth), F32),
            ((4, tall, depth), F32),
            ((len(COEFFICIENTS), tall, depth), F32),
            wide,
            ((2, tile, depth), F32),
        ],
        [pltpu.VMEM] * (4 + len(x_messages) + len(y_messages)),
        name="inner",
        cost=3000,
    )(now, base, fwd, med, *x_messages, *y_messages)
    slab = ((16 // shares * 8, depth), F32)
    outer = ((fields, len(OUTER) * ROWS, depth), F32)
    if not corners:
        corners = [jnp.zeros((2, 2, 32, depth), F32)] * len(x_rounds)
    edge, own_share, *sent = call(
        functools.partial(edge_kernel, events, x_rounds, y_rounds, shares),
        [outer] + [slab] * shares,
        [pltpu.VMEM] * (9 + len(corners)),
        [
            outer,
            outer,
            ((4, len(OUTER) * ROWS, depth), F32),
            ((len(COEFFICIENTS), 5 * ROWS, depth), F32),
            ((shares,) + slab[0], F32),
        ],
        "edges",
    )(*corners, here, start, stored, tall_medium, coef, then, part, fwd, med)
    pieces = [own_share]
    for m in reversed(range(1, shares)):
        pairs = [(i, i ^ m) for i in range(shares)]
        pieces.append(lax.ppermute(sent[m - 1], "ev", pairs))
    mid, after = call(
        functools.partial(second_kernel, events),
        [own, own],
        [pltpu.VMEM] * 7,
        name="second",
    )(now, extra, med, tall_medium, coef, then, edge)
    shear, density = call(
        functools.partial(finish_kernel, shares, 1.0 / (events * shares)),
        [((tile, depth // shares), F32)] * 2,
        [pltpu.VMEM] * shares,
        name="finish",
    )(*pieces)
    shape = adjoint_now.shape
    grad = (width_x, width_y, depth // shares)
    return mid.reshape(shape), after.reshape(shape), shear.reshape(grad), density.reshape(grad)


def solution(mesh):
    in_specs = (
        P("ev", None, "gx", "gy", None),
        P("ev", None, "gx", "gy", None),
        P("ev", None, None, "gx", "gy", None),
        P(None, "gx", "gy", None),
        P("gx", "gy", None),
        P("ev", None, None, "gx", "gy", None),
    )
    out_specs = (
        P("ev", None, "gx", "gy", None),
        P("ev", None, "gx", "gy", None),
        P("gx", "gy", "ev"),
        P("gx", "gy", "ev"),
    )
    return jax.shard_map(body, mesh=mesh, in_specs=in_specs, out_specs=out_specs, check_vma=False)
```

```python
import functools
import itertools

import jax
import jax.numpy as jnp
from jax import lax
from jax.experimental import pallas as pl
from jax.experimental.pallas import tpu as pltpu
from jax.sharding import PartitionSpec as P

STEP_FACTOR = 0.01
F32, BF16 = jnp.float32, jnp.bfloat16
SHEAR, LAME, BUOY, INV = range(4)
ROWS = 16
VMEM_LIMIT = 40 * 1024 * 1024
PACK_LIMIT = 60 * 1024 * 1024


def rounds_of(count):
    return "AB"[: max(0, min(2, count - 1))]


def swap(values, rounds):
    names = ("ev", "gx", "gy")
    sizes = [lax.axis_size(a) for a in names]
    pairs = []
    for source in itertools.product(*map(range, sizes)):
        target = list(source)
        for axis, name in rounds.items():
            along = names.index(axis)
            target[along] += 1 if (source[along] % 2 == 0) == (name == "A") else -1
        if not all(0 <= t < size for t, size in zip(target, sizes)):
            target = [source[0] ^ 1, *source[1:]]
        flat = [(s[0] * sizes[1] + s[1]) * sizes[2] + s[2] for s in (source, target)]
        pairs.append(tuple(flat))
    return lax.ppermute(values, names, pairs)


def linked(axis, name):
    other = lax.axis_index(axis) + jnp.where(upward(axis, name), 1, -1)
    return jnp.logical_and(other >= 0, other < lax.axis_size(axis))


def upward(axis, name):
    even = lax.rem(lax.axis_index(axis), 2) == 0
    return even if name == "A" else jnp.logical_not(even)


def split(values):
    high = values.astype(BF16)
    low = (values - high.astype(F32)).astype(BF16)
    return jnp.concatenate([high, low], axis=0)


def join(tile):
    tile = tile.astype(F32)
    return tile[:8] + tile[8:]


def force_field(cells, force_rows, width):
    depth = 128
    count = cells.shape[1]
    place = lax.broadcasted_iota(jnp.int32, (width, count), 0)
    mask = place == cells // depth
    level = lax.broadcasted_iota(jnp.int32, (depth, count), 0)
    hot = jnp.where(level == lax.rem(cells, depth), 1.0, 0.0).astype(BF16)
    left = jnp.concatenate([jnp.where(mask, row, 0.0) for row in force_rows], axis=0)
    total = None
    for _ in range(3):
        part = left.astype(BF16)
        left = left - part.astype(F32)
        term = lax.dot_general(part, hot, (((1,), (1,)), ((), ())), preferred_element_type=F32)
        total = term if total is None else total + term
    return total


def pack_kernel(events, x_rounds, y_rounds, *refs):
    fields = 3 * events
    total = len(x_rounds) + len(y_rounds) + len(x_rounds) * len(y_rounds)
    sources, targets, refs = refs[:6], refs[6 : 6 + total], refs[6 + total :]
    now, prev, fwd, med, cells, force, base, stored, arrived, left = refs[:10]
    messages = refs[10:]
    now_in, prev_in, fwd_in, med_in, cells_in, force_in = sources
    pairs = [(cells_in, cells), (force_in, force), (now_in, now), (prev_in, prev), (med_in, med)]
    for e in range(events):
        pairs.append((fwd_in.at[pl.ds(e * 12 + 3, 6)], fwd.at[pl.ds(e * 6, 6)]))
    copies = [
        pltpu.make_async_copy(source, target, arrived.at[k])
        for k, (source, target) in enumerate(pairs)
    ]
    for copy in copies:
        copy.start()
    for copy in copies[:2]:
        copy.wait()
    rows = [force[e, 0, c, 0] for e in range(events) for c in range(3)]
    pushed = force_field(cells[0], rows, 64)
    for copy in copies[2:]:
        copy.wait()
    scale = STEP_FACTOR * med[pl.ds(BUOY * 64, 64), :]
    for f in range(fields):
        spot = pl.ds(f * 64, 64)
        base[spot, :] = 2.0 * now[spot, :] - prev[spot, :] + scale * pushed[f * 64 : (f + 1) * 64]
        e, c = f // 3, f % 3
        for t in range(2):
            part = fwd[(e * 2 + t) * 3 + c].astype(F32).reshape(64, 128)
            stored[pl.ds((f * 2 + t) * 64, 64), :] = part

    def fill(message, pick):
        for f in range(fields):
            message[2 * f] = split(pick(now, f, 1))
            message[2 * f + 1] = split(pick(now, f, 2))
            message[2 * fields + f] = split(pick(base, f, 1))
            message[3 * fields + f] = jnp.concatenate(
                [pick(stored, 2 * f, 1), pick(stored, 2 * f + 1, 1)], axis=0
            ).astype(BF16)
        for k, m in enumerate((SHEAR, LAME, INV)):
            message[4 * fields + k] = jnp.concatenate(
                [pick(med, m, 1), pick(med, m, 2)], axis=0
            ).astype(BF16)
        edge = pick(med, BUOY, 1)
        message[4 * fields + 3] = jnp.concatenate([edge, edge], axis=0).astype(BF16)

    def face(axis, name, ring):
        return jnp.where(upward(axis, name), 8 - ring, ring - 1)

    out = []

    def send():
        k = len(out)
        out.append(pltpu.make_async_copy(messages[k], targets[k], left.at[k]))
        out[k].start()

    for name in y_rounds:

        def pick_y(ref, index, ring, name=name):
            return ref[pl.ds(index * 64 + face("gy", name, ring), 8, stride=8), :]

        fill(messages[len(out)], pick_y)
        send()
    for name in x_rounds:

        def pick_x(ref, index, ring, name=name):
            row = pl.multiple_of(face("gx", name, ring) * 8, 8)
            return ref[pl.ds(index * 64 + row, 8), :]

        fill(messages[len(out)], pick_x)
        send()
    for name_x in x_rounds:
        for name_y in y_rounds:
            message = messages[len(out)]
            for ring_x in (1, 2):
                for ring_y in (1, 2):
                    cell = face("gx", name_x, ring_x) * 8 + face("gy", name_y, ring_y)
                    target = message.at[ring_x - 1, ring_y - 1]
                    target[pl.ds(0, fields), :] = now[pl.ds(cell, fields, stride=64), :]
                    target[pl.ds(fields, 4), :] = med[pl.ds(cell, 4, stride=64), :]
                    picked = base[pl.ds(cell, fields, stride=64), :]
                    target[pl.ds(fields + 4, fields), :] = picked
            send()
    for copy in out:
        copy.wait()


def masked(message, axis, name):
    if name == "A" and lax.axis_size(axis) % 2 == 0:
        return lambda index: message[index]
    real = linked(axis, name)
    return lambda index: jnp.where(real, message[index].astype(F32), 0.0).astype(BF16)


def shift_z(values, step):
    depth = values.shape[-1]
    lane = lax.broadcasted_iota(jnp.int32, values.shape, values.ndim - 1)
    moved = pltpu.roll(values, (-step) % depth, axis=values.ndim - 1)
    return jnp.where(lane == (depth - 1 if step > 0 else 0), 0.0, moved)


def shift_y(values, step):
    return pltpu.roll(values, (-step) % ROWS, axis=0)


def row_of(ref, index, row):
    return ref[index, pl.ds(row * ROWS, ROWS), :]


COEFFICIENTS = (
    ("own_x", "other_x", "own_y", "other_y", "own_z", "other_z", "cross", "cross_z")
    + ("own_y_down", "other_y_down", "own_z_down", "other_z_down")
)


def coefficients(medium, row, ahead=True):
    def both_of(row):
        return medium(LAME, row) + 2.0 * medium(SHEAR, row)

    shear, lame, inverse = (medium(m, row) for m in (SHEAR, LAME, INV))
    both = both_of(row)
    values = {}
    if ahead:
        values["own_x"] = 0.5 * (both + both_of(row + 1))
        values["other_x"] = 0.5 * (shear + medium(SHEAR, row + 1))
    for tail, step in (("", 1), ("_down", -1)):
        values["own_y" + tail] = 0.5 * (both + shift_y(both, step))
        values["other_y" + tail] = 0.5 * (shear + shift_y(shear, step))
        spacing = 0.25 * (inverse + shift_z(inverse, step))
        values["own_z" + tail] = spacing * (both + shift_z(both, step))
        values["other_z" + tail] = spacing * (shear + shift_z(shear, step))
    values["cross"] = 0.25 * (lame + shear)
    values["cross_z"] = values["cross"] * inverse
    return values


class Event:
    def __init__(self, value):
        self.value = functools.cache(value)
        self.y = functools.cache(lambda c, row, step: shift_y(self.value(c, row), step))
        self.z = functools.cache(lambda c, row, step: shift_z(self.value(c, row), step))

    def slopes(self, c, row):
        return (
            (self.value(c, row + 1) - self.value(c, row - 1))[:8],
            (self.y(c, row, 1) - self.y(c, row, -1))[:8],
            (self.z(c, row, 1) - self.z(c, row, -1))[:8],
        )

    def operator(self, faces):
        value = self.value

        @functools.cache
        def slope(d, row):
            if d == 0:
                return faces("cross", row) * (value(0, row + 1) - value(0, row - 1))
            if d == 1:
                return faces("cross", row) * (self.y(1, row, 1) - self.y(1, row, -1))
            return faces("cross_z", row) * (self.z(2, row, 1) - self.z(2, row, -1))

        @functools.cache
        def flux_x(c, row):
            kind = "own_x" if c == 0 else "other_x"
            return faces(kind, row) * (value(c, row + 1) - value(c, row))

        def apply(row):
            results = []
            for c in range(3):
                here = value(c, row)
                total = flux_x(c, row) - flux_x(c, row - 1)
                kind = "own_y" if c == 1 else "other_y"
                total = total + (
                    faces(kind, row) * (self.y(c, row, 1) - here)
                    - faces(kind + "_down", row) * (here - self.y(c, row, -1))
                )
                kind = "own_z" if c == 2 else "other_z"
                upright = faces(kind, row) * (self.z(c, row, 1) - here) - faces(
                    kind + "_down", row
                ) * (here - self.z(c, row, -1))
                if c == 0:
                    total = total + (
                        (slope(1, row + 1) + slope(2, row + 1))
                        - (slope(1, row - 1) + slope(2, row - 1))
                    )
                elif c == 1:
                    mixed = slope(0, row) + slope(2, row)
                    total = total + (shift_y(mixed, 1) - shift_y(mixed, -1))
                else:
                    mixed = slope(0, row) + slope(1, row)
                    upright = upright + (shift_z(mixed, 1) - shift_z(mixed, -1))
                results.append(total + faces("inverse", row) * upright)
            return results

        return apply


def x_row(up, ring):
    return jnp.where(up, 9 + ring, 2 - ring)


def y_place(up, ring):
    return jnp.where(up, 7 + ring, ROWS - ring)


def tile_row(ref, index, row):
    return ref[index, pl.ds((row - 2) * 8, 8), :]


def own_kernel(events, now, prev, med, cells, force, *refs):
    base, extra = refs[-2:]
    fields = 3 * events
    rows = [force[e, s, c, 0] for s in range(2) for e in range(events) for c in range(3)]
    pushed = force_field(cells[0], rows, 64)
    scale = STEP_FACTOR * med[BUOY]
    for f in range(fields):
        base[f] = 2.0 * now[f] - prev[f] + scale * pushed[f * 64 : (f + 1) * 64]
        extra[f] = scale * pushed[(fields + f) * 64 : (fields + f + 1) * 64]


def add_to(sums, key, value):
    sums[key] = sums[key] + value if key in sums else value


def inner_kernel(events, x_rounds, y_rounds, now, base, fwd, med, *refs):
    fields = 3 * events
    x_messages, refs = refs[: len(x_rounds)], refs[len(x_rounds) :]
    y_messages, refs = refs[: len(y_rounds)], refs[len(y_rounds) :]
    here, start, stored, medium, coef, then, part = refs

    for f in range(fields):
        e, c = f // 3, f % 3
        for x in range(8):
            spot = pl.ds((x + 2) * ROWS, 8)
            here[f, spot, :] = now[f, pl.ds(x * 8, 8), :]
            start[f, spot, :] = base[f, pl.ds(x * 8, 8), :]
            for t in range(2):
                stored[2 * f + t, spot, :] = fwd[(e * 4 + t + 1) * 3 + c, x].astype(F32)
    for m in range(4):
        for x in range(8):
            medium[m, pl.ds((x + 2) * ROWS, 8), :] = med[m, pl.ds(x * 8, 8), :]

    def place(tile, put):
        for f in range(fields):
            put(here, f, 1, join(tile(2 * f)))
            put(here, f, 2, join(tile(2 * f + 1)))
            put(start, f, 1, join(tile(2 * fields + f)))
            both = tile(3 * fields + f).astype(F32)
            put(stored, 2 * f, 1, both[:8])
            put(stored, 2 * f + 1, 1, both[8:])
        for k, m in enumerate((SHEAR, LAME, INV)):
            both = tile(4 * fields + k).astype(F32)
            put(medium, m, 1, both[:8])
            put(medium, m, 2, both[8:])
        put(medium, BUOY, 1, tile(4 * fields + 3).astype(F32)[:8])

    def nothing(_):
        return jnp.zeros((16, 128), BF16)

    for k, name in enumerate("AB"):
        up = upward("gx", name)

        def put_x(ref, index, ring, values, up=up):
            row = pl.multiple_of(x_row(up, ring) * ROWS, ROWS)
            ref[index, pl.ds(row, 8), :] = values

        place(masked(x_messages[k], "gx", name) if k < len(x_rounds) else nothing, put_x)
    for k, name in enumerate("AB"):
        up = upward("gy", name)

        def put_y(ref, index, ring, values, up=up):
            ref[index, pl.ds(2 * ROWS + y_place(up, ring), 8, stride=ROWS), :] = values

        place(masked(y_messages[k], "gy", name) if k < len(y_rounds) else nothing, put_y)

    for row in range(1, 11):
        values = coefficients(lambda m, r: row_of(medium, m, r), row, row < 10)
        for name, value in values.items():
            coef[COEFFICIENTS.index(name), pl.ds(row * ROWS, ROWS), :] = value

    def faces(name, row):
        if name == "inverse":
            return row_of(medium, INV, row)
        return row_of(coef, COEFFICIENTS.index(name), row)

    sums = {}
    for e in range(events):
        first = Event(lambda c, row, e=e: row_of(here, 3 * e + c, row))
        apply = first.operator(faces)
        waves = [
            Event(lambda c, row, e=e, t=t: row_of(stored, 2 * (3 * e + c) + t, row))
            for t in range(2)
        ]
        for row in range(2, 10):
            if 3 <= row <= 8:
                scale = STEP_FACTOR * row_of(medium, BUOY, row)
                for c, result in enumerate(apply(row)):
                    f = 3 * e + c
                    then[f, pl.ds(row * ROWS, ROWS), :] = row_of(start, f, row) + scale * result
            gather(sums, first, waves[0], fwd, e, 0, row)
        second = Event(lambda c, row, e=e: row_of(then, 3 * e + c, row))
        for row in range(4, 8):
            gather(sums, second, waves[1], fwd, e, 1, row)
    for row in range(2, 10):
        inverse = tile_row(med, INV, row)
        shear = sums["lateral", row] + inverse * inverse * sums["upright", row]
        part[0, pl.ds((row - 2) * 8, 8), :] = -0.25 * shear
        part[1, pl.ds((row - 2) * 8, 8), :] = -sums["density", row]


def gather(sums, field, wave, fwd, e, t, row):
    for c in range(3):
        ax, ay, az = field.slopes(c, row)
        ux, uy, uz = wave.slopes(c, row)
        newer = fwd[(e * 4 + t) * 3 + c, row - 2].astype(F32)
        older = fwd[(e * 4 + t + 2) * 3 + c, row - 2].astype(F32)
        bend = newer - 2.0 * wave.value(c, row)[:8] + older
        add_to(sums, ("lateral", row), ax * ux + ay * uy)
        add_to(sums, ("upright", row), az * uz)
        add_to(sums, ("density", row), field.value(c, row)[:8] * bend)


OUTER = (0, 1, 10, 11)
EDGES = (1, 2, 9, 10)


def edge_kernel(events, x_rounds, y_rounds, shares, *refs):
    fields = 3 * events
    count = len(x_rounds) * len(y_rounds)
    corners, refs = refs[:count], refs[count:]
    (here, start, stored, medium, coef, then, part, fwd, med), refs = refs[:9], refs[9:]
    edge, own_share, *sent = refs[: 1 + shares]
    outer, outer_start, outer_medium, outer_coef, slabs = refs[1 + shares :]

    height = len(OUTER) * ROWS
    for k, row in enumerate(OUTER):
        for f in range(fields):
            spot = pl.ds(f * height + k * ROWS, ROWS)
            outer[spot, :] = row_of(here, f, row)
            if row in EDGES:
                outer_start[spot, :] = row_of(start, f, row)
        for m in range(4):
            outer_medium[pl.ds(m * height + k * ROWS, ROWS), :] = row_of(medium, m, row)
    for kx, name_x in enumerate("AB"):
        for ky, name_y in enumerate("AB"):
            corner = None
            if kx < len(x_rounds) and ky < len(y_rounds):
                corner = corners[kx * len(y_rounds) + ky]
            up_x, up_y = upward("gx", name_x), upward("gy", name_y)
            real = jnp.logical_and(linked("gx", name_x), linked("gy", name_y))
            for ring_x in (1, 2):
                for ring_y in (1, 2):
                    place = jnp.where(up_x, 1 + ring_x, 2 - ring_x)
                    spot = place * ROWS + y_place(up_y, ring_y)

                    def put(ref, first, count):
                        values = jnp.zeros((count, 128), F32)
                        if corner is not None:
                            values = corner[ring_x - 1, ring_y - 1, pl.ds(first, count), :]
                            values = jnp.where(real, values, 0.0)
                        ref[pl.ds(spot, count, stride=height), :] = values

                    put(outer, 0, fields)
                    put(outer_medium, fields, 4)
                    if ring_x == 1 and ring_y == 1:
                        put(outer_start, fields + 4, fields)

    def outer_or(ref, full):
        def pick(index, row):
            if row in OUTER:
                return ref[pl.ds(index * height + OUTER.index(row) * ROWS, ROWS), :]
            return row_of(full, index, row)

        return pick

    field_row, start_row = outer_or(outer, here), outer_or(outer_start, start)
    medium_row = outer_or(outer_medium, medium)
    fresh = (0, 1, 9, 10, 11)
    for k, row in enumerate(fresh):
        for name, value in coefficients(medium_row, row, row < 11).items():
            outer_coef[COEFFICIENTS.index(name), pl.ds(k * ROWS, ROWS), :] = value

    def faces(name, row):
        if name == "inverse":
            return medium_row(INV, row)
        index = COEFFICIENTS.index(name)
        if row in fresh:
            return row_of(outer_coef, index, fresh.index(row))
        return row_of(coef, index, row)

    def then_row(f, row):
        if row in EDGES:
            return row_of(edge, f, EDGES.index(row))
        return row_of(then, f, row)

    sums = {}
    for e in range(events):
        apply = Event(lambda c, row, e=e: field_row(3 * e + c, row)).operator(faces)
        for k, row in enumerate(EDGES):
            scale = STEP_FACTOR * medium_row(BUOY, row)
            for c, result in enumerate(apply(row)):
                f = 3 * e + c
                edge[f, pl.ds(k * ROWS, ROWS), :] = start_row(f, row) + scale * result
        second = Event(lambda c, row, e=e: then_row(3 * e + c, row))
        wave = Event(lambda c, row, e=e: row_of(stored, 2 * (3 * e + c) + 1, row))
        for row in (2, 3, 8, 9):
            gather(sums, second, wave, fwd, e, 1, row)
    grads = [[], []]
    for row in range(2, 10):
        shear, density = tile_row(part, 0, row), tile_row(part, 1, row)
        if row in (2, 3, 8, 9):
            inverse = tile_row(med, INV, row)
            more = sums["lateral", row] + inverse * inverse * sums["upright", row]
            shear = shear - 0.25 * more
            density = density - sums["density", row]
        grads[0].append(shear)
        grads[1].append(density)
    grads = grads[0] + grads[1]
    piece = 128 // shares
    quarter = lax.broadcasted_iota(jnp.int32, (8, 128), 1) // piece
    per = len(grads) // shares
    for j in range(shares):
        for r in range(per):
            tile = None
            for g in range(shares):
                source = grads[r * shares + g]
                moved = pltpu.roll(source, ((g - j) * piece) % 128, axis=1) if g != j else source
                tile = moved if tile is None else jnp.where(quarter == g, moved, tile)
            slabs[j, pl.ds(r * 8, 8), :] = tile
    me = lax.axis_index("ev")
    own_share[...] = slabs[me]
    for m in range(1, shares):
        sent[m - 1][...] = slabs[me ^ m]


def second_kernel(events, now, extra, med, medium, coef, then, edge, mid, after):
    def faces(name, row):
        if name == "inverse":
            return row_of(medium, INV, row)
        return row_of(coef, COEFFICIENTS.index(name), row)

    def then_row(f, row):
        if row in EDGES:
            return row_of(edge, f, EDGES.index(row))
        return row_of(then, f, row)

    for e in range(events):
        apply = Event(lambda c, row, e=e: then_row(3 * e + c, row)).operator(faces)
        for row in range(2, 10):
            spot = pl.ds((row - 2) * 8, 8)
            scale = STEP_FACTOR * tile_row(med, BUOY, row)
            for c, result in enumerate(apply(row)):
                f = 3 * e + c
                current = then_row(f, row)[:8]
                mid[f, spot, :] = current
                after[f, spot, :] = (
                    2.0 * current - now[f, spot, :] + extra[f, spot, :] + scale * result[:8]
                )


def finish_kernel(shares, scale, *refs):
    pieces, (shear, density) = refs[:shares], refs[shares:]
    total = pieces[0][...]
    for piece in pieces[1:]:
        total = total + piece[...]
    width = 128 // shares
    for v in range(16):
        g, r = v % shares, v // shares
        tile = total[r * 8 : (r + 1) * 8]
        if g:
            tile = pltpu.roll(tile, (-g * width) % 128, axis=1)
        out = shear if v < 8 else density
        out[pl.ds((v % 8) * 8, 8), :] = tile[:, :width] * scale


def call(
    kernel, outs, ins, scratch=(), name=None, limit=VMEM_LIMIT, cost=1000, out_memory=pltpu.VMEM
):
    return pl.pallas_call(
        kernel,
        out_shape=[jax.ShapeDtypeStruct(s, d) for s, d in outs],
        in_specs=[pl.BlockSpec(memory_space=m) for m in ins],
        out_specs=[pl.BlockSpec(memory_space=out_memory)] * len(outs),
        scratch_shapes=[s if not isinstance(s, tuple) else pltpu.VMEM(*s) for s in scratch],
        compiler_params=pltpu.CompilerParams(vmem_limit_bytes=limit),
        cost_estimate=pl.CostEstimate(
            flops=cost * 1024, bytes_accessed=cost * 1024, transcendentals=0
        ),
        name=name,
    )


def body(adjoint_now, adjoint_prev, forward, medium, drm_cells, drm_force):
    events, _, width_x, width_y, depth = adjoint_now.shape
    fields = 3 * events
    tile = width_x * width_y
    shares = lax.axis_size("ev")
    x_rounds, y_rounds = rounds_of(lax.axis_size("gx")), rounds_of(lax.axis_size("gy"))
    now = adjoint_now.reshape(fields, tile, depth)
    prev = adjoint_prev.reshape(fields, tile, depth)
    fwd = forward.reshape(events * 12, width_x, width_y, depth)
    med = medium.reshape(4, tile, depth)
    own = ((fields, tile, depth), F32)
    tall = 12 * ROWS

    face = ((4 * fields + 4, 16, depth), BF16)
    corner = ((2, 2, 2 * fields + 4, depth), F32)
    shapes = [face] * (len(y_rounds) + len(x_rounds)) + [corner] * (len(x_rounds) * len(y_rounds))
    flat = ((fields * tile, depth), F32)
    messages = call(
        functools.partial(pack_kernel, events, x_rounds, y_rounds),
        shapes,
        [pltpu.HBM] * 6,
        [
            flat,
            flat,
            ((2 * fields, width_x, width_y, depth), BF16),
            ((4 * tile, depth), F32),
            (drm_cells.shape, drm_cells.dtype),
            (drm_force.shape, F32),
            flat,
            ((2 * fields * tile, depth), F32),
            pltpu.SemaphoreType.DMA((5 + events,)),
            pltpu.SemaphoreType.DMA((len(shapes),)),
            *shapes,
        ],
        "pack",
        PACK_LIMIT,
        cost=8000,
        out_memory=pltpu.HBM,
    )(now.reshape(-1, depth), prev.reshape(-1, depth), fwd, med.reshape(-1, depth), drm_cells, drm_force)
    kinds = [{"gy": r} for r in y_rounds] + [{"gx": r} for r in x_rounds]
    kinds += [{"gx": x, "gy": y} for x in x_rounds for y in y_rounds]
    received = [swap(message, kind) for message, kind in zip(messages, kinds)]
    y_messages, rest = received[: len(y_rounds)], received[len(y_rounds) :]
    x_messages, corners = rest[: len(x_rounds)], rest[len(x_rounds) :]
    arrival = ()
    if y_messages:
        arrival = call(
            lambda *refs: None,
            [((8, depth), F32)],
            [pl.ANY] * len(y_messages),
            name="arrival",
            out_memory=pl.ANY,
            cost=8000,
        )(*y_messages)
    base, extra = call(
        functools.partial(own_kernel, events),
        [own, own],
        [pltpu.VMEM] * 5 + [pl.ANY] * len(arrival),
        name="own",
    )(now, prev, med, drm_cells, drm_force, *arrival)

    wide = ((fields, tall, depth), F32)
    here, start, stored, tall_medium, coef, then, part = call(
        functools.partial(inner_kernel, events, x_rounds, y_rounds),
        [
            wide,
            wide,
            ((2 * fields, tall, depth), F32),
            ((4, tall, depth), F32),
            ((len(COEFFICIENTS), tall, depth), F32),
            wide,
            ((2, tile, depth), F32),
        ],
        [pltpu.VMEM] * (4 + len(x_messages) + len(y_messages)),
        name="inner",
        cost=3000,
    )(now, base, fwd, med, *x_messages, *y_messages)
    slab = ((16 // shares * 8, depth), F32)
    outer = ((fields, len(OUTER) * ROWS, depth), F32)
    edge, own_share, *sent = call(
        functools.partial(edge_kernel, events, x_rounds, y_rounds, shares),
        [outer] + [slab] * shares,
        [pltpu.VMEM] * (9 + len(corners)),
        [
            ((fields * len(OUTER) * ROWS, depth), F32),
            ((fields * len(OUTER) * ROWS, depth), F32),
            ((4 * len(OUTER) * ROWS, depth), F32),
            ((len(COEFFICIENTS), 5 * ROWS, depth), F32),
            ((shares,) + slab[0], F32),
        ],
        "edges",
    )(*corners, here, start, stored, tall_medium, coef, then, part, fwd, med)
    pieces = [own_share]
    for m in reversed(range(1, shares)):
        pairs = [(i, i ^ m) for i in range(shares)]
        pieces.append(lax.ppermute(sent[m - 1], "ev", pairs))
    mid, after = call(
        functools.partial(second_kernel, events),
        [own, own],
        [pltpu.VMEM] * 7,
        name="second",
    )(now, extra, med, tall_medium, coef, then, edge)
    shear, density = call(
        functools.partial(finish_kernel, shares, 1.0 / (events * shares)),
        [((tile, depth // shares), F32)] * 2,
        [pltpu.VMEM] * shares,
        name="finish",
    )(*pieces)
    shape = adjoint_now.shape
    grad = (width_x, width_y, depth // shares)
    return mid.reshape(shape), after.reshape(shape), shear.reshape(grad), density.reshape(grad)


def solution(mesh):
    in_specs = (
        P("ev", None, "gx", "gy", None),
        P("ev", None, "gx", "gy", None),
        P("ev", None, None, "gx", "gy", None),
        P(None, "gx", "gy", None),
        P("gx", "gy", None),
        P("ev", None, None, "gx", "gy", None),
    )
    out_specs = (
        P("ev", None, "gx", "gy", None),
        P("ev", None, "gx", "gy", None),
        P("gx", "gy", "ev"),
        P("gx", "gy", "ev"),
    )
    return jax.shard_map(body, mesh=mesh, in_specs=in_specs, out_specs=out_specs, check_vma=False)
```

```python
import functools
import itertools

import jax
import jax.numpy as jnp
from jax import lax
from jax.experimental import pallas as pl
from jax.experimental.pallas import tpu as pltpu
from jax.sharding import PartitionSpec as P

STEP_FACTOR = 0.01
F32, BF16 = jnp.float32, jnp.bfloat16
SHEAR, LAME, BUOY, INV = range(4)
ROWS = 16
VMEM_LIMIT = 40 * 1024 * 1024
PACK_LIMIT = 60 * 1024 * 1024


def rounds_of(count):
    return "AB"[: max(0, min(2, count - 1))]


def swap(values, rounds, first_along_x=False, first_idle=False):
    names = ("ev", "gx", "gy")
    sizes = [lax.axis_size(a) for a in names]
    pairs = []
    for source in itertools.product(*map(range, sizes)):
        target = list(source)
        steps = {"gx": "A"}.items() if first_along_x and source[2] == 0 else rounds.items()
        for axis, name in steps:
            along = names.index(axis)
            target[along] += 1 if (source[along] % 2 == 0) == (name == "A") else -1
        idle = first_idle and source[2] == 0
        if idle or not all(0 <= t < size for t, size in zip(target, sizes)):
            target = [source[0] ^ 1, *source[1:]]
        flat = [(s[0] * sizes[1] + s[1]) * sizes[2] + s[2] for s in (source, target)]
        pairs.append(tuple(flat))
    return lax.ppermute(values, names, pairs)


def their_turn(x_rounds, y_rounds):
    return bool(x_rounds) and "B" in y_rounds


def is_first():
    return lax.axis_index("gy") == 0


def linked(axis, name):
    other = lax.axis_index(axis) + jnp.where(upward(axis, name), 1, -1)
    return jnp.logical_and(other >= 0, other < lax.axis_size(axis))


def upward(axis, name):
    even = lax.rem(lax.axis_index(axis), 2) == 0
    return even if name == "A" else jnp.logical_not(even)


def split(values):
    high = values.astype(BF16)
    low = (values - high.astype(F32)).astype(BF16)
    return jnp.concatenate([high, low], axis=0)


def join(tile):
    tile = tile.astype(F32)
    return tile[:8] + tile[8:]


def force_field(cells, force_rows, width):
    depth = 128
    count = cells.shape[1]
    place = lax.broadcasted_iota(jnp.int32, (width, count), 0)
    mask = place == cells // depth
    level = lax.broadcasted_iota(jnp.int32, (depth, count), 0)
    hot = jnp.where(level == lax.rem(cells, depth), 1.0, 0.0).astype(BF16)
    left = jnp.concatenate([jnp.where(mask, row, 0.0) for row in force_rows], axis=0)
    total = None
    for _ in range(3):
        part = left.astype(BF16)
        left = left - part.astype(F32)
        term = lax.dot_general(part, hot, (((1,), (1,)), ((), ())), preferred_element_type=F32)
        total = term if total is None else total + term
    return total


def pack_kernel(events, x_rounds, y_rounds, *refs):
    fields = 3 * events
    total = len(x_rounds) + len(y_rounds) + len(x_rounds) * len(y_rounds)
    sources, targets, refs = refs[:6], refs[6 : 6 + total], refs[6 + total :]
    now, prev, fwd, med, cells, force, base, stored, arrived, left = refs[:10]
    messages = refs[10:]
    now_in, prev_in, fwd_in, med_in, cells_in, force_in = sources
    pairs = [(cells_in, cells), (force_in, force), (now_in, now), (prev_in, prev), (med_in, med)]
    for e in range(events):
        pairs.append((fwd_in.at[pl.ds(e * 12 + 3, 6)], fwd.at[pl.ds(e * 6, 6)]))
    copies = [
        pltpu.make_async_copy(source, target, arrived.at[k])
        for k, (source, target) in enumerate(pairs)
    ]
    for copy in copies:
        copy.start()
    for copy in copies[:2]:
        copy.wait()
    rows = [force[e, 0, c, 0] for e in range(events) for c in range(3)]
    pushed = force_field(cells[0], rows, 64)
    for copy in copies[2:]:
        copy.wait()
    scale = STEP_FACTOR * med[pl.ds(BUOY * 64, 64), :]
    for f in range(fields):
        spot = pl.ds(f * 64, 64)
        base[spot, :] = 2.0 * now[spot, :] - prev[spot, :] + scale * pushed[f * 64 : (f + 1) * 64]
        e, c = f // 3, f % 3
        for t in range(2):
            part = fwd[(e * 2 + t) * 3 + c].astype(F32).reshape(64, 128)
            stored[pl.ds((f * 2 + t) * 64, 64), :] = part

    def fill(message, pick):
        for f in range(fields):
            message[2 * f] = split(pick(now, f, 1))
            message[2 * f + 1] = split(pick(now, f, 2))
            message[2 * fields + f] = split(pick(base, f, 1))
            message[3 * fields + f] = jnp.concatenate(
                [pick(stored, 2 * f, 1), pick(stored, 2 * f + 1, 1)], axis=0
            ).astype(BF16)
        for k, m in enumerate((SHEAR, LAME, INV)):
            message[4 * fields + k] = jnp.concatenate(
                [pick(med, m, 1), pick(med, m, 2)], axis=0
            ).astype(BF16)
        edge = pick(med, BUOY, 1)
        message[4 * fields + 3] = jnp.concatenate([edge, edge], axis=0).astype(BF16)

    def face(axis, name, ring):
        return jnp.where(upward(axis, name), 8 - ring, ring - 1)

    def pick_x(name):
        def pick(ref, index, ring):
            row = pl.multiple_of(face("gx", name, ring) * 8, 8)
            return ref[pl.ds(index * 64 + row, 8), :]

        return pick

    out = []

    def send():
        k = len(out)
        out.append(pltpu.make_async_copy(messages[k], targets[k], left.at[k]))
        out[k].start()

    for name in y_rounds:

        def pick_y(ref, index, ring, name=name):
            return ref[pl.ds(index * 64 + face("gy", name, ring), 8, stride=8), :]

        if name == "B" and their_turn(x_rounds, y_rounds):
            pl.when(is_first())(functools.partial(fill, messages[len(out)], pick_x("A")))
            pl.when(jnp.logical_not(is_first()))(functools.partial(fill, messages[len(out)], pick_y))
        else:
            fill(messages[len(out)], pick_y)
        send()
    for name in x_rounds:
        fill(messages[len(out)], pick_x(name))
        send()
    for name_x in x_rounds:
        for name_y in y_rounds:
            message = messages[len(out)]
            for ring_x in (1, 2):
                for ring_y in (1, 2):
                    cell = face("gx", name_x, ring_x) * 8 + face("gy", name_y, ring_y)
                    target = message.at[ring_x - 1, ring_y - 1]
                    target[pl.ds(0, fields), :] = now[pl.ds(cell, fields, stride=64), :]
                    target[pl.ds(fields, 4), :] = med[pl.ds(cell, 4, stride=64), :]
                    picked = base[pl.ds(cell, fields, stride=64), :]
                    target[pl.ds(fields + 4, fields), :] = picked
            send()
    for copy in out:
        copy.wait()


def masked(message, axis, name):
    if name == "A" and lax.axis_size(axis) % 2 == 0:
        return lambda index: message[index]
    real = linked(axis, name)
    return lambda index: jnp.where(real, message[index].astype(F32), 0.0).astype(BF16)


def shift_z(values, step):
    depth = values.shape[-1]
    lane = lax.broadcasted_iota(jnp.int32, values.shape, values.ndim - 1)
    moved = pltpu.roll(values, (-step) % depth, axis=values.ndim - 1)
    return jnp.where(lane == (depth - 1 if step > 0 else 0), 0.0, moved)


def shift_y(values, step):
    return pltpu.roll(values, (-step) % ROWS, axis=0)


def row_of(ref, index, row):
    return ref[index, pl.ds(row * ROWS, ROWS), :]


COEFFICIENTS = (
    ("own_x", "other_x", "own_y", "other_y", "own_z", "other_z", "cross", "cross_z")
    + ("own_y_down", "other_y_down", "own_z_down", "other_z_down")
)


def coefficients(medium, row, ahead=True):
    def both_of(row):
        return medium(LAME, row) + 2.0 * medium(SHEAR, row)

    shear, lame, inverse = (medium(m, row) for m in (SHEAR, LAME, INV))
    both = both_of(row)
    values = {}
    if ahead:
        values["own_x"] = 0.5 * (both + both_of(row + 1))
        values["other_x"] = 0.5 * (shear + medium(SHEAR, row + 1))
    for tail, step in (("", 1), ("_down", -1)):
        values["own_y" + tail] = 0.5 * (both + shift_y(both, step))
        values["other_y" + tail] = 0.5 * (shear + shift_y(shear, step))
        spacing = 0.25 * (inverse + shift_z(inverse, step))
        values["own_z" + tail] = spacing * (both + shift_z(both, step))
        values["other_z" + tail] = spacing * (shear + shift_z(shear, step))
    values["cross"] = 0.25 * (lame + shear)
    values["cross_z"] = values["cross"] * inverse
    return values


class Event:
    def __init__(self, value):
        self.value = functools.cache(value)
        self.y = functools.cache(lambda c, row, step: shift_y(self.value(c, row), step))
        self.z = functools.cache(lambda c, row, step: shift_z(self.value(c, row), step))

    def slopes(self, c, row):
        return (
            (self.value(c, row + 1) - self.value(c, row - 1))[:8],
            (self.y(c, row, 1) - self.y(c, row, -1))[:8],
            (self.z(c, row, 1) - self.z(c, row, -1))[:8],
        )

    def operator(self, faces):
        value = self.value

        @functools.cache
        def slope(d, row):
            if d == 0:
                return faces("cross", row) * (value(0, row + 1) - value(0, row - 1))
            if d == 1:
                return faces("cross", row) * (self.y(1, row, 1) - self.y(1, row, -1))
            return faces("cross_z", row) * (self.z(2, row, 1) - self.z(2, row, -1))

        @functools.cache
        def flux_x(c, row):
            kind = "own_x" if c == 0 else "other_x"
            return faces(kind, row) * (value(c, row + 1) - value(c, row))

        def apply(row):
            results = []
            for c in range(3):
                here = value(c, row)
                total = flux_x(c, row) - flux_x(c, row - 1)
                kind = "own_y" if c == 1 else "other_y"
                total = total + (
                    faces(kind, row) * (self.y(c, row, 1) - here)
                    - faces(kind + "_down", row) * (here - self.y(c, row, -1))
                )
                kind = "own_z" if c == 2 else "other_z"
                upright = faces(kind, row) * (self.z(c, row, 1) - here) - faces(
                    kind + "_down", row
                ) * (here - self.z(c, row, -1))
                if c == 0:
                    total = total + (
                        (slope(1, row + 1) + slope(2, row + 1))
                        - (slope(1, row - 1) + slope(2, row - 1))
                    )
                elif c == 1:
                    mixed = slope(0, row) + slope(2, row)
                    total = total + (shift_y(mixed, 1) - shift_y(mixed, -1))
                else:
                    mixed = slope(0, row) + slope(1, row)
                    upright = upright + (shift_z(mixed, 1) - shift_z(mixed, -1))
                results.append(total + faces("inverse", row) * upright)
            return results

        return apply


def x_row(up, ring):
    return jnp.where(up, 9 + ring, 2 - ring)


def y_place(up, ring):
    return jnp.where(up, 7 + ring, ROWS - ring)


def tile_row(ref, index, row):
    return ref[index, pl.ds((row - 2) * 8, 8), :]


def own_kernel(events, now, prev, med, cells, force, *refs):
    base, extra = refs[-2:]
    fields = 3 * events
    rows = [force[e, s, c, 0] for s in range(2) for e in range(events) for c in range(3)]
    pushed = force_field(cells[0], rows, 64)
    scale = STEP_FACTOR * med[BUOY]
    for f in range(fields):
        base[f] = 2.0 * now[f] - prev[f] + scale * pushed[f * 64 : (f + 1) * 64]
        extra[f] = scale * pushed[(fields + f) * 64 : (fields + f + 1) * 64]


def add_to(sums, key, value):
    sums[key] = sums[key] + value if key in sums else value


def inner_kernel(events, x_rounds, y_rounds, now, base, fwd, med, *refs):
    fields = 3 * events
    x_messages, refs = refs[: len(x_rounds)], refs[len(x_rounds) :]
    y_messages, refs = refs[: len(y_rounds)], refs[len(y_rounds) :]
    here, start, stored, medium, coef, then, part = refs[-7:]

    for f in range(fields):
        e, c = f // 3, f % 3
        for x in range(8):
            spot = pl.ds((x + 2) * ROWS, 8)
            here[f, spot, :] = now[f, pl.ds(x * 8, 8), :]
            start[f, spot, :] = base[f, pl.ds(x * 8, 8), :]
            for t in range(2):
                stored[2 * f + t, spot, :] = fwd[(e * 4 + t + 1) * 3 + c, x].astype(F32)
    for m in range(4):
        for x in range(8):
            medium[m, pl.ds((x + 2) * ROWS, 8), :] = med[m, pl.ds(x * 8, 8), :]

    def place(tile, put):
        for f in range(fields):
            put(here, f, 1, join(tile(2 * f)))
            put(here, f, 2, join(tile(2 * f + 1)))
            put(start, f, 1, join(tile(2 * fields + f)))
            both = tile(3 * fields + f).astype(F32)
            put(stored, 2 * f, 1, both[:8])
            put(stored, 2 * f + 1, 1, both[8:])
        for k, m in enumerate((SHEAR, LAME, INV)):
            both = tile(4 * fields + k).astype(F32)
            put(medium, m, 1, both[:8])
            put(medium, m, 2, both[8:])
        put(medium, BUOY, 1, tile(4 * fields + 3).astype(F32)[:8])

    def nothing(_):
        return jnp.zeros((16, 128), BF16)

    for k, name in enumerate("AB"):
        up = upward("gx", name)

        def put_x(ref, index, ring, values, up=up):
            row = pl.multiple_of(x_row(up, ring) * ROWS, ROWS)
            ref[index, pl.ds(row, 8), :] = values

        if name == "A" and their_turn(x_rounds, y_rounds):
            for message, when in (
                (y_messages[1], is_first()),
                (x_messages[0], jnp.logical_not(is_first())),
            ):
                pl.when(when)(functools.partial(place, masked(message, "gx", name), put_x))
        else:
            place(masked(x_messages[k], "gx", name) if k < len(x_rounds) else nothing, put_x)
    for k, name in enumerate("AB"):
        up = upward("gy", name)

        def put_y(ref, index, ring, values, up=up):
            ref[index, pl.ds(2 * ROWS + y_place(up, ring), 8, stride=ROWS), :] = values

        place(masked(y_messages[k], "gy", name) if k < len(y_rounds) else nothing, put_y)

    for row in range(1, 11):
        values = coefficients(lambda m, r: row_of(medium, m, r), row, row < 10)
        for name, value in values.items():
            coef[COEFFICIENTS.index(name), pl.ds(row * ROWS, ROWS), :] = value

    def faces(name, row):
        if name == "inverse":
            return row_of(medium, INV, row)
        return row_of(coef, COEFFICIENTS.index(name), row)

    sums = {}
    for e in range(events):
        first = Event(lambda c, row, e=e: row_of(here, 3 * e + c, row))
        apply = first.operator(faces)
        waves = [
            Event(lambda c, row, e=e, t=t: row_of(stored, 2 * (3 * e + c) + t, row))
            for t in range(2)
        ]
        for row in range(2, 10):
            if 3 <= row <= 8:
                scale = STEP_FACTOR * row_of(medium, BUOY, row)
                for c, result in enumerate(apply(row)):
                    f = 3 * e + c
                    then[f, pl.ds(row * ROWS, ROWS), :] = row_of(start, f, row) + scale * result
            gather(sums, first, waves[0], fwd, e, 0, row)
        second = Event(lambda c, row, e=e: row_of(then, 3 * e + c, row))
        for row in range(4, 8):
            gather(sums, second, waves[1], fwd, e, 1, row)
    for row in range(2, 10):
        inverse = tile_row(med, INV, row)
        shear = sums["lateral", row] + inverse * inverse * sums["upright", row]
        part[0, pl.ds((row - 2) * 8, 8), :] = -0.25 * shear
        part[1, pl.ds((row - 2) * 8, 8), :] = -sums["density", row]


def gather(sums, field, wave, fwd, e, t, row):
    for c in range(3):
        ax, ay, az = field.slopes(c, row)
        ux, uy, uz = wave.slopes(c, row)
        newer = fwd[(e * 4 + t) * 3 + c, row - 2].astype(F32)
        older = fwd[(e * 4 + t + 2) * 3 + c, row - 2].astype(F32)
        bend = newer - 2.0 * wave.value(c, row)[:8] + older
        add_to(sums, ("lateral", row), ax * ux + ay * uy)
        add_to(sums, ("upright", row), az * uz)
        add_to(sums, ("density", row), field.value(c, row)[:8] * bend)


OUTER = (0, 1, 10, 11)
EDGES = (1, 2, 9, 10)


def edge_kernel(events, x_rounds, y_rounds, shares, *refs):
    fields = 3 * events
    count = len(x_rounds) * len(y_rounds)
    corners, refs = refs[:count], refs[count:]
    (here, start, stored, medium, coef, then, part, fwd, med), refs = refs[:9], refs[9:]
    edge, own_share, *sent = refs[: 1 + shares]
    outer, outer_start, outer_medium, outer_coef, slabs = refs[1 + shares :]

    height = len(OUTER) * ROWS
    for k, row in enumerate(OUTER):
        for f in range(fields):
            spot = pl.ds(f * height + k * ROWS, ROWS)
            outer[spot, :] = row_of(here, f, row)
            if row in EDGES:
                outer_start[spot, :] = row_of(start, f, row)
        for m in range(4):
            outer_medium[pl.ds(m * height + k * ROWS, ROWS), :] = row_of(medium, m, row)
    for kx, name_x in enumerate("AB"):
        for ky, name_y in enumerate("AB"):
            corner = None
            if kx < len(x_rounds) and ky < len(y_rounds):
                corner = corners[kx * len(y_rounds) + ky]
            up_x, up_y = upward("gx", name_x), upward("gy", name_y)
            real = jnp.logical_and(linked("gx", name_x), linked("gy", name_y))
            for ring_x in (1, 2):
                for ring_y in (1, 2):
                    place = jnp.where(up_x, 1 + ring_x, 2 - ring_x)
                    spot = place * ROWS + y_place(up_y, ring_y)

                    def put(ref, first, count):
                        values = jnp.zeros((count, 128), F32)
                        if corner is not None:
                            values = corner[ring_x - 1, ring_y - 1, pl.ds(first, count), :]
                            values = jnp.where(real, values, 0.0)
                        ref[pl.ds(spot, count, stride=height), :] = values

                    put(outer, 0, fields)
                    put(outer_medium, fields, 4)
                    if ring_x == 1 and ring_y == 1:
                        put(outer_start, fields + 4, fields)

    def outer_or(ref, full):
        def pick(index, row):
            if row in OUTER:
                return ref[pl.ds(index * height + OUTER.index(row) * ROWS, ROWS), :]
            return row_of(full, index, row)

        return pick

    field_row, start_row = outer_or(outer, here), outer_or(outer_start, start)
    medium_row = outer_or(outer_medium, medium)
    fresh = (0, 1, 9, 10, 11)
    for k, row in enumerate(fresh):
        for name, value in coefficients(medium_row, row, row < 11).items():
            outer_coef[COEFFICIENTS.index(name), pl.ds(k * ROWS, ROWS), :] = value

    def faces(name, row):
        if name == "inverse":
            return medium_row(INV, row)
        index = COEFFICIENTS.index(name)
        if row in fresh:
            return row_of(outer_coef, index, fresh.index(row))
        return row_of(coef, index, row)

    def then_row(f, row):
        if row in EDGES:
            return row_of(edge, f, EDGES.index(row))
        return row_of(then, f, row)

    sums = {}
    for e in range(events):
        apply = Event(lambda c, row, e=e: field_row(3 * e + c, row)).operator(faces)
        for k, row in enumerate(EDGES):
            scale = STEP_FACTOR * medium_row(BUOY, row)
            for c, result in enumerate(apply(row)):
                f = 3 * e + c
                edge[f, pl.ds(k * ROWS, ROWS), :] = start_row(f, row) + scale * result
        second = Event(lambda c, row, e=e: then_row(3 * e + c, row))
        wave = Event(lambda c, row, e=e: row_of(stored, 2 * (3 * e + c) + 1, row))
        for row in (2, 3, 8, 9):
            gather(sums, second, wave, fwd, e, 1, row)
    grads = [[], []]
    for row in range(2, 10):
        shear, density = tile_row(part, 0, row), tile_row(part, 1, row)
        if row in (2, 3, 8, 9):
            inverse = tile_row(med, INV, row)
            more = sums["lateral", row] + inverse * inverse * sums["upright", row]
            shear = shear - 0.25 * more
            density = density - sums["density", row]
        grads[0].append(shear)
        grads[1].append(density)
    grads = grads[0] + grads[1]
    piece = 128 // shares
    quarter = lax.broadcasted_iota(jnp.int32, (8, 128), 1) // piece
    per = len(grads) // shares
    for j in range(shares):
        for r in range(per):
            tile = None
            for g in range(shares):
                source = grads[r * shares + g]
                moved = pltpu.roll(source, ((g - j) * piece) % 128, axis=1) if g != j else source
                tile = moved if tile is None else jnp.where(quarter == g, moved, tile)
            slabs[j, pl.ds(r * 8, 8), :] = tile
    me = lax.axis_index("ev")
    own_share[...] = slabs[me]
    for m in range(1, shares):
        sent[m - 1][...] = slabs[me ^ m]


def second_kernel(events, now, extra, med, medium, coef, then, edge, mid, after):
    def faces(name, row):
        if name == "inverse":
            return row_of(medium, INV, row)
        return row_of(coef, COEFFICIENTS.index(name), row)

    def then_row(f, row):
        if row in EDGES:
            return row_of(edge, f, EDGES.index(row))
        return row_of(then, f, row)

    for e in range(events):
        apply = Event(lambda c, row, e=e: then_row(3 * e + c, row)).operator(faces)
        for row in range(2, 10):
            spot = pl.ds((row - 2) * 8, 8)
            scale = STEP_FACTOR * tile_row(med, BUOY, row)
            for c, result in enumerate(apply(row)):
                f = 3 * e + c
                current = then_row(f, row)[:8]
                mid[f, spot, :] = current
                after[f, spot, :] = (
                    2.0 * current - now[f, spot, :] + extra[f, spot, :] + scale * result[:8]
                )


def finish_kernel(shares, scale, *refs):
    pieces, (shear, density) = refs[:shares], refs[shares:]
    total = pieces[0][...]
    for piece in pieces[1:]:
        total = total + piece[...]
    width = 128 // shares
    for v in range(16):
        g, r = v % shares, v // shares
        tile = total[r * 8 : (r + 1) * 8]
        if g:
            tile = pltpu.roll(tile, (-g * width) % 128, axis=1)
        out = shear if v < 8 else density
        out[pl.ds((v % 8) * 8, 8), :] = tile[:, :width] * scale


def call(
    kernel, outs, ins, scratch=(), name=None, limit=VMEM_LIMIT, cost=1000, out_memory=pltpu.VMEM
):
    return pl.pallas_call(
        kernel,
        out_shape=[jax.ShapeDtypeStruct(s, d) for s, d in outs],
        in_specs=[pl.BlockSpec(memory_space=m) for m in ins],
        out_specs=[pl.BlockSpec(memory_space=out_memory)] * len(outs),
        scratch_shapes=[s if not isinstance(s, tuple) else pltpu.VMEM(*s) for s in scratch],
        compiler_params=pltpu.CompilerParams(vmem_limit_bytes=limit),
        cost_estimate=pl.CostEstimate(
            flops=cost * 1024, bytes_accessed=cost * 1024, transcendentals=0
        ),
        name=name,
    )


def wait_for(before, messages):
    arrays = [*before, *messages]
    return call(
        lambda *refs: None,
        [((8, 128), F32)],
        [pl.ANY] * len(arrays),
        name="arrival",
        out_memory=pl.ANY,
        cost=8000,
    )(*arrays)


def body(adjoint_now, adjoint_prev, forward, medium, drm_cells, drm_force):
    events, _, width_x, width_y, depth = adjoint_now.shape
    fields = 3 * events
    tile = width_x * width_y
    shares = lax.axis_size("ev")
    x_rounds, y_rounds = rounds_of(lax.axis_size("gx")), rounds_of(lax.axis_size("gy"))
    now = adjoint_now.reshape(fields, tile, depth)
    prev = adjoint_prev.reshape(fields, tile, depth)
    fwd = forward.reshape(events * 12, width_x, width_y, depth)
    med = medium.reshape(4, tile, depth)
    own = ((fields, tile, depth), F32)
    tall = 12 * ROWS

    face = ((4 * fields + 4, 16, depth), BF16)
    corner = ((2, 2, 2 * fields + 4, depth), F32)
    shapes = [face] * (len(y_rounds) + len(x_rounds)) + [corner] * (len(x_rounds) * len(y_rounds))
    flat = ((fields * tile, depth), F32)
    messages = call(
        functools.partial(pack_kernel, events, x_rounds, y_rounds),
        shapes,
        [pltpu.HBM] * 6,
        [
            flat,
            flat,
            ((2 * fields, width_x, width_y, depth), BF16),
            ((4 * tile, depth), F32),
            (drm_cells.shape, drm_cells.dtype),
            (drm_force.shape, F32),
            flat,
            ((2 * fields * tile, depth), F32),
            pltpu.SemaphoreType.DMA((5 + events,)),
            pltpu.SemaphoreType.DMA((len(shapes),)),
            *shapes,
        ],
        "pack",
        PACK_LIMIT,
        cost=8000,
        out_memory=pltpu.HBM,
    )(now.reshape(-1, depth), prev.reshape(-1, depth), fwd, med.reshape(-1, depth), drm_cells, drm_force)
    kinds = [{"gy": r} for r in y_rounds] + [{"gx": r} for r in x_rounds]
    kinds += [{"gx": x, "gy": y} for x in x_rounds for y in y_rounds]
    turn = their_turn(x_rounds, y_rounds)
    received = [
        swap(message, kind, turn and kind == {"gy": "B"}, turn and kind == {"gx": "A"})
        for message, kind in zip(messages, kinds)
    ]
    y_messages, rest = received[: len(y_rounds)], received[len(y_rounds) :]
    x_messages, corners = rest[: len(x_rounds)], rest[len(x_rounds) :]
    order = [y_messages[1], y_messages[0]] if turn else [*x_messages[:1], *y_messages[:1]]
    arrival = wait_for([], order[:1])
    arrival = wait_for(arrival, order[1:2])
    base, extra = call(
        functools.partial(own_kernel, events),
        [own, own],
        [pltpu.VMEM] * 5 + [pl.ANY] * len(arrival),
        name="own",
    )(now, prev, med, drm_cells, drm_force, *arrival)
    wide = ((fields, tall, depth), F32)
    here, start, stored, tall_medium, coef, then, part = call(
        functools.partial(inner_kernel, events, x_rounds, y_rounds),
        [
            wide,
            wide,
            ((2 * fields, tall, depth), F32),
            ((4, tall, depth), F32),
            ((len(COEFFICIENTS), tall, depth), F32),
            wide,
            ((2, tile, depth), F32),
        ],
        [pltpu.VMEM] * (4 + len(x_messages) + len(y_messages)),
        name="inner",
        cost=3000,
    )(now, base, fwd, med, *x_messages, *y_messages)
    slab = ((16 // shares * 8, depth), F32)
    outer = ((fields, len(OUTER) * ROWS, depth), F32)
    edge, own_share, *sent = call(
        functools.partial(edge_kernel, events, x_rounds, y_rounds, shares),
        [outer] + [slab] * shares,
        [pltpu.VMEM] * (9 + len(corners)),
        [
            ((fields * len(OUTER) * ROWS, depth), F32),
            ((fields * len(OUTER) * ROWS, depth), F32),
            ((4 * len(OUTER) * ROWS, depth), F32),
            ((len(COEFFICIENTS), 5 * ROWS, depth), F32),
            ((shares,) + slab[0], F32),
        ],
        "edges",
    )(*corners, here, start, stored, tall_medium, coef, then, part, fwd, med)
    pieces = [own_share]
    for m in reversed(range(1, shares)):
        pairs = [(i, i ^ m) for i in range(shares)]
        pieces.append(lax.ppermute(sent[m - 1], "ev", pairs))
    mid, after = call(
        functools.partial(second_kernel, events),
        [own, own],
        [pltpu.VMEM] * 7,
        name="second",
    )(now, extra, med, tall_medium, coef, then, edge)
    shear, density = call(
        functools.partial(finish_kernel, shares, 1.0 / (events * shares)),
        [((tile, depth // shares), F32)] * 2,
        [pltpu.VMEM] * shares,
        name="finish",
    )(*pieces)
    shape = adjoint_now.shape
    grad = (width_x, width_y, depth // shares)
    return mid.reshape(shape), after.reshape(shape), shear.reshape(grad), density.reshape(grad)


def solution(mesh):
    in_specs = (
        P("ev", None, "gx", "gy", None),
        P("ev", None, "gx", "gy", None),
        P("ev", None, None, "gx", "gy", None),
        P(None, "gx", "gy", None),
        P("gx", "gy", None),
        P("ev", None, None, "gx", "gy", None),
    )
    out_specs = (
        P("ev", None, "gx", "gy", None),
        P("ev", None, "gx", "gy", None),
        P("gx", "gy", "ev"),
        P("gx", "gy", "ev"),
    )
    return jax.shard_map(body, mesh=mesh, in_specs=in_specs, out_specs=out_specs, check_vma=False)
```

```python
import functools
import itertools

import jax
import jax.numpy as jnp
from jax import lax
from jax.experimental import pallas as pl
from jax.experimental.pallas import tpu as pltpu
from jax.sharding import PartitionSpec as P

STEP_FACTOR = 0.01
F32, BF16 = jnp.float32, jnp.bfloat16
SHEAR, LAME, BUOY, INV = range(4)
ROWS = 16
VMEM_LIMIT = 40 * 1024 * 1024


def rounds_of(count):
    return "AB"[: max(0, min(2, count - 1))]


def swap(values, rounds, first_along_x=False, first_idle=False):
    names = ("ev", "gx", "gy")
    sizes = [lax.axis_size(a) for a in names]
    pairs = []
    for source in itertools.product(*map(range, sizes)):
        target = list(source)
        steps = {"gx": "A"}.items() if first_along_x and source[2] == 0 else rounds.items()
        for axis, name in steps:
            along = names.index(axis)
            target[along] += 1 if (source[along] % 2 == 0) == (name == "A") else -1
        idle = first_idle and source[2] == 0
        if idle or not all(0 <= t < size for t, size in zip(target, sizes)):
            target = [source[0] ^ 1, *source[1:]]
        flat = [(s[0] * sizes[1] + s[1]) * sizes[2] + s[2] for s in (source, target)]
        pairs.append(tuple(flat))
    return lax.ppermute(values, names, pairs)


def their_turn(x_rounds, y_rounds):
    return bool(x_rounds) and "B" in y_rounds


def is_first():
    return lax.axis_index("gy") == 0


def linked(axis, name):
    other = lax.axis_index(axis) + jnp.where(upward(axis, name), 1, -1)
    return jnp.logical_and(other >= 0, other < lax.axis_size(axis))


def upward(axis, name):
    even = lax.rem(lax.axis_index(axis), 2) == 0
    return even if name == "A" else jnp.logical_not(even)


def split(values):
    high = values.astype(BF16)
    low = (values - high.astype(F32)).astype(BF16)
    return jnp.concatenate([high, low], axis=0)


def join(tile):
    tile = tile.astype(F32)
    return tile[:8] + tile[8:]


def force_field(cells, force_rows, width):
    depth = 128
    count = cells.shape[1]
    place = lax.broadcasted_iota(jnp.int32, (width, count), 0)
    mask = place == cells // depth
    level = lax.broadcasted_iota(jnp.int32, (depth, count), 0)
    hot = jnp.where(level == lax.rem(cells, depth), 1.0, 0.0).astype(BF16)
    left = jnp.concatenate([jnp.where(mask, row, 0.0) for row in force_rows], axis=0)
    total = None
    for _ in range(3):
        part = left.astype(BF16)
        left = left - part.astype(F32)
        term = lax.dot_general(part, hot, (((1,), (1,)), ((), ())), preferred_element_type=F32)
        total = term if total is None else total + term
    return total


def pack_kernel(events, x_rounds, y_rounds, *refs):
    fields = 3 * events
    now_in, prev_in, fwd_in, med_in, cells_in, force_in = refs[:6]
    now, fwd, med, cells, force, base = refs[6:12]
    messages, (prev, stored, arrived) = refs[12:-3], refs[-3:]
    pairs = [(cells_in, cells), (force_in, force), (now_in, now), (prev_in, prev), (med_in, med)]
    for first, count in ((3, 6), (0, 3), (9, 3)):
        for e in range(events):
            part = pl.ds(e * 12 + first, count)
            pairs.append((fwd_in.at[part], fwd.at[part]))
    copies = [
        pltpu.make_async_copy(source, target, arrived.at[k])
        for k, (source, target) in enumerate(pairs)
    ]
    for copy in copies:
        copy.start()
    for copy in copies[:2]:
        copy.wait()
    rows = [force[e, 0, c, 0] for e in range(events) for c in range(3)]
    pushed = force_field(cells[0], rows, 64)
    for copy in copies[2 : 5 + events]:
        copy.wait()
    scale = STEP_FACTOR * med[pl.ds(BUOY * 64, 64), :]
    for f in range(fields):
        spot = pl.ds(f * 64, 64)
        base[spot, :] = 2.0 * now[spot, :] - prev[spot, :] + scale * pushed[f * 64 : (f + 1) * 64]
        e, c = f // 3, f % 3
        for t in range(2):
            part = fwd[(e * 4 + t + 1) * 3 + c].astype(F32).reshape(64, 128)
            stored[pl.ds((f * 2 + t) * 64, 64), :] = part

    def fill(message, pick):
        for f in range(fields):
            message[2 * f] = split(pick(now, f, 1))
            message[2 * f + 1] = split(pick(now, f, 2))
            message[2 * fields + f] = split(pick(base, f, 1))
            message[3 * fields + f] = jnp.concatenate(
                [pick(stored, 2 * f, 1), pick(stored, 2 * f + 1, 1)], axis=0
            ).astype(BF16)
        for k, m in enumerate((SHEAR, LAME, INV)):
            message[4 * fields + k] = jnp.concatenate(
                [pick(med, m, 1), pick(med, m, 2)], axis=0
            ).astype(BF16)
        edge = pick(med, BUOY, 1)
        message[4 * fields + 3] = jnp.concatenate([edge, edge], axis=0).astype(BF16)

    def face(axis, name, ring):
        return jnp.where(upward(axis, name), 8 - ring, ring - 1)

    def pick_x(name):
        def pick(ref, index, ring):
            row = pl.multiple_of(face("gx", name, ring) * 8, 8)
            return ref[pl.ds(index * 64 + row, 8), :]

        return pick

    targets = iter(messages)
    for name in y_rounds:

        def pick_y(ref, index, ring, name=name):
            return ref[pl.ds(index * 64 + face("gy", name, ring), 8, stride=8), :]

        if name == "B" and their_turn(x_rounds, y_rounds):
            message = next(targets)
            pl.when(is_first())(functools.partial(fill, message, pick_x("A")))
            pl.when(jnp.logical_not(is_first()))(functools.partial(fill, message, pick_y))
        else:
            fill(next(targets), pick_y)
    for name in x_rounds:
        fill(next(targets), pick_x(name))
    for name_x in x_rounds:
        for name_y in y_rounds:
            message = next(targets)
            for ring_x in (1, 2):
                for ring_y in (1, 2):
                    cell = face("gx", name_x, ring_x) * 8 + face("gy", name_y, ring_y)
                    target = message.at[ring_x - 1, ring_y - 1]
                    target[pl.ds(0, fields), :] = now[pl.ds(cell, fields, stride=64), :]
                    target[pl.ds(fields, 4), :] = med[pl.ds(cell, 4, stride=64), :]
                    picked = base[pl.ds(cell, fields, stride=64), :]
                    target[pl.ds(fields + 4, fields), :] = picked
    for copy in copies[5 + events :]:
        copy.wait()


def masked(message, axis, name):
    if name == "A" and lax.axis_size(axis) % 2 == 0:
        return lambda index: message[index]
    real = linked(axis, name)
    return lambda index: jnp.where(real, message[index].astype(F32), 0.0).astype(BF16)


def shift_z(values, step):
    depth = values.shape[-1]
    lane = lax.broadcasted_iota(jnp.int32, values.shape, values.ndim - 1)
    moved = pltpu.roll(values, (-step) % depth, axis=values.ndim - 1)
    return jnp.where(lane == (depth - 1 if step > 0 else 0), 0.0, moved)


def shift_y(values, step):
    return pltpu.roll(values, (-step) % ROWS, axis=0)


def row_of(ref, index, row):
    return ref[index, pl.ds(row * ROWS, ROWS), :]


COEFFICIENTS = (
    ("own_x", "other_x", "own_y", "other_y", "own_z", "other_z", "cross", "cross_z")
    + ("own_y_down", "other_y_down", "own_z_down", "other_z_down")
)


def coefficients(medium, row, ahead=True):
    def both_of(row):
        return medium(LAME, row) + 2.0 * medium(SHEAR, row)

    shear, lame, inverse = (medium(m, row) for m in (SHEAR, LAME, INV))
    both = both_of(row)
    values = {}
    if ahead:
        values["own_x"] = 0.5 * (both + both_of(row + 1))
        values["other_x"] = 0.5 * (shear + medium(SHEAR, row + 1))
    for tail, step in (("", 1), ("_down", -1)):
        values["own_y" + tail] = 0.5 * (both + shift_y(both, step))
        values["other_y" + tail] = 0.5 * (shear + shift_y(shear, step))
        spacing = 0.25 * (inverse + shift_z(inverse, step))
        values["own_z" + tail] = spacing * (both + shift_z(both, step))
        values["other_z" + tail] = spacing * (shear + shift_z(shear, step))
    values["cross"] = 0.25 * (lame + shear)
    values["cross_z"] = values["cross"] * inverse
    return values


class Event:
    def __init__(self, value):
        self.value = functools.cache(value)
        self.y = functools.cache(lambda c, row, step: shift_y(self.value(c, row), step))
        self.z = functools.cache(lambda c, row, step: shift_z(self.value(c, row), step))

    def slopes(self, c, row):
        return (
            (self.value(c, row + 1) - self.value(c, row - 1))[:8],
            (self.y(c, row, 1) - self.y(c, row, -1))[:8],
            (self.z(c, row, 1) - self.z(c, row, -1))[:8],
        )

    def operator(self, faces):
        value = self.value

        @functools.cache
        def slope(d, row):
            if d == 0:
                return faces("cross", row) * (value(0, row + 1) - value(0, row - 1))
            if d == 1:
                return faces("cross", row) * (self.y(1, row, 1) - self.y(1, row, -1))
            return faces("cross_z", row) * (self.z(2, row, 1) - self.z(2, row, -1))

        @functools.cache
        def flux_x(c, row):
            kind = "own_x" if c == 0 else "other_x"
            return faces(kind, row) * (value(c, row + 1) - value(c, row))

        def apply(row):
            results = []
            for c in range(3):
                here = value(c, row)
                total = flux_x(c, row) - flux_x(c, row - 1)
                kind = "own_y" if c == 1 else "other_y"
                total = total + (
                    faces(kind, row) * (self.y(c, row, 1) - here)
                    - faces(kind + "_down", row) * (here - self.y(c, row, -1))
                )
                kind = "own_z" if c == 2 else "other_z"
                upright = faces(kind, row) * (self.z(c, row, 1) - here) - faces(
                    kind + "_down", row
                ) * (here - self.z(c, row, -1))
                if c == 0:
                    total = total + (
                        (slope(1, row + 1) + slope(2, row + 1))
                        - (slope(1, row - 1) + slope(2, row - 1))
                    )
                elif c == 1:
                    mixed = slope(0, row) + slope(2, row)
                    total = total + (shift_y(mixed, 1) - shift_y(mixed, -1))
                else:
                    mixed = slope(0, row) + slope(1, row)
                    upright = upright + (shift_z(mixed, 1) - shift_z(mixed, -1))
                results.append(total + faces("inverse", row) * upright)
            return results

        return apply


def x_row(up, ring):
    return jnp.where(up, 9 + ring, 2 - ring)


def y_place(up, ring):
    return jnp.where(up, 7 + ring, ROWS - ring)


def tile_row(ref, index, row):
    return ref[pl.ds(index * 64 + (row - 2) * 8, 8), :]


def add_to(sums, key, value):
    sums[key] = sums[key] + value if key in sums else value


def inner_kernel(events, x_rounds, y_rounds, now, base, fwd, med, *refs):
    fields = 3 * events
    x_messages, refs = refs[: len(x_rounds)], refs[len(x_rounds) :]
    y_messages, refs = refs[: len(y_rounds)], refs[len(y_rounds) :]
    here, start, stored, medium, coef, then, part = refs[-7:]

    for f in range(fields):
        e, c = f // 3, f % 3
        for x in range(8):
            spot = pl.ds((x + 2) * ROWS, 8)
            here[f, spot, :] = now[pl.ds(f * 64 + x * 8, 8), :]
            start[f, spot, :] = base[pl.ds(f * 64 + x * 8, 8), :]
            for t in range(2):
                stored[2 * f + t, spot, :] = fwd[(e * 4 + t + 1) * 3 + c, x].astype(F32)
    for m in range(4):
        for x in range(8):
            medium[m, pl.ds((x + 2) * ROWS, 8), :] = med[pl.ds(m * 64 + x * 8, 8), :]

    def place(tile, put):
        for f in range(fields):
            put(here, f, 1, join(tile(2 * f)))
            put(here, f, 2, join(tile(2 * f + 1)))
            put(start, f, 1, join(tile(2 * fields + f)))
            both = tile(3 * fields + f).astype(F32)
            put(stored, 2 * f, 1, both[:8])
            put(stored, 2 * f + 1, 1, both[8:])
        for k, m in enumerate((SHEAR, LAME, INV)):
            both = tile(4 * fields + k).astype(F32)
            put(medium, m, 1, both[:8])
            put(medium, m, 2, both[8:])
        put(medium, BUOY, 1, tile(4 * fields + 3).astype(F32)[:8])

    def nothing(_):
        return jnp.zeros((16, 128), BF16)

    for k, name in enumerate("AB"):
        up = upward("gx", name)

        def put_x(ref, index, ring, values, up=up):
            row = pl.multiple_of(x_row(up, ring) * ROWS, ROWS)
            ref[index, pl.ds(row, 8), :] = values

        if name == "A" and their_turn(x_rounds, y_rounds):
            for message, when in (
                (y_messages[1], is_first()),
                (x_messages[0], jnp.logical_not(is_first())),
            ):
                pl.when(when)(functools.partial(place, masked(message, "gx", name), put_x))
        else:
            place(masked(x_messages[k], "gx", name) if k < len(x_rounds) else nothing, put_x)
    for k, name in enumerate("AB"):
        up = upward("gy", name)

        def put_y(ref, index, ring, values, up=up):
            ref[index, pl.ds(2 * ROWS + y_place(up, ring), 8, stride=ROWS), :] = values

        place(masked(y_messages[k], "gy", name) if k < len(y_rounds) else nothing, put_y)

    for row in range(1, 11):
        values = coefficients(lambda m, r: row_of(medium, m, r), row, row < 10)
        for name, value in values.items():
            coef[COEFFICIENTS.index(name), pl.ds(row * ROWS, ROWS), :] = value

    def faces(name, row):
        if name == "inverse":
            return row_of(medium, INV, row)
        return row_of(coef, COEFFICIENTS.index(name), row)

    sums = {}
    for e in range(events):
        first = Event(lambda c, row, e=e: row_of(here, 3 * e + c, row))
        apply = first.operator(faces)
        waves = [
            Event(lambda c, row, e=e, t=t: row_of(stored, 2 * (3 * e + c) + t, row))
            for t in range(2)
        ]
        for row in range(2, 10):
            if 3 <= row <= 8:
                scale = STEP_FACTOR * row_of(medium, BUOY, row)
                for c, result in enumerate(apply(row)):
                    f = 3 * e + c
                    then[f, pl.ds(row * ROWS, ROWS), :] = row_of(start, f, row) + scale * result
            gather(sums, first, waves[0], fwd, e, 0, row)
        second = Event(lambda c, row, e=e: row_of(then, 3 * e + c, row))
        for row in range(4, 8):
            gather(sums, second, waves[1], fwd, e, 1, row)
    for row in range(2, 10):
        inverse = tile_row(med, INV, row)
        shear = sums["lateral", row] + inverse * inverse * sums["upright", row]
        part[pl.ds((row - 2) * 8, 8), :] = -0.25 * shear
        part[pl.ds(64 + (row - 2) * 8, 8), :] = -sums["density", row]


def gather(sums, field, wave, fwd, e, t, row):
    for c in range(3):
        ax, ay, az = field.slopes(c, row)
        ux, uy, uz = wave.slopes(c, row)
        newer = fwd[(e * 4 + t) * 3 + c, row - 2].astype(F32)
        older = fwd[(e * 4 + t + 2) * 3 + c, row - 2].astype(F32)
        bend = newer - 2.0 * wave.value(c, row)[:8] + older
        add_to(sums, ("lateral", row), ax * ux + ay * uy)
        add_to(sums, ("upright", row), az * uz)
        add_to(sums, ("density", row), field.value(c, row)[:8] * bend)


OUTER = (0, 1, 10, 11)
EDGES = (1, 2, 9, 10)


def edge_kernel(events, x_rounds, y_rounds, shares, *refs):
    fields = 3 * events
    count = len(x_rounds) * len(y_rounds)
    corners, refs = refs[:count], refs[count:]
    (here, start, stored, medium, coef, then, part, fwd, med), refs = refs[:9], refs[9:]
    edge, own_share, *sent = refs[: 1 + shares]
    outer, outer_start, outer_medium, outer_coef, slabs = refs[1 + shares :]

    height = len(OUTER) * ROWS
    for k, row in enumerate(OUTER):
        for f in range(fields):
            spot = pl.ds(f * height + k * ROWS, ROWS)
            outer[spot, :] = row_of(here, f, row)
            if row in EDGES:
                outer_start[spot, :] = row_of(start, f, row)
        for m in range(4):
            outer_medium[pl.ds(m * height + k * ROWS, ROWS), :] = row_of(medium, m, row)
    for kx, name_x in enumerate("AB"):
        for ky, name_y in enumerate("AB"):
            corner = None
            if kx < len(x_rounds) and ky < len(y_rounds):
                corner = corners[kx * len(y_rounds) + ky]
            up_x, up_y = upward("gx", name_x), upward("gy", name_y)
            real = jnp.logical_and(linked("gx", name_x), linked("gy", name_y))
            for ring_x in (1, 2):
                for ring_y in (1, 2):
                    place = jnp.where(up_x, 1 + ring_x, 2 - ring_x)
                    spot = place * ROWS + y_place(up_y, ring_y)

                    def put(ref, first, count):
                        values = jnp.zeros((count, 128), F32)
                        if corner is not None:
                            values = corner[ring_x - 1, ring_y - 1, pl.ds(first, count), :]
                            values = jnp.where(real, values, 0.0)
                        ref[pl.ds(spot, count, stride=height), :] = values

                    put(outer, 0, fields)
                    put(outer_medium, fields, 4)
                    if ring_x == 1 and ring_y == 1:
                        put(outer_start, fields + 4, fields)

    def outer_or(ref, full):
        def pick(index, row):
            if row in OUTER:
                return ref[pl.ds(index * height + OUTER.index(row) * ROWS, ROWS), :]
            return row_of(full, index, row)

        return pick

    field_row, start_row = outer_or(outer, here), outer_or(outer_start, start)
    medium_row = outer_or(outer_medium, medium)
    fresh = (0, 1, 9, 10, 11)
    for k, row in enumerate(fresh):
        for name, value in coefficients(medium_row, row, row < 11).items():
            outer_coef[COEFFICIENTS.index(name), pl.ds(k * ROWS, ROWS), :] = value

    def faces(name, row):
        if name == "inverse":
            return medium_row(INV, row)
        index = COEFFICIENTS.index(name)
        if row in fresh:
            return row_of(outer_coef, index, fresh.index(row))
        return row_of(coef, index, row)

    def then_row(f, row):
        if row in EDGES:
            return row_of(edge, f, EDGES.index(row))
        return row_of(then, f, row)

    sums = {}
    for e in range(events):
        apply = Event(lambda c, row, e=e: field_row(3 * e + c, row)).operator(faces)
        for k, row in enumerate(EDGES):
            scale = STEP_FACTOR * medium_row(BUOY, row)
            for c, result in enumerate(apply(row)):
                f = 3 * e + c
                edge[f, pl.ds(k * ROWS, ROWS), :] = start_row(f, row) + scale * result
        second = Event(lambda c, row, e=e: then_row(3 * e + c, row))
        wave = Event(lambda c, row, e=e: row_of(stored, 2 * (3 * e + c) + 1, row))
        for row in (2, 3, 8, 9):
            gather(sums, second, wave, fwd, e, 1, row)
    grads = [[], []]
    for row in range(2, 10):
        shear, density = tile_row(part, 0, row), tile_row(part, 1, row)
        if row in (2, 3, 8, 9):
            inverse = tile_row(med, INV, row)
            more = sums["lateral", row] + inverse * inverse * sums["upright", row]
            shear = shear - 0.25 * more
            density = density - sums["density", row]
        grads[0].append(shear)
        grads[1].append(density)
    grads = grads[0] + grads[1]
    piece = 128 // shares
    quarter = lax.broadcasted_iota(jnp.int32, (8, 128), 1) // piece
    per = len(grads) // shares
    for j in range(shares):
        for r in range(per):
            tile = None
            for g in range(shares):
                source = grads[r * shares + g]
                moved = pltpu.roll(source, ((g - j) * piece) % 128, axis=1) if g != j else source
                tile = moved if tile is None else jnp.where(quarter == g, moved, tile)
            slabs[j, pl.ds(r * 8, 8), :] = tile
    me = lax.axis_index("ev")
    own_share[...] = slabs[me]
    for m in range(1, shares):
        sent[m - 1][...] = slabs[me ^ m]


def second_kernel(events, now, med, cells, force, medium, coef, then, edge, mid, after):
    rows = [force[e, 1, c, 0] for e in range(events) for c in range(3)]
    pushed = force_field(cells[0], rows, 64)

    def faces(name, row):
        if name == "inverse":
            return row_of(medium, INV, row)
        return row_of(coef, COEFFICIENTS.index(name), row)

    def then_row(f, row):
        if row in EDGES:
            return row_of(edge, f, EDGES.index(row))
        return row_of(then, f, row)

    for e in range(events):
        apply = Event(lambda c, row, e=e: then_row(3 * e + c, row)).operator(faces)
        for row in range(2, 10):
            scale = STEP_FACTOR * tile_row(med, BUOY, row)
            for c, result in enumerate(apply(row)):
                f = 3 * e + c
                first = f * 64 + (row - 2) * 8
                spot = pl.ds(first, 8)
                current = then_row(f, row)[:8]
                mid[spot, :] = current
                after[spot, :] = (
                    2.0 * current - now[spot, :] + scale * (result[:8] + pushed[first : first + 8])
                )


def finish_kernel(shares, scale, *refs):
    pieces, (shear, density) = refs[:shares], refs[shares:]
    total = pieces[0][...]
    for piece in pieces[1:]:
        total = total + piece[...]
    width = 128 // shares
    for v in range(16):
        g, r = v % shares, v // shares
        tile = total[r * 8 : (r + 1) * 8]
        if g:
            tile = pltpu.roll(tile, (-g * width) % 128, axis=1)
        out = shear if v < 8 else density
        out[pl.ds((v % 8) * 8, 8), :] = tile[:, :width] * scale


def call(kernel, outs, ins, scratch=(), name=None, cost=1000, out_memory=pltpu.VMEM, pinned=False):
    return pl.pallas_call(
        kernel,
        out_shape=[pltpu.VMEM(s, d) if pinned else jax.ShapeDtypeStruct(s, d) for s, d in outs],
        in_specs=[pl.BlockSpec(memory_space=m) for m in ins],
        out_specs=[pl.BlockSpec(memory_space=out_memory)] * len(outs),
        scratch_shapes=[s if not isinstance(s, tuple) else pltpu.VMEM(*s) for s in scratch],
        compiler_params=pltpu.CompilerParams(vmem_limit_bytes=VMEM_LIMIT),
        cost_estimate=pl.CostEstimate(
            flops=cost * 1024, bytes_accessed=cost * 1024, transcendentals=0
        ),
        name=name,
    )


def wait_for(before, messages):
    arrays = [*before, *messages]
    return call(
        lambda *refs: None,
        [((8, 128), F32)],
        [pl.ANY] * len(arrays),
        name="arrival",
        out_memory=pl.ANY,
        cost=8000,
    )(*arrays)


def body(adjoint_now, adjoint_prev, forward, medium, drm_cells, drm_force):
    events, _, width_x, width_y, depth = adjoint_now.shape
    fields = 3 * events
    tile = width_x * width_y
    shares = lax.axis_size("ev")
    x_rounds, y_rounds = rounds_of(lax.axis_size("gx")), rounds_of(lax.axis_size("gy"))
    flat = ((fields * tile, depth), F32)
    tall = 12 * ROWS

    face = ((4 * fields + 4, 16, depth), BF16)
    corner = ((2, 2, 2 * fields + 4, depth), F32)
    inputs = [
        adjoint_now.reshape(flat[0]),
        adjoint_prev.reshape(flat[0]),
        forward.reshape(events * 12, width_x, width_y, depth),
        medium.reshape(4 * tile, depth),
        drm_cells,
        drm_force,
    ]
    now, fwd, med, cells, force, base, *messages = call(
        functools.partial(pack_kernel, events, x_rounds, y_rounds),
        [(a.shape, a.dtype) for k, a in enumerate(inputs) if k != 1]
        + [flat]
        + [face] * (len(y_rounds) + len(x_rounds))
        + [corner] * (len(x_rounds) * len(y_rounds)),
        [pltpu.HBM] * len(inputs),
        [flat, ((2 * fields * tile, depth), F32), pltpu.SemaphoreType.DMA((5 + 3 * events,))],
        "pack",
        cost=8000,
        pinned=True,
    )(*(pltpu.with_memory_space_constraint(a, pltpu.HBM) for a in inputs))
    kinds = [{"gy": r} for r in y_rounds] + [{"gx": r} for r in x_rounds]
    kinds += [{"gx": x, "gy": y} for x in x_rounds for y in y_rounds]
    turn = their_turn(x_rounds, y_rounds)
    received = [
        swap(message, kind, turn and kind == {"gy": "B"}, turn and kind == {"gx": "A"})
        for message, kind in zip(messages, kinds)
    ]
    y_messages, rest = received[: len(y_rounds)], received[len(y_rounds) :]
    x_messages, corners = rest[: len(x_rounds)], rest[len(x_rounds) :]
    order = [y_messages[1], y_messages[0]] if turn else [*x_messages[:1], *y_messages[:1]]
    arrival = ()
    for message in order:
        arrival = wait_for(arrival, [message])

    wide = ((fields, tall, depth), F32)
    here, start, stored, tall_medium, coef, then, part = call(
        functools.partial(inner_kernel, events, x_rounds, y_rounds),
        [
            wide,
            wide,
            ((2 * fields, tall, depth), F32),
            ((4, tall, depth), F32),
            ((len(COEFFICIENTS), tall, depth), F32),
            wide,
            ((2 * tile, depth), F32),
        ],
        [pltpu.VMEM] * (4 + len(x_messages) + len(y_messages)) + [pl.ANY] * len(arrival),
        name="inner",
        cost=3000,
    )(now, base, fwd, med, *x_messages, *y_messages, *arrival)
    slab = ((16 // shares * 8, depth), F32)
    outer = ((fields, len(OUTER) * ROWS, depth), F32)
    edge, own_share, *sent = call(
        functools.partial(edge_kernel, events, x_rounds, y_rounds, shares),
        [outer] + [slab] * shares,
        [pltpu.VMEM] * (9 + len(corners)),
        [
            ((fields * len(OUTER) * ROWS, depth), F32),
            ((fields * len(OUTER) * ROWS, depth), F32),
            ((4 * len(OUTER) * ROWS, depth), F32),
            ((len(COEFFICIENTS), 5 * ROWS, depth), F32),
            ((shares,) + slab[0], F32),
        ],
        "edges",
    )(*corners, here, start, stored, tall_medium, coef, then, part, fwd, med)
    pieces = [own_share]
    for m in reversed(range(1, shares)):
        pairs = [(i, i ^ m) for i in range(shares)]
        pieces.append(lax.ppermute(sent[m - 1], "ev", pairs))
    mid, after = call(
        functools.partial(second_kernel, events),
        [flat, flat],
        [pltpu.VMEM] * 8,
        name="second",
    )(now, med, cells, force, tall_medium, coef, then, edge)
    shear, density = call(
        functools.partial(finish_kernel, shares, 1.0 / (events * shares)),
        [((tile, depth // shares), F32)] * 2,
        [pltpu.VMEM] * shares,
        name="finish",
    )(*pieces)
    shape = adjoint_now.shape
    grad = (width_x, width_y, depth // shares)
    return mid.reshape(shape), after.reshape(shape), shear.reshape(grad), density.reshape(grad)


def solution(mesh):
    in_specs = (
        P("ev", None, "gx", "gy", None),
        P("ev", None, "gx", "gy", None),
        P("ev", None, None, "gx", "gy", None),
        P(None, "gx", "gy", None),
        P("gx", "gy", None),
        P("ev", None, None, "gx", "gy", None),
    )
    out_specs = (
        P("ev", None, "gx", "gy", None),
        P("ev", None, "gx", "gy", None),
        P("gx", "gy", "ev"),
        P("gx", "gy", "ev"),
    )
    return jax.shard_map(body, mesh=mesh, in_specs=in_specs, out_specs=out_specs, check_vma=False)
```

```python
import functools
import itertools

import jax
import jax.numpy as jnp
from jax import lax
from jax.experimental import pallas as pl
from jax.experimental.pallas import tpu as pltpu
from jax.sharding import PartitionSpec as P

STEP_FACTOR = 0.01
F32, BF16 = jnp.float32, jnp.bfloat16
SHEAR, LAME, BUOY, INV = range(4)
ROWS = 16
VMEM_LIMIT = 40 * 1024 * 1024


def rounds_of(count):
    return "AB"[: max(0, min(2, count - 1))]


def swap(values, rounds, first_along_x=False, first_idle=False):
    names = ("ev", "gx", "gy")
    sizes = [lax.axis_size(a) for a in names]
    pairs = []
    for source in itertools.product(*map(range, sizes)):
        target = list(source)
        steps = {"gx": "A"}.items() if first_along_x and source[2] == 0 else rounds.items()
        for axis, name in steps:
            along = names.index(axis)
            target[along] += 1 if (source[along] % 2 == 0) == (name == "A") else -1
        idle = first_idle and source[2] == 0
        if idle or not all(0 <= t < size for t, size in zip(target, sizes)):
            target = [source[0] ^ 1, *source[1:]]
        flat = [(s[0] * sizes[1] + s[1]) * sizes[2] + s[2] for s in (source, target)]
        pairs.append(tuple(flat))
    return lax.ppermute(values, names, pairs)


def their_turn(x_rounds, y_rounds):
    return bool(x_rounds) and "B" in y_rounds


def is_first():
    return lax.axis_index("gy") == 0


def linked(axis, name):
    other = lax.axis_index(axis) + jnp.where(upward(axis, name), 1, -1)
    return jnp.logical_and(other >= 0, other < lax.axis_size(axis))


def upward(axis, name):
    even = lax.rem(lax.axis_index(axis), 2) == 0
    return even if name == "A" else jnp.logical_not(even)


def split(values):
    high = values.astype(BF16)
    low = (values - high.astype(F32)).astype(BF16)
    return jnp.concatenate([high, low], axis=0)


def join(tile):
    tile = tile.astype(F32)
    return tile[:8] + tile[8:]


def force_field(cells, force_rows, width):
    depth = 128
    count = cells.shape[1]
    place = lax.broadcasted_iota(jnp.int32, (width, count), 0)
    mask = place == cells // depth
    level = lax.broadcasted_iota(jnp.int32, (depth, count), 0)
    hot = jnp.where(level == lax.rem(cells, depth), 1.0, 0.0).astype(BF16)
    left = jnp.concatenate([jnp.where(mask, row, 0.0) for row in force_rows], axis=0)
    total = None
    for _ in range(3):
        part = left.astype(BF16)
        left = left - part.astype(F32)
        term = lax.dot_general(part, hot, (((1,), (1,)), ((), ())), preferred_element_type=F32)
        total = term if total is None else total + term
    return total


def pack_kernel(events, x_rounds, y_rounds, *refs):
    fields = 3 * events
    now_in, prev_in, fwd_in, med_in, cells_in, force_in = refs[:6]
    now, fwd, med, cells, force, base = refs[6:12]
    messages, (prev, stored, arrived) = refs[12:-3], refs[-3:]
    pairs = [(cells_in, cells), (force_in, force), (now_in, now), (prev_in, prev), (med_in, med)]
    for first, count in ((3, 6), (0, 3), (9, 3)):
        for e in range(events):
            part = pl.ds(e * 12 + first, count)
            pairs.append((fwd_in.at[part], fwd.at[part]))
    copies = [
        pltpu.make_async_copy(source, target, arrived.at[k])
        for k, (source, target) in enumerate(pairs)
    ]
    for copy in copies:
        copy.start()
    for copy in copies[:2]:
        copy.wait()
    rows = [force[e, 0, c, 0] for e in range(events) for c in range(3)]
    pushed = force_field(cells[0], rows, 64)
    for copy in copies[2 : 5 + events]:
        copy.wait()
    scale = STEP_FACTOR * med[pl.ds(BUOY * 64, 64), :]
    for f in range(fields):
        spot = pl.ds(f * 64, 64)
        base[spot, :] = 2.0 * now[spot, :] - prev[spot, :] + scale * pushed[f * 64 : (f + 1) * 64]
        e, c = f // 3, f % 3
        for t in range(2):
            part = fwd[(e * 4 + t + 1) * 3 + c].astype(F32).reshape(64, 128)
            stored[pl.ds((f * 2 + t) * 64, 64), :] = part

    def fill(message, pick):
        for f in range(fields):
            message[2 * f] = split(pick(now, f, 1))
            message[2 * f + 1] = split(pick(now, f, 2))
            message[2 * fields + f] = split(pick(base, f, 1))
            message[3 * fields + f] = jnp.concatenate(
                [pick(stored, 2 * f, 1), pick(stored, 2 * f + 1, 1)], axis=0
            ).astype(BF16)
        for k, m in enumerate((SHEAR, LAME, INV)):
            message[4 * fields + k] = jnp.concatenate(
                [pick(med, m, 1), pick(med, m, 2)], axis=0
            ).astype(BF16)
        edge = pick(med, BUOY, 1)
        message[4 * fields + 3] = jnp.concatenate([edge, edge], axis=0).astype(BF16)

    def face(axis, name, ring):
        return jnp.where(upward(axis, name), 8 - ring, ring - 1)

    def pick_x(name):
        def pick(ref, index, ring):
            row = pl.multiple_of(face("gx", name, ring) * 8, 8)
            return ref[pl.ds(index * 64 + row, 8), :]

        return pick

    targets = iter(messages)
    for name in y_rounds:

        def pick_y(ref, index, ring, name=name):
            return ref[pl.ds(index * 64 + face("gy", name, ring), 8, stride=8), :]

        if name == "B" and their_turn(x_rounds, y_rounds):
            message = next(targets)
            pl.when(is_first())(functools.partial(fill, message, pick_x("A")))
            pl.when(jnp.logical_not(is_first()))(functools.partial(fill, message, pick_y))
        else:
            fill(next(targets), pick_y)
    for name in x_rounds:
        fill(next(targets), pick_x(name))
    for name_x in x_rounds:
        for name_y in y_rounds:
            message = next(targets)
            for ring_x in (1, 2):
                for ring_y in (1, 2):
                    cell = face("gx", name_x, ring_x) * 8 + face("gy", name_y, ring_y)
                    target = message.at[ring_x - 1, ring_y - 1]
                    target[pl.ds(0, fields), :] = now[pl.ds(cell, fields, stride=64), :]
                    target[pl.ds(fields, 4), :] = med[pl.ds(cell, 4, stride=64), :]
                    picked = base[pl.ds(cell, fields, stride=64), :]
                    target[pl.ds(fields + 4, fields), :] = picked
    for copy in copies[5 + events :]:
        copy.wait()


def masked(message, axis, name):
    if name == "A" and lax.axis_size(axis) % 2 == 0:
        return lambda index: message[index]
    real = linked(axis, name)
    return lambda index: jnp.where(real, message[index].astype(F32), 0.0).astype(BF16)


def shift_z(values, step):
    depth = values.shape[-1]
    lane = lax.broadcasted_iota(jnp.int32, values.shape, values.ndim - 1)
    moved = pltpu.roll(values, (-step) % depth, axis=values.ndim - 1)
    return jnp.where(lane == (depth - 1 if step > 0 else 0), 0.0, moved)


def shift_y(values, step):
    return pltpu.roll(values, (-step) % ROWS, axis=0)


def row_of(ref, index, row):
    return ref[index, pl.ds(row * ROWS, ROWS), :]


COEFFICIENTS = (
    ("own_x", "other_x", "own_y", "other_y", "own_z", "other_z", "cross", "cross_z")
    + ("own_y_down", "other_y_down", "own_z_down", "other_z_down")
)


def coefficients(medium, row, ahead=True):
    def both_of(row):
        return medium(LAME, row) + 2.0 * medium(SHEAR, row)

    shear, lame, inverse = (medium(m, row) for m in (SHEAR, LAME, INV))
    both = both_of(row)
    values = {}
    if ahead:
        values["own_x"] = 0.5 * (both + both_of(row + 1))
        values["other_x"] = 0.5 * (shear + medium(SHEAR, row + 1))
    for tail, step in (("", 1), ("_down", -1)):
        values["own_y" + tail] = 0.5 * (both + shift_y(both, step))
        values["other_y" + tail] = 0.5 * (shear + shift_y(shear, step))
        spacing = 0.25 * (inverse + shift_z(inverse, step))
        values["own_z" + tail] = spacing * (both + shift_z(both, step))
        values["other_z" + tail] = spacing * (shear + shift_z(shear, step))
    values["cross"] = 0.25 * (lame + shear)
    values["cross_z"] = values["cross"] * inverse
    return values


class Event:
    def __init__(self, value):
        self.value = functools.cache(value)
        self.y = functools.cache(lambda c, row, step: shift_y(self.value(c, row), step))
        self.z = functools.cache(lambda c, row, step: shift_z(self.value(c, row), step))

    def slopes(self, c, row):
        return (
            (self.value(c, row + 1) - self.value(c, row - 1))[:8],
            (self.y(c, row, 1) - self.y(c, row, -1))[:8],
            (self.z(c, row, 1) - self.z(c, row, -1))[:8],
        )

    def operator(self, faces, sign=None):
        value = self.value

        def signed(values):
            return values if sign is None else sign * values

        @functools.cache
        def slope(d, row):
            if d == 0:
                return signed(faces("cross", row) * (value(0, row + 1) - value(0, row - 1)))
            if d == 1:
                return faces("cross", row) * (self.y(1, row, 1) - self.y(1, row, -1))
            return faces("cross_z", row) * (self.z(2, row, 1) - self.z(2, row, -1))

        @functools.cache
        def flux_x(c, row):
            kind = "own_x" if c == 0 else "other_x"
            return faces(kind, row) * (value(c, row + 1) - value(c, row))

        def apply(row):
            results = []
            for c in range(3):
                here = value(c, row)
                total = flux_x(c, row) - flux_x(c, row - 1)
                kind = "own_y" if c == 1 else "other_y"
                total = total + (
                    faces(kind, row) * (self.y(c, row, 1) - here)
                    - faces(kind + "_down", row) * (here - self.y(c, row, -1))
                )
                kind = "own_z" if c == 2 else "other_z"
                upright = faces(kind, row) * (self.z(c, row, 1) - here) - faces(
                    kind + "_down", row
                ) * (here - self.z(c, row, -1))
                if c == 0:
                    total = total + signed(
                        (slope(1, row + 1) + slope(2, row + 1))
                        - (slope(1, row - 1) + slope(2, row - 1))
                    )
                elif c == 1:
                    mixed = slope(0, row) + slope(2, row)
                    total = total + (shift_y(mixed, 1) - shift_y(mixed, -1))
                else:
                    mixed = slope(0, row) + slope(1, row)
                    upright = upright + (shift_z(mixed, 1) - shift_z(mixed, -1))
                results.append(total + faces("inverse", row) * upright)
            return results

        return apply


def x_row(up, ring):
    return jnp.where(up, 9 + ring, 2 - ring)


def y_place(up, ring):
    return jnp.where(up, 7 + ring, ROWS - ring)


def tile_row(ref, index, row):
    return ref[pl.ds(index * 64 + (row - 2) * 8, 8), :]


def add_to(sums, key, value):
    sums[key] = sums[key] + value if key in sums else value


def inner_kernel(events, x_rounds, y_rounds, now, base, fwd, med, *refs):
    fields = 3 * events
    x_messages, refs = refs[: len(x_rounds)], refs[len(x_rounds) :]
    y_messages, refs = refs[: len(y_rounds)], refs[len(y_rounds) :]
    here, start, stored, medium, coef, then, part = refs[-7:]

    for f in range(fields):
        e, c = f // 3, f % 3
        for x in range(8):
            spot = pl.ds((x + 2) * ROWS, 8)
            here[f, spot, :] = now[pl.ds(f * 64 + x * 8, 8), :]
            start[f, spot, :] = base[pl.ds(f * 64 + x * 8, 8), :]
            for t in range(2):
                stored[2 * f + t, spot, :] = fwd[(e * 4 + t + 1) * 3 + c, x].astype(F32)
    for m in range(4):
        for x in range(8):
            medium[m, pl.ds((x + 2) * ROWS, 8), :] = med[pl.ds(m * 64 + x * 8, 8), :]

    def place(tile, put):
        for f in range(fields):
            put(here, f, 1, join(tile(2 * f)))
            put(here, f, 2, join(tile(2 * f + 1)))
            put(start, f, 1, join(tile(2 * fields + f)))
            both = tile(3 * fields + f).astype(F32)
            put(stored, 2 * f, 1, both[:8])
            put(stored, 2 * f + 1, 1, both[8:])
        for k, m in enumerate((SHEAR, LAME, INV)):
            both = tile(4 * fields + k).astype(F32)
            put(medium, m, 1, both[:8])
            put(medium, m, 2, both[8:])
        put(medium, BUOY, 1, tile(4 * fields + 3).astype(F32)[:8])

    def nothing(_):
        return jnp.zeros((16, 128), BF16)

    near = one_sided(x_rounds)
    if near:
        zeros = jnp.zeros((ROWS, 128), F32)
        for row in (0, 1, 10, 11):
            spot = pl.ds(row * ROWS, ROWS)
            for f in range(fields):
                here[f, spot, :] = zeros
                start[f, spot, :] = zeros
            for m in range(4):
                medium[m, spot, :] = zeros
        for row in (1, 10):
            for k in range(2 * fields):
                stored[k, pl.ds(row * ROWS, 8), :] = zeros[:8]
    for k, name in enumerate("A" if near else "AB"):
        up = upward("gx", name)

        def put_x(ref, index, ring, values, up=up):
            row = pl.multiple_of(x_row(up, ring) * ROWS, ROWS)
            ref[index, pl.ds(row, 8), :] = values

        if name == "A" and their_turn(x_rounds, y_rounds):
            for message, when in (
                (y_messages[1], is_first()),
                (x_messages[0], jnp.logical_not(is_first())),
            ):
                pl.when(when)(functools.partial(place, masked(message, "gx", name), put_x))
        else:
            place(masked(x_messages[k], "gx", name) if k < len(x_rounds) else nothing, put_x)
    for k, name in enumerate("AB"):
        up = upward("gy", name)

        def put_y(ref, index, ring, values, up=up):
            ref[index, pl.ds(2 * ROWS + y_place(up, ring), 8, stride=ROWS), :] = values

        place(masked(y_messages[k], "gy", name) if k < len(y_rounds) else nothing, put_y)

    for row in range(1, 11):
        values = coefficients(lambda m, r: row_of(medium, m, r), row, row < 10)
        for name, value in values.items():
            coef[COEFFICIENTS.index(name), pl.ds(row * ROWS, ROWS), :] = value

    def faces(name, row):
        if name == "inverse":
            return row_of(medium, INV, row)
        return row_of(coef, COEFFICIENTS.index(name), row)

    sums = {}
    for e in range(events):
        first = Event(lambda c, row, e=e: row_of(here, 3 * e + c, row))
        apply = first.operator(faces)
        waves = [
            Event(lambda c, row, e=e, t=t: row_of(stored, 2 * (3 * e + c) + t, row))
            for t in range(2)
        ]
        for row in range(2, 10):
            if near or 3 <= row <= 8:
                scale = STEP_FACTOR * row_of(medium, BUOY, row)
                for c, result in enumerate(apply(row)):
                    f = 3 * e + c
                    then[f, pl.ds(row * ROWS, ROWS), :] = row_of(start, f, row) + scale * result
            gather(sums, first, waves[0], fwd, e, 0, row)
        second = Event(lambda c, row, e=e: row_of(then, 3 * e + c, row))
        for row in range(4, 8):
            gather(sums, second, waves[1], fwd, e, 1, row)
    for row in range(2, 10):
        inverse = tile_row(med, INV, row)
        shear = sums["lateral", row] + inverse * inverse * sums["upright", row]
        part[pl.ds((row - 2) * 8, 8), :] = -0.25 * shear
        part[pl.ds(64 + (row - 2) * 8, 8), :] = -sums["density", row]
    if near:
        mirror, sums = Mirror(), {}
        for f in range(fields):
            then[f, pl.ds(pl.multiple_of(mirror.row(1) * ROWS, ROWS), ROWS), :] = zeros
        for e in range(events):
            second = Event(lambda c, row, e=e: mirror.of(then, 3 * e + c, row))
            wave = Event(lambda c, row, e=e: mirror.of(stored, 2 * (3 * e + c) + 1, row))
            for row in (2, 3):
                gather(sums, second, wave, fwd, e, 1, row, mirror.row(row) - 2)
        for row in (2, 3):
            mirror.add(part, sums, med, row)


def gather(sums, field, wave, fwd, e, t, row, x=None):
    x = row - 2 if x is None else x
    for c in range(3):
        ax, ay, az = field.slopes(c, row)
        ux, uy, uz = wave.slopes(c, row)
        newer = fwd[(e * 4 + t) * 3 + c, x].astype(F32)
        older = fwd[(e * 4 + t + 2) * 3 + c, x].astype(F32)
        bend = newer - 2.0 * wave.value(c, row)[:8] + older
        add_to(sums, ("lateral", row), ax * ux + ay * uy)
        add_to(sums, ("upright", row), az * uz)
        add_to(sums, ("density", row), field.value(c, row)[:8] * bend)


def one_sided(x_rounds):
    return x_rounds == "A" and lax.axis_size("gx") == 2


class Mirror:
    def __init__(self):
        self.up = upward("gx", "A")
        self.sign = jnp.where(self.up, 1.0, -1.0)
        self.row = functools.cache(lambda r: jnp.where(self.up, r, 11 - r))

    def of(self, ref, index, row):
        start = pl.multiple_of(self.row(row) * ROWS, ROWS)
        return ref[index, pl.ds(start, ROWS), :]

    def tile(self, index, row):
        return pl.ds(pl.multiple_of(index * 64 + (self.row(row) - 2) * 8, 8), 8)

    def add(self, part, sums, med, row):
        inverse = med[self.tile(INV, row), :]
        more = sums["lateral", row] + inverse * inverse * sums["upright", row]
        for index, value in ((0, -0.25 * more), (1, -sums["density", row])):
            spot = self.tile(index, row)
            part[spot, :] = part[spot, :] + value


OUTER = (0, 1, 10, 11)
EDGES = (1, 2, 9, 10)


def edge_kernel(events, x_rounds, y_rounds, shares, *refs):
    fields = 3 * events
    count = len(x_rounds) * len(y_rounds)
    corners, refs = refs[:count], refs[count:]
    (here, start, stored, medium, coef, then, part, fwd, med), refs = refs[:9], refs[9:]
    edge, own_share, *sent = refs[: 1 + shares]
    outer, outer_start, outer_medium, outer_coef, slabs = refs[1 + shares :]

    height = len(OUTER) * ROWS
    for k, row in enumerate(OUTER):
        for f in range(fields):
            spot = pl.ds(f * height + k * ROWS, ROWS)
            outer[spot, :] = row_of(here, f, row)
            if row in EDGES:
                outer_start[spot, :] = row_of(start, f, row)
        for m in range(4):
            outer_medium[pl.ds(m * height + k * ROWS, ROWS), :] = row_of(medium, m, row)
    for kx, name_x in enumerate("AB"):
        for ky, name_y in enumerate("AB"):
            corner = None
            if kx < len(x_rounds) and ky < len(y_rounds):
                corner = corners[kx * len(y_rounds) + ky]
            up_x, up_y = upward("gx", name_x), upward("gy", name_y)
            real = jnp.logical_and(linked("gx", name_x), linked("gy", name_y))
            for ring_x in (1, 2):
                for ring_y in (1, 2):
                    place = jnp.where(up_x, 1 + ring_x, 2 - ring_x)
                    spot = place * ROWS + y_place(up_y, ring_y)

                    def put(ref, first, count):
                        values = jnp.zeros((count, 128), F32)
                        if corner is not None:
                            values = corner[ring_x - 1, ring_y - 1, pl.ds(first, count), :]
                            values = jnp.where(real, values, 0.0)
                        ref[pl.ds(spot, count, stride=height), :] = values

                    put(outer, 0, fields)
                    put(outer_medium, fields, 4)
                    if ring_x == 1 and ring_y == 1:
                        put(outer_start, fields + 4, fields)

    def outer_or(ref, full):
        def pick(index, row):
            if row in OUTER:
                return ref[pl.ds(index * height + OUTER.index(row) * ROWS, ROWS), :]
            return row_of(full, index, row)

        return pick

    field_row, start_row = outer_or(outer, here), outer_or(outer_start, start)
    medium_row = outer_or(outer_medium, medium)
    fresh = (0, 1, 9, 10, 11)
    for k, row in enumerate(fresh):
        for name, value in coefficients(medium_row, row, row < 11).items():
            outer_coef[COEFFICIENTS.index(name), pl.ds(k * ROWS, ROWS), :] = value

    def faces(name, row):
        if name == "inverse":
            return medium_row(INV, row)
        index = COEFFICIENTS.index(name)
        if row in fresh:
            return row_of(outer_coef, index, fresh.index(row))
        return row_of(coef, index, row)

    def then_row(f, row):
        if row in EDGES:
            return row_of(edge, f, EDGES.index(row))
        return row_of(then, f, row)

    sums = {}
    for e in range(events):
        apply = Event(lambda c, row, e=e: field_row(3 * e + c, row)).operator(faces)
        for k, row in enumerate(EDGES):
            scale = STEP_FACTOR * medium_row(BUOY, row)
            for c, result in enumerate(apply(row)):
                f = 3 * e + c
                edge[f, pl.ds(k * ROWS, ROWS), :] = start_row(f, row) + scale * result
        second = Event(lambda c, row, e=e: then_row(3 * e + c, row))
        wave = Event(lambda c, row, e=e: row_of(stored, 2 * (3 * e + c) + 1, row))
        for row in (2, 3, 8, 9):
            gather(sums, second, wave, fwd, e, 1, row)
    grads = [[], []]
    for row in range(2, 10):
        shear, density = tile_row(part, 0, row), tile_row(part, 1, row)
        if row in (2, 3, 8, 9):
            inverse = tile_row(med, INV, row)
            more = sums["lateral", row] + inverse * inverse * sums["upright", row]
            shear = shear - 0.25 * more
            density = density - sums["density", row]
        grads[0].append(shear)
        grads[1].append(density)
    cut(grads[0] + grads[1], shares, slabs, own_share, sent)


def cut(grads, shares, slabs, own_share, sent):
    piece = 128 // shares
    quarter = lax.broadcasted_iota(jnp.int32, (8, 128), 1) // piece
    per = len(grads) // shares
    for j in range(shares):
        for r in range(per):
            tile = None
            for g in range(shares):
                source = grads[r * shares + g]
                moved = pltpu.roll(source, ((g - j) * piece) % 128, axis=1) if g != j else source
                tile = moved if tile is None else jnp.where(quarter == g, moved, tile)
            slabs[j, pl.ds(r * 8, 8), :] = tile
    me = lax.axis_index("ev")
    own_share[...] = slabs[me]
    for m in range(1, shares):
        sent[m - 1][...] = slabs[me ^ m]


def near_kernel(events, x_rounds, y_rounds, shares, *refs):
    fields = 3 * events
    corners, refs = refs[: len(y_rounds)], refs[len(y_rounds) :]
    (here, start, stored, medium, coef, then, part, fwd, med), refs = refs[:9], refs[9:]
    edge, own_share, *sent = refs[: 1 + shares]
    outer, outer_start, outer_medium, outer_coef, total, slabs = refs[1 + shares :]
    mirror = Mirror()

    height = 2 * ROWS
    for f in range(fields):
        outer_start[pl.ds(f * ROWS, ROWS), :] = mirror.of(start, f, 10)
    for k, row in enumerate((10, 11)):
        for f in range(fields):
            outer[pl.ds(f * height + k * ROWS, ROWS), :] = mirror.of(here, f, row)
        for m in range(4):
            outer_medium[pl.ds(m * height + k * ROWS, ROWS), :] = mirror.of(medium, m, row)
    for corner, name in zip(corners, y_rounds):
        up_y, real = upward("gy", name), linked("gy", name)
        for ring_x in (1, 2):
            for ring_y in (1, 2):
                place = y_place(up_y, ring_y)
                spot = (ring_x - 1) * ROWS + place

                def put(ref, spot, first, count, stride):
                    values = corner[ring_x - 1, ring_y - 1, pl.ds(first, count), :]
                    ref[pl.ds(spot, count, stride=stride), :] = jnp.where(real, values, 0.0)

                put(outer, spot, 0, fields, height)
                put(outer_medium, spot, fields, 4, height)
                if ring_x == 1 and ring_y == 1:
                    put(outer_start, place, fields + 4, fields, ROWS)

    def row_with(ref, full):
        def pick(index, row):
            if row >= 10:
                return ref[pl.ds(index * height + (row - 10) * ROWS, ROWS), :]
            return mirror.of(full, index, row)

        return pick

    field_row, medium_row = row_with(outer, here), row_with(outer_medium, medium)
    for k, row in enumerate((9, 10, 11)):
        for name, value in coefficients(medium_row, row, row < 11).items():
            if row > 9 or name in ("own_x", "other_x"):
                outer_coef[COEFFICIENTS.index(name), pl.ds(k * ROWS, ROWS), :] = value

    def faces(name, row):
        if name == "inverse":
            return medium_row(INV, row)
        index = COEFFICIENTS.index(name)
        along_x = name in ("own_x", "other_x")
        if row >= (9 if along_x else 10):
            return row_of(outer_coef, index, row - 9)
        first = jnp.where(mirror.up, row, 10 - row) if along_x else mirror.row(row)
        return coef[index, pl.ds(pl.multiple_of(first * ROWS, ROWS), ROWS), :]

    def slot(row):
        up, down = EDGES.index(row), EDGES.index(11 - row)
        return pl.ds(pl.multiple_of(jnp.where(mirror.up, up, down) * ROWS, ROWS), ROWS)

    def then_row(f, row):
        return edge[f, slot(row), :] if row > 8 else mirror.of(then, f, row)

    sums = {}
    for e in range(events):
        apply = Event(lambda c, row, e=e: field_row(3 * e + c, row)).operator(faces, mirror.sign)
        for row in (9, 10):
            scale = STEP_FACTOR * medium_row(BUOY, row)
            for c, result in enumerate(apply(row)):
                f = 3 * e + c
                first = outer_start[pl.ds(f * ROWS, ROWS), :] if row == 10 else mirror.of(start, f, 9)
                edge[f, slot(row), :] = first + scale * result
                edge[f, slot(11 - row), :] = mirror.of(then, f, 11 - row)
        second = Event(lambda c, row, e=e: then_row(3 * e + c, row))
        wave = Event(lambda c, row, e=e: mirror.of(stored, 2 * (3 * e + c) + 1, row))
        for row in (8, 9):
            gather(sums, second, wave, fwd, e, 1, row, mirror.row(row) - 2)
    total[...] = part[...]
    for row in (8, 9):
        mirror.add(total, sums, med, row)
    grads = [total[pl.ds(8 * k, 8), :] for k in range(16)]
    cut(grads, shares, slabs, own_share, sent)


def second_kernel(events, now, med, cells, force, medium, coef, then, edge, mid, after):
    rows = [force[e, 1, c, 0] for e in range(events) for c in range(3)]
    pushed = force_field(cells[0], rows, 64)

    def faces(name, row):
        if name == "inverse":
            return row_of(medium, INV, row)
        return row_of(coef, COEFFICIENTS.index(name), row)

    def then_row(f, row):
        if row in EDGES:
            return row_of(edge, f, EDGES.index(row))
        return row_of(then, f, row)

    for e in range(events):
        apply = Event(lambda c, row, e=e: then_row(3 * e + c, row)).operator(faces)
        for row in range(2, 10):
            scale = STEP_FACTOR * tile_row(med, BUOY, row)
            for c, result in enumerate(apply(row)):
                f = 3 * e + c
                first = f * 64 + (row - 2) * 8
                spot = pl.ds(first, 8)
                current = then_row(f, row)[:8]
                mid[spot, :] = current
                after[spot, :] = (
                    2.0 * current - now[spot, :] + scale * (result[:8] + pushed[first : first + 8])
                )


def finish_kernel(shares, scale, *refs):
    pieces, (shear, density) = refs[:shares], refs[shares:]
    total = pieces[0][...]
    for piece in pieces[1:]:
        total = total + piece[...]
    width = 128 // shares
    for v in range(16):
        g, r = v % shares, v // shares
        tile = total[r * 8 : (r + 1) * 8]
        if g:
            tile = pltpu.roll(tile, (-g * width) % 128, axis=1)
        out = shear if v < 8 else density
        out[pl.ds((v % 8) * 8, 8), :] = tile[:, :width] * scale


def call(kernel, outs, ins, scratch=(), name=None, cost=1000, out_memory=pltpu.VMEM, pinned=False):
    return pl.pallas_call(
        kernel,
        out_shape=[pltpu.VMEM(s, d) if pinned else jax.ShapeDtypeStruct(s, d) for s, d in outs],
        in_specs=[pl.BlockSpec(memory_space=m) for m in ins],
        out_specs=[pl.BlockSpec(memory_space=out_memory)] * len(outs),
        scratch_shapes=[s if not isinstance(s, tuple) else pltpu.VMEM(*s) for s in scratch],
        compiler_params=pltpu.CompilerParams(vmem_limit_bytes=VMEM_LIMIT),
        cost_estimate=pl.CostEstimate(
            flops=cost * 1024, bytes_accessed=cost * 1024, transcendentals=0
        ),
        name=name,
    )


def wait_for(before, messages):
    arrays = [*before, *messages]
    return call(
        lambda *refs: None,
        [((8, 128), F32)],
        [pl.ANY] * len(arrays),
        name="arrival",
        out_memory=pl.ANY,
        cost=8000,
    )(*arrays)


def body(adjoint_now, adjoint_prev, forward, medium, drm_cells, drm_force):
    events, _, width_x, width_y, depth = adjoint_now.shape
    fields = 3 * events
    tile = width_x * width_y
    shares = lax.axis_size("ev")
    x_rounds, y_rounds = rounds_of(lax.axis_size("gx")), rounds_of(lax.axis_size("gy"))
    flat = ((fields * tile, depth), F32)
    tall = 12 * ROWS

    face = ((4 * fields + 4, 16, depth), BF16)
    corner = ((2, 2, 2 * fields + 4, depth), F32)
    inputs = [
        adjoint_now.reshape(flat[0]),
        adjoint_prev.reshape(flat[0]),
        forward.reshape(events * 12, width_x, width_y, depth),
        medium.reshape(4 * tile, depth),
        drm_cells,
        drm_force,
    ]
    now, fwd, med, cells, force, base, *messages = call(
        functools.partial(pack_kernel, events, x_rounds, y_rounds),
        [(a.shape, a.dtype) for k, a in enumerate(inputs) if k != 1]
        + [flat]
        + [face] * (len(y_rounds) + len(x_rounds))
        + [corner] * (len(x_rounds) * len(y_rounds)),
        [pltpu.HBM] * len(inputs),
        [flat, ((2 * fields * tile, depth), F32), pltpu.SemaphoreType.DMA((5 + 3 * events,))],
        "pack",
        cost=8000,
        pinned=True,
    )(*(pltpu.with_memory_space_constraint(a, pltpu.HBM) for a in inputs))
    kinds = [{"gy": r} for r in y_rounds] + [{"gx": r} for r in x_rounds]
    kinds += [{"gx": x, "gy": y} for x in x_rounds for y in y_rounds]
    turn = their_turn(x_rounds, y_rounds)
    received = [
        swap(message, kind, turn and kind == {"gy": "B"}, turn and kind == {"gx": "A"})
        for message, kind in zip(messages, kinds)
    ]
    y_messages, rest = received[: len(y_rounds)], received[len(y_rounds) :]
    x_messages, corners = rest[: len(x_rounds)], rest[len(x_rounds) :]
    order = [y_messages[1], y_messages[0]] if turn else [*x_messages[:1], *y_messages[:1]]
    arrival = ()
    for message in order:
        arrival = wait_for(arrival, [message])

    wide = ((fields, tall, depth), F32)
    here, start, stored, tall_medium, coef, then, part = call(
        functools.partial(inner_kernel, events, x_rounds, y_rounds),
        [
            wide,
            wide,
            ((2 * fields, tall, depth), F32),
            ((4, tall, depth), F32),
            ((len(COEFFICIENTS), tall, depth), F32),
            wide,
            ((2 * tile, depth), F32),
        ],
        [pltpu.VMEM] * (4 + len(x_messages) + len(y_messages)) + [pl.ANY] * len(arrival),
        name="inner",
        cost=3000,
    )(now, base, fwd, med, *x_messages, *y_messages, *arrival)
    slab = ((16 // shares * 8, depth), F32)
    outer = ((fields, len(OUTER) * ROWS, depth), F32)
    if one_sided(x_rounds):
        edge_step, scratch = near_kernel, (fields * 2, fields, 4 * 2, 3, ((2 * tile, depth), F32))
    else:
        edge_step, scratch = edge_kernel, (fields * 4, fields * 4, 4 * 4, 5)
    edge, own_share, *sent = call(
        functools.partial(edge_step, events, x_rounds, y_rounds, shares),
        [outer] + [slab] * shares,
        [pltpu.VMEM] * (9 + len(corners)),
        [
            *(((rows * ROWS, depth), F32) for rows in scratch[:3]),
            ((len(COEFFICIENTS), scratch[3] * ROWS, depth), F32),
            *scratch[4:],
            ((shares,) + slab[0], F32),
        ],
        "edges",
    )(*corners, here, start, stored, tall_medium, coef, then, part, fwd, med)
    pieces = [own_share]
    for m in reversed(range(1, shares)):
        pairs = [(i, i ^ m) for i in range(shares)]
        pieces.append(lax.ppermute(sent[m - 1], "ev", pairs))
    mid, after = call(
        functools.partial(second_kernel, events),
        [flat, flat],
        [pltpu.VMEM] * 8,
        name="second",
    )(now, med, cells, force, tall_medium, coef, then, edge)
    shear, density = call(
        functools.partial(finish_kernel, shares, 1.0 / (events * shares)),
        [((tile, depth // shares), F32)] * 2,
        [pltpu.VMEM] * shares,
        name="finish",
    )(*pieces)
    shape = adjoint_now.shape
    grad = (width_x, width_y, depth // shares)
    return mid.reshape(shape), after.reshape(shape), shear.reshape(grad), density.reshape(grad)


def solution(mesh):
    in_specs = (
        P("ev", None, "gx", "gy", None),
        P("ev", None, "gx", "gy", None),
        P("ev", None, None, "gx", "gy", None),
        P(None, "gx", "gy", None),
        P("gx", "gy", None),
        P("ev", None, None, "gx", "gy", None),
    )
    out_specs = (
        P("ev", None, "gx", "gy", None),
        P("ev", None, "gx", "gy", None),
        P("gx", "gy", "ev"),
        P("gx", "gy", "ev"),
    )
    return jax.shard_map(body, mesh=mesh, in_specs=in_specs, out_specs=out_specs, check_vma=False)
```

```python
import functools
import itertools

import jax
import jax.numpy as jnp
from jax import lax
from jax.experimental import pallas as pl
from jax.experimental.pallas import tpu as pltpu
from jax.sharding import PartitionSpec as P

STEP_FACTOR = 0.01
F32, BF16 = jnp.float32, jnp.bfloat16
SHEAR, LAME, BUOY, INV = range(4)
ROWS = 16
VMEM_LIMIT = 40 * 1024 * 1024


def rounds_of(count):
    return "AB"[: max(0, min(2, count - 1))]


def swap(values, rounds, first_along_x=False, first_idle=False):
    names = ("ev", "gx", "gy")
    sizes = [lax.axis_size(a) for a in names]
    pairs = []
    for source in itertools.product(*map(range, sizes)):
        target = list(source)
        steps = {"gx": "A"}.items() if first_along_x and source[2] == 0 else rounds.items()
        for axis, name in steps:
            along = names.index(axis)
            target[along] += 1 if (source[along] % 2 == 0) == (name == "A") else -1
        idle = first_idle and source[2] == 0
        if idle or not all(0 <= t < size for t, size in zip(target, sizes)):
            target = [source[0] ^ 1, *source[1:]]
        flat = [(s[0] * sizes[1] + s[1]) * sizes[2] + s[2] for s in (source, target)]
        pairs.append(tuple(flat))
    return lax.ppermute(values, names, pairs)


def their_turn(x_rounds, y_rounds):
    return bool(x_rounds) and "B" in y_rounds


def is_first():
    return lax.axis_index("gy") == 0


def linked(axis, name):
    other = lax.axis_index(axis) + jnp.where(upward(axis, name), 1, -1)
    return jnp.logical_and(other >= 0, other < lax.axis_size(axis))


def upward(axis, name):
    even = lax.rem(lax.axis_index(axis), 2) == 0
    return even if name == "A" else jnp.logical_not(even)


def padded(count):
    return -(-count // 8) * 8


def face_parts(fields):
    parts = []
    for f in range(fields):
        for kind in ("field", "base"):
            parts += [(kind, f, 1, False)] + [(kind, f, 1, True)]
    parts += [("field", f, 2, False) for f in range(fields)]
    parts += [("wave", k, 1, False) for k in range(2 * fields)]
    for m in (SHEAR, LAME, INV):
        parts += [("medium", m, 1, False), ("medium", m, 2, False)]
    parts.append(("medium", BUOY, 1, False))
    return parts


def corner_layout(fields):
    layout, at = [], 0
    for ring_x in (1, 2):
        for ring_y in (1, 2):
            layout.append(("field", ring_x, ring_y, at))
            at += fields
            if ring_x == 1 and ring_y == 1:
                layout.append(("base", ring_x, ring_y, at))
                at += fields
            layout.append(("medium", ring_x, ring_y, at))
            at += 4
    return layout, -(-at // 16) * 16, -(-at // 16) * 16 + padded(fields) + 8


def take_corner(fields, corner, real, spread, put):
    layout, rows, _ = corner_layout(fields)
    if corner is not None:
        spread[pl.ds(0, rows), :] = jnp.where(real, corner[...].astype(F32), 0.0)
    for kind, ring_x, ring_y, first in layout:
        count = 8 if kind == "medium" else padded(fields)
        values = jnp.zeros((count, 128), F32)
        if corner is not None:
            values = spread[pl.ds(first, count), :]
        put(kind, ring_x, ring_y, values)


def force_field(cells, force_rows, width):
    depth = 128
    count = cells.shape[1]
    place = lax.broadcasted_iota(jnp.int32, (width, count), 0)
    mask = place == cells // depth
    level = lax.broadcasted_iota(jnp.int32, (depth, count), 0)
    hot = jnp.where(level == lax.rem(cells, depth), 1.0, 0.0).astype(BF16)
    left = jnp.concatenate([jnp.where(mask, row, 0.0) for row in force_rows], axis=0)
    total = None
    for _ in range(3):
        part = left.astype(BF16)
        left = left - part.astype(F32)
        term = lax.dot_general(part, hot, (((1,), (1,)), ((), ())), preferred_element_type=F32)
        total = term if total is None else total + term
    return total


def pack_kernel(events, x_rounds, y_rounds, *refs):
    fields = 3 * events
    now_in, prev_in, fwd_in, med_in, cells_in, force_in = refs[:6]
    now, fwd, med, cells, force, base = refs[6:12]
    messages, (prev, stored, spread, arrived) = refs[12:-4], refs[-4:]
    pairs = [(cells_in, cells), (force_in, force), (now_in, now), (prev_in, prev), (med_in, med)]
    for first, count in ((3, 6), (0, 3), (9, 3)):
        for e in range(events):
            part = pl.ds(e * 12 + first, count)
            pairs.append((fwd_in.at[part], fwd.at[part]))
    copies = []
    for k, (source, target) in enumerate(pairs):
        if target.shape != source.shape:
            target = target.at[pl.ds(0, source.shape[0])]
        copies.append(pltpu.make_async_copy(source, target, arrived.at[k]))
    for copy in copies:
        copy.start()
    for copy in copies[:2]:
        copy.wait()
    rows = [force[e, 0, c, 0] for e in range(events) for c in range(3)]
    pushed = force_field(cells[0], rows, 64)
    for copy in copies[2 : 5 + events]:
        copy.wait()
    scale = STEP_FACTOR * med[pl.ds(BUOY * 64, 64), :]
    for f in range(fields):
        spot = pl.ds(f * 64, 64)
        base[spot, :] = 2.0 * now[spot, :] - prev[spot, :] + scale * pushed[f * 64 : (f + 1) * 64]
        e, c = f // 3, f % 3
        for t in range(2):
            part = fwd[(e * 4 + t + 1) * 3 + c].astype(F32).reshape(64, 128)
            stored[pl.ds((f * 2 + t) * 64, 64), :] = part

    sources = {"field": now, "base": base, "wave": stored, "medium": med}

    def fill(message, pick):
        halves = []
        for kind, index, ring, remainder in face_parts(fields):
            value = pick(sources[kind], index, ring)
            halves.append(value - value.astype(BF16).astype(F32) if remainder else value)
        halves += [halves[-1]] * (len(halves) % 2)
        for k in range(0, len(halves), 2):
            message[k // 2] = jnp.concatenate(halves[k : k + 2], axis=0).astype(BF16)

    def face(axis, name, ring):
        return jnp.where(upward(axis, name), 8 - ring, ring - 1)

    def pick_x(name):
        def pick(ref, index, ring):
            row = pl.multiple_of(face("gx", name, ring) * 8, 8)
            return ref[pl.ds(index * 64 + row, 8), :]

        return pick

    targets = iter(messages)
    for name in y_rounds:

        def pick_y(ref, index, ring, name=name):
            return ref[pl.ds(index * 64 + face("gy", name, ring), 8, stride=8), :]

        if name == "B" and their_turn(x_rounds, y_rounds):
            message = next(targets)
            pl.when(is_first())(functools.partial(fill, message, pick_x("A")))
            pl.when(jnp.logical_not(is_first()))(functools.partial(fill, message, pick_y))
        else:
            fill(next(targets), pick_y)
    for name in x_rounds:
        fill(next(targets), pick_x(name))
    for name_x in x_rounds:
        for name_y in y_rounds:
            message = next(targets)
            layout, rows, _ = corner_layout(fields)
            for kind, ring_x, ring_y, first in layout:
                cell = face("gx", name_x, ring_x) * 8 + face("gy", name_y, ring_y)
                count = 8 if kind == "medium" else padded(fields)
                spread[pl.ds(first, count), :] = sources[kind][pl.ds(cell, count, stride=64), :]
            message[...] = spread[pl.ds(0, rows), :].astype(BF16)
    for copy in copies[5 + events :]:
        copy.wait()


def masked(message, axis, name):
    if name == "A" and lax.axis_size(axis) % 2 == 0:
        return lambda index: message[index]
    real = linked(axis, name)
    return lambda index: jnp.where(real, message[index].astype(F32), 0.0).astype(BF16)


def shift_z(values, step):
    depth = values.shape[-1]
    lane = lax.broadcasted_iota(jnp.int32, values.shape, values.ndim - 1)
    moved = pltpu.roll(values, (-step) % depth, axis=values.ndim - 1)
    return jnp.where(lane == (depth - 1 if step > 0 else 0), 0.0, moved)


def shift_y(values, step):
    return pltpu.roll(values, (-step) % ROWS, axis=0)


def row_of(ref, index, row):
    return ref[index, pl.ds(row * ROWS, ROWS), :]


COEFFICIENTS = (
    ("own_x", "other_x", "own_y", "other_y", "own_z", "other_z", "cross", "cross_z")
    + ("own_y_down", "other_y_down", "own_z_down", "other_z_down")
)


def coefficients(medium, row, ahead=True):
    def both_of(row):
        return medium(LAME, row) + 2.0 * medium(SHEAR, row)

    shear, lame, inverse = (medium(m, row) for m in (SHEAR, LAME, INV))
    both = both_of(row)
    values = {}
    if ahead:
        values["own_x"] = 0.5 * (both + both_of(row + 1))
        values["other_x"] = 0.5 * (shear + medium(SHEAR, row + 1))
    for tail, step in (("", 1), ("_down", -1)):
        values["own_y" + tail] = 0.5 * (both + shift_y(both, step))
        values["other_y" + tail] = 0.5 * (shear + shift_y(shear, step))
        spacing = 0.25 * (inverse + shift_z(inverse, step))
        values["own_z" + tail] = spacing * (both + shift_z(both, step))
        values["other_z" + tail] = spacing * (shear + shift_z(shear, step))
    values["cross"] = 0.25 * (lame + shear)
    values["cross_z"] = values["cross"] * inverse
    return values


class Event:
    def __init__(self, value):
        self.value = functools.cache(value)
        self.y = functools.cache(lambda c, row, step: shift_y(self.value(c, row), step))
        self.z = functools.cache(lambda c, row, step: shift_z(self.value(c, row), step))

    def slopes(self, c, row):
        return (
            (self.value(c, row + 1) - self.value(c, row - 1))[:8],
            (self.y(c, row, 1) - self.y(c, row, -1))[:8],
            (self.z(c, row, 1) - self.z(c, row, -1))[:8],
        )

    def operator(self, faces, sign=None):
        value = self.value

        def signed(values):
            return values if sign is None else sign * values

        @functools.cache
        def slope(d, row):
            if d == 0:
                return signed(faces("cross", row) * (value(0, row + 1) - value(0, row - 1)))
            if d == 1:
                return faces("cross", row) * (self.y(1, row, 1) - self.y(1, row, -1))
            return faces("cross_z", row) * (self.z(2, row, 1) - self.z(2, row, -1))

        @functools.cache
        def flux_x(c, row):
            kind = "own_x" if c == 0 else "other_x"
            return faces(kind, row) * (value(c, row + 1) - value(c, row))

        def apply(row):
            results = []
            for c in range(3):
                here = value(c, row)
                total = flux_x(c, row) - flux_x(c, row - 1)
                kind = "own_y" if c == 1 else "other_y"
                total = total + (
                    faces(kind, row) * (self.y(c, row, 1) - here)
                    - faces(kind + "_down", row) * (here - self.y(c, row, -1))
                )
                kind = "own_z" if c == 2 else "other_z"
                upright = faces(kind, row) * (self.z(c, row, 1) - here) - faces(
                    kind + "_down", row
                ) * (here - self.z(c, row, -1))
                if c == 0:
                    total = total + signed(
                        (slope(1, row + 1) + slope(2, row + 1))
                        - (slope(1, row - 1) + slope(2, row - 1))
                    )
                elif c == 1:
                    mixed = slope(0, row) + slope(2, row)
                    total = total + (shift_y(mixed, 1) - shift_y(mixed, -1))
                else:
                    mixed = slope(0, row) + slope(1, row)
                    upright = upright + (shift_z(mixed, 1) - shift_z(mixed, -1))
                results.append(total + faces("inverse", row) * upright)
            return results

        return apply


def x_row(up, ring):
    return jnp.where(up, 9 + ring, 2 - ring)


def y_place(up, ring):
    return jnp.where(up, 7 + ring, ROWS - ring)


def tile_row(ref, index, row):
    return ref[pl.ds(index * 64 + (row - 2) * 8, 8), :]


def add_to(sums, key, value):
    sums[key] = sums[key] + value if key in sums else value


def inner_kernel(events, x_rounds, y_rounds, now, base, fwd, med, *refs):
    fields = 3 * events
    x_messages, refs = refs[: len(x_rounds)], refs[len(x_rounds) :]
    y_messages, refs = refs[: len(y_rounds)], refs[len(y_rounds) :]
    here, start, stored, medium, coef, then, part = refs[-7:]

    for f in range(fields):
        e, c = f // 3, f % 3
        for x in range(8):
            spot = pl.ds((x + 2) * ROWS, 8)
            here[f, spot, :] = now[pl.ds(f * 64 + x * 8, 8), :]
            start[f, spot, :] = base[pl.ds(f * 64 + x * 8, 8), :]
            for t in range(2):
                stored[2 * f + t, spot, :] = fwd[(e * 4 + t + 1) * 3 + c, x].astype(F32)
    for m in range(4):
        for x in range(8):
            medium[m, pl.ds((x + 2) * ROWS, 8), :] = med[pl.ds(m * 64 + x * 8, 8), :]

    targets = {"field": here, "base": start, "wave": stored, "medium": medium}
    parts = face_parts(fields)

    def place(tile, put):
        whole = functools.cache(lambda k: tile(k).astype(F32))
        for k, (kind, index, ring, remainder) in enumerate(parts):
            if remainder:
                continue
            value = whole(k // 2)[8 * (k % 2) :][:8]
            if parts[k + 1 : k + 2] == [(kind, index, ring, True)]:
                value = value + whole((k + 1) // 2)[8 * ((k + 1) % 2) :][:8]
            put(targets[kind], index, ring, value)

    def nothing(_):
        return jnp.zeros((16, 128), BF16)

    near = one_sided(x_rounds)
    if near:
        zeros = jnp.zeros((ROWS, 128), F32)
        for row in (0, 1, 10, 11):
            spot = pl.ds(row * ROWS, ROWS)
            for f in range(fields):
                here[f, spot, :] = zeros
                start[f, spot, :] = zeros
            for m in range(4):
                medium[m, spot, :] = zeros
        for row in (1, 10):
            for k in range(2 * fields):
                stored[k, pl.ds(row * ROWS, 8), :] = zeros[:8]
    for k, name in enumerate("A" if near else "AB"):
        up = upward("gx", name)

        def put_x(ref, index, ring, values, up=up):
            row = pl.multiple_of(x_row(up, ring) * ROWS, ROWS)
            ref[index, pl.ds(row, 8), :] = values

        if name == "A" and their_turn(x_rounds, y_rounds):
            for message, when in (
                (y_messages[1], is_first()),
                (x_messages[0], jnp.logical_not(is_first())),
            ):
                pl.when(when)(functools.partial(place, masked(message, "gx", name), put_x))
        else:
            place(masked(x_messages[k], "gx", name) if k < len(x_rounds) else nothing, put_x)
    for k, name in enumerate("AB"):
        up = upward("gy", name)

        def put_y(ref, index, ring, values, up=up):
            ref[index, pl.ds(2 * ROWS + y_place(up, ring), 8, stride=ROWS), :] = values

        place(masked(y_messages[k], "gy", name) if k < len(y_rounds) else nothing, put_y)

    for row in range(1, 11):
        values = coefficients(lambda m, r: row_of(medium, m, r), row, row < 10)
        for name, value in values.items():
            coef[COEFFICIENTS.index(name), pl.ds(row * ROWS, ROWS), :] = value

    def faces(name, row):
        if name == "inverse":
            return row_of(medium, INV, row)
        return row_of(coef, COEFFICIENTS.index(name), row)

    sums = {}
    for e in range(events):
        first = Event(lambda c, row, e=e: row_of(here, 3 * e + c, row))
        apply = first.operator(faces)
        waves = [
            Event(lambda c, row, e=e, t=t: row_of(stored, 2 * (3 * e + c) + t, row))
            for t in range(2)
        ]
        for row in range(2, 10):
            if near or 3 <= row <= 8:
                scale = STEP_FACTOR * row_of(medium, BUOY, row)
                for c, result in enumerate(apply(row)):
                    f = 3 * e + c
                    then[f, pl.ds(row * ROWS, ROWS), :] = row_of(start, f, row) + scale * result
            gather(sums, first, waves[0], fwd, e, 0, row)
        second = Event(lambda c, row, e=e: row_of(then, 3 * e + c, row))
        for row in range(4, 8):
            gather(sums, second, waves[1], fwd, e, 1, row)
    for row in range(2, 10):
        inverse = tile_row(med, INV, row)
        shear = sums["lateral", row] + inverse * inverse * sums["upright", row]
        part[pl.ds((row - 2) * 8, 8), :] = -0.25 * shear
        part[pl.ds(64 + (row - 2) * 8, 8), :] = -sums["density", row]
    if near:
        mirror, sums = Mirror(), {}
        for f in range(fields):
            then[f, pl.ds(pl.multiple_of(mirror.row(1) * ROWS, ROWS), ROWS), :] = zeros
        for e in range(events):
            second = Event(lambda c, row, e=e: mirror.of(then, 3 * e + c, row))
            wave = Event(lambda c, row, e=e: mirror.of(stored, 2 * (3 * e + c) + 1, row))
            for row in (2, 3):
                gather(sums, second, wave, fwd, e, 1, row, mirror.row(row) - 2)
        for row in (2, 3):
            mirror.add(part, sums, med, row)


def gather(sums, field, wave, fwd, e, t, row, x=None):
    x = row - 2 if x is None else x
    for c in range(3):
        ax, ay, az = field.slopes(c, row)
        ux, uy, uz = wave.slopes(c, row)
        newer = fwd[(e * 4 + t) * 3 + c, x].astype(F32)
        older = fwd[(e * 4 + t + 2) * 3 + c, x].astype(F32)
        bend = newer - 2.0 * wave.value(c, row)[:8] + older
        add_to(sums, ("lateral", row), ax * ux + ay * uy)
        add_to(sums, ("upright", row), az * uz)
        add_to(sums, ("density", row), field.value(c, row)[:8] * bend)


def one_sided(x_rounds):
    return x_rounds == "A" and lax.axis_size("gx") == 2


class Mirror:
    def __init__(self):
        self.up = upward("gx", "A")
        self.sign = jnp.where(self.up, 1.0, -1.0)
        self.row = functools.cache(lambda r: jnp.where(self.up, r, 11 - r))

    def of(self, ref, index, row):
        start = pl.multiple_of(self.row(row) * ROWS, ROWS)
        return ref[index, pl.ds(start, ROWS), :]

    def tile(self, index, row):
        return pl.ds(pl.multiple_of(index * 64 + (self.row(row) - 2) * 8, 8), 8)

    def add(self, part, sums, med, row):
        inverse = med[self.tile(INV, row), :]
        more = sums["lateral", row] + inverse * inverse * sums["upright", row]
        for index, value in ((0, -0.25 * more), (1, -sums["density", row])):
            spot = self.tile(index, row)
            part[spot, :] = part[spot, :] + value


OUTER = (0, 1, 10, 11)
EDGES = (1, 2, 9, 10)


def edge_kernel(events, x_rounds, y_rounds, shares, *refs):
    fields = 3 * events
    count = len(x_rounds) * len(y_rounds)
    corners, refs = refs[:count], refs[count:]
    (here, start, stored, medium, coef, then, part, fwd, med), refs = refs[:9], refs[9:]
    edge, own_share, *sent = refs[: 1 + shares]
    outer, outer_start, outer_medium, outer_coef, spread, slabs = refs[1 + shares :]

    height = len(OUTER) * ROWS
    for k, row in enumerate(OUTER):
        for f in range(fields):
            spot = pl.ds(f * height + k * ROWS, ROWS)
            outer[spot, :] = row_of(here, f, row)
            if row in EDGES:
                outer_start[spot, :] = row_of(start, f, row)
        for m in range(4):
            outer_medium[pl.ds(m * height + k * ROWS, ROWS), :] = row_of(medium, m, row)
    for kx, name_x in enumerate("AB"):
        for ky, name_y in enumerate("AB"):
            corner = None
            if kx < len(x_rounds) and ky < len(y_rounds):
                corner = corners[kx * len(y_rounds) + ky]
            up_x, up_y = upward("gx", name_x), upward("gy", name_y)
            real = jnp.logical_and(linked("gx", name_x), linked("gy", name_y))

            def put(kind, ring_x, ring_y, values):
                place = jnp.where(up_x, 1 + ring_x, 2 - ring_x)
                spot = pl.ds(place * ROWS + y_place(up_y, ring_y), values.shape[0], stride=height)
                {"field": outer, "base": outer_start, "medium": outer_medium}[kind][spot, :] = values

            take_corner(fields, corner, real, spread, put)

    def outer_or(ref, full):
        def pick(index, row):
            if row in OUTER:
                return ref[pl.ds(index * height + OUTER.index(row) * ROWS, ROWS), :]
            return row_of(full, index, row)

        return pick

    field_row, start_row = outer_or(outer, here), outer_or(outer_start, start)
    medium_row = outer_or(outer_medium, medium)
    fresh = (0, 1, 9, 10, 11)
    for k, row in enumerate(fresh):
        for name, value in coefficients(medium_row, row, row < 11).items():
            outer_coef[COEFFICIENTS.index(name), pl.ds(k * ROWS, ROWS), :] = value

    def faces(name, row):
        if name == "inverse":
            return medium_row(INV, row)
        index = COEFFICIENTS.index(name)
        if row in fresh:
            return row_of(outer_coef, index, fresh.index(row))
        return row_of(coef, index, row)

    def then_row(f, row):
        if row in EDGES:
            return row_of(edge, f, EDGES.index(row))
        return row_of(then, f, row)

    sums = {}
    for e in range(events):
        apply = Event(lambda c, row, e=e: field_row(3 * e + c, row)).operator(faces)
        for k, row in enumerate(EDGES):
            scale = STEP_FACTOR * medium_row(BUOY, row)
            for c, result in enumerate(apply(row)):
                f = 3 * e + c
                edge[f, pl.ds(k * ROWS, ROWS), :] = start_row(f, row) + scale * result
        second = Event(lambda c, row, e=e: then_row(3 * e + c, row))
        wave = Event(lambda c, row, e=e: row_of(stored, 2 * (3 * e + c) + 1, row))
        for row in (2, 3, 8, 9):
            gather(sums, second, wave, fwd, e, 1, row)
    grads = [[], []]
    for row in range(2, 10):
        shear, density = tile_row(part, 0, row), tile_row(part, 1, row)
        if row in (2, 3, 8, 9):
            inverse = tile_row(med, INV, row)
            more = sums["lateral", row] + inverse * inverse * sums["upright", row]
            shear = shear - 0.25 * more
            density = density - sums["density", row]
        grads[0].append(shear)
        grads[1].append(density)
    cut(grads[0] + grads[1], shares, slabs, own_share, sent)


def cut(grads, shares, slabs, own_share, sent):
    piece = 128 // shares
    quarter = lax.broadcasted_iota(jnp.int32, (8, 128), 1) // piece
    per = len(grads) // shares
    for j in range(shares):
        for r in range(per):
            tile = None
            for g in range(shares):
                source = grads[r * shares + g]
                moved = pltpu.roll(source, ((g - j) * piece) % 128, axis=1) if g != j else source
                tile = moved if tile is None else jnp.where(quarter == g, moved, tile)
            slabs[j, pl.ds(r * 8, 8), :] = tile
    me = lax.axis_index("ev")
    own_share[...] = slabs[me]
    for m in range(1, shares):
        sent[m - 1][...] = slabs[me ^ m]


def near_kernel(events, x_rounds, y_rounds, shares, *refs):
    fields = 3 * events
    corners, refs = refs[: len(y_rounds)], refs[len(y_rounds) :]
    (here, start, stored, medium, coef, then, part, fwd, med), refs = refs[:9], refs[9:]
    edge, own_share, *sent = refs[: 1 + shares]
    outer, outer_start, outer_medium, outer_coef, spread, total, slabs = refs[1 + shares :]
    mirror = Mirror()

    height = 2 * ROWS
    for f in range(fields):
        outer_start[pl.ds(f * ROWS, ROWS), :] = mirror.of(start, f, 10)
    for k, row in enumerate((10, 11)):
        for f in range(fields):
            outer[pl.ds(f * height + k * ROWS, ROWS), :] = mirror.of(here, f, row)
        for m in range(4):
            outer_medium[pl.ds(m * height + k * ROWS, ROWS), :] = mirror.of(medium, m, row)
    for corner, name in zip(corners, y_rounds):
        up_y, real = upward("gy", name), linked("gy", name)

        def put(kind, ring_x, ring_y, values):
            place = y_place(up_y, ring_y)
            count = values.shape[0]
            if kind == "base":
                outer_start[pl.ds(place, count, stride=ROWS), :] = values
            else:
                target = outer if kind == "field" else outer_medium
                target[pl.ds((ring_x - 1) * ROWS + place, count, stride=height), :] = values

        take_corner(fields, corner, real, spread, put)

    def row_with(ref, full):
        def pick(index, row):
            if row >= 10:
                return ref[pl.ds(index * height + (row - 10) * ROWS, ROWS), :]
            return mirror.of(full, index, row)

        return pick

    field_row, medium_row = row_with(outer, here), row_with(outer_medium, medium)
    for k, row in enumerate((9, 10, 11)):
        for name, value in coefficients(medium_row, row, row < 11).items():
            if row > 9 or name in ("own_x", "other_x"):
                outer_coef[COEFFICIENTS.index(name), pl.ds(k * ROWS, ROWS), :] = value

    def faces(name, row):
        if name == "inverse":
            return medium_row(INV, row)
        index = COEFFICIENTS.index(name)
        along_x = name in ("own_x", "other_x")
        if row >= (9 if along_x else 10):
            return row_of(outer_coef, index, row - 9)
        first = jnp.where(mirror.up, row, 10 - row) if along_x else mirror.row(row)
        return coef[index, pl.ds(pl.multiple_of(first * ROWS, ROWS), ROWS), :]

    def slot(row):
        up, down = EDGES.index(row), EDGES.index(11 - row)
        return pl.ds(pl.multiple_of(jnp.where(mirror.up, up, down) * ROWS, ROWS), ROWS)

    def then_row(f, row):
        return edge[f, slot(row), :] if row > 8 else mirror.of(then, f, row)

    sums = {}
    for e in range(events):
        apply = Event(lambda c, row, e=e: field_row(3 * e + c, row)).operator(faces, mirror.sign)
        for row in (9, 10):
            scale = STEP_FACTOR * medium_row(BUOY, row)
            for c, result in enumerate(apply(row)):
                f = 3 * e + c
                first = outer_start[pl.ds(f * ROWS, ROWS), :] if row == 10 else mirror.of(start, f, 9)
                edge[f, slot(row), :] = first + scale * result
                edge[f, slot(11 - row), :] = mirror.of(then, f, 11 - row)
        second = Event(lambda c, row, e=e: then_row(3 * e + c, row))
        wave = Event(lambda c, row, e=e: mirror.of(stored, 2 * (3 * e + c) + 1, row))
        for row in (8, 9):
            gather(sums, second, wave, fwd, e, 1, row, mirror.row(row) - 2)
    total[...] = part[...]
    for row in (8, 9):
        mirror.add(total, sums, med, row)
    grads = [total[pl.ds(8 * k, 8), :] for k in range(16)]
    cut(grads, shares, slabs, own_share, sent)


def second_kernel(events, now, med, cells, force, medium, coef, then, edge, mid, after):
    rows = [force[e, 1, c, 0] for e in range(events) for c in range(3)]
    pushed = force_field(cells[0], rows, 64)

    def faces(name, row):
        if name == "inverse":
            return row_of(medium, INV, row)
        return row_of(coef, COEFFICIENTS.index(name), row)

    def then_row(f, row):
        if row in EDGES:
            return row_of(edge, f, EDGES.index(row))
        return row_of(then, f, row)

    for e in range(events):
        apply = Event(lambda c, row, e=e: then_row(3 * e + c, row)).operator(faces)
        for row in range(2, 10):
            scale = STEP_FACTOR * tile_row(med, BUOY, row)
            for c, result in enumerate(apply(row)):
                f = 3 * e + c
                first = f * 64 + (row - 2) * 8
                spot = pl.ds(first, 8)
                current = then_row(f, row)[:8]
                mid[spot, :] = current
                after[spot, :] = (
                    2.0 * current - now[spot, :] + scale * (result[:8] + pushed[first : first + 8])
                )


def finish_kernel(shares, scale, *refs):
    pieces, (shear, density) = refs[:shares], refs[shares:]
    total = pieces[0][...]
    for piece in pieces[1:]:
        total = total + piece[...]
    width = 128 // shares
    for v in range(16):
        g, r = v % shares, v // shares
        tile = total[r * 8 : (r + 1) * 8]
        if g:
            tile = pltpu.roll(tile, (-g * width) % 128, axis=1)
        out = shear if v < 8 else density
        out[pl.ds((v % 8) * 8, 8), :] = tile[:, :width] * scale


def call(kernel, outs, ins, scratch=(), name=None, cost=1000, out_memory=pltpu.VMEM, pinned=False):
    return pl.pallas_call(
        kernel,
        out_shape=[pltpu.VMEM(s, d) if pinned else jax.ShapeDtypeStruct(s, d) for s, d in outs],
        in_specs=[pl.BlockSpec(memory_space=m) for m in ins],
        out_specs=[pl.BlockSpec(memory_space=out_memory)] * len(outs),
        scratch_shapes=[s if not isinstance(s, tuple) else pltpu.VMEM(*s) for s in scratch],
        compiler_params=pltpu.CompilerParams(vmem_limit_bytes=VMEM_LIMIT),
        cost_estimate=pl.CostEstimate(
            flops=cost * 1024, bytes_accessed=cost * 1024, transcendentals=0
        ),
        name=name,
    )


def wait_for(before, messages):
    arrays = [*before, *messages]
    return call(
        lambda *refs: None,
        [((8, 128), F32)],
        [pl.ANY] * len(arrays),
        name="arrival",
        out_memory=pl.ANY,
        cost=8000,
    )(*arrays)


def body(adjoint_now, adjoint_prev, forward, medium, drm_cells, drm_force):
    events, _, width_x, width_y, depth = adjoint_now.shape
    fields = 3 * events
    tile = width_x * width_y
    shares = lax.axis_size("ev")
    x_rounds, y_rounds = rounds_of(lax.axis_size("gx")), rounds_of(lax.axis_size("gy"))
    flat = ((fields * tile, depth), F32)
    tall = 12 * ROWS

    face = (((len(face_parts(fields)) + 1) // 2, 16, depth), BF16)
    wide_fields = padded(fields)
    _, corner_rows, spread_rows = corner_layout(fields)
    corner, spread = ((corner_rows, depth), BF16), ((spread_rows, depth), F32)
    roomy = (((wide_fields + 1) * tile, depth), F32)
    inputs = [
        adjoint_now.reshape(flat[0]),
        adjoint_prev.reshape(flat[0]),
        forward.reshape(events * 12, width_x, width_y, depth),
        medium.reshape(4 * tile, depth),
        drm_cells,
        drm_force,
    ]
    now, fwd, med, cells, force, base, *messages = call(
        functools.partial(pack_kernel, events, x_rounds, y_rounds),
        [roomy, (inputs[2].shape, BF16), ((9 * tile, depth), F32)]
        + [(a.shape, a.dtype) for a in inputs[4:]]
        + [roomy]
        + [face] * (len(y_rounds) + len(x_rounds))
        + [corner] * (len(x_rounds) * len(y_rounds)),
        [pltpu.HBM] * len(inputs),
        [
            flat,
            (((2 * fields + 1) * tile, depth), F32),
            spread,
            pltpu.SemaphoreType.DMA((5 + 3 * events,)),
        ],
        "pack",
        cost=8000,
        pinned=True,
    )(*(pltpu.with_memory_space_constraint(a, pltpu.HBM) for a in inputs))
    kinds = [{"gy": r} for r in y_rounds] + [{"gx": r} for r in x_rounds]
    kinds += [{"gx": x, "gy": y} for x in x_rounds for y in y_rounds]
    turn = their_turn(x_rounds, y_rounds)
    received = [
        swap(message, kind, turn and kind == {"gy": "B"}, turn and kind == {"gx": "A"})
        for message, kind in zip(messages, kinds)
    ]
    y_messages, rest = received[: len(y_rounds)], received[len(y_rounds) :]
    x_messages, corners = rest[: len(x_rounds)], rest[len(x_rounds) :]
    order = [y_messages[1], y_messages[0]] if turn else [*x_messages[:1], *y_messages[:1]]
    arrival = ()
    for message in order:
        arrival = wait_for(arrival, [message])

    wide = ((fields, tall, depth), F32)
    here, start, stored, tall_medium, coef, then, part = call(
        functools.partial(inner_kernel, events, x_rounds, y_rounds),
        [
            wide,
            wide,
            ((2 * fields, tall, depth), F32),
            ((4, tall, depth), F32),
            ((len(COEFFICIENTS), tall, depth), F32),
            wide,
            ((2 * tile, depth), F32),
        ],
        [pltpu.VMEM] * (4 + len(x_messages) + len(y_messages)) + [pl.ANY] * len(arrival),
        name="inner",
        cost=3000,
    )(now, base, fwd, med, *x_messages, *y_messages, *arrival)
    slab = ((16 // shares * 8, depth), F32)
    outer = ((fields, len(OUTER) * ROWS, depth), F32)
    if one_sided(x_rounds):
        edge_step, each, fresh, more = near_kernel, (2, 1, 2), 3, [((2 * tile, depth), F32)]
    else:
        edge_step, each, fresh, more = edge_kernel, (len(OUTER),) * 3, 5, []
    room = [wide_fields + 1, wide_fields + 1, 9]
    edge, own_share, *sent = call(
        functools.partial(edge_step, events, x_rounds, y_rounds, shares),
        [outer] + [slab] * shares,
        [pltpu.VMEM] * (9 + len(corners)),
        [
            *(((count * rows * ROWS, depth), F32) for count, rows in zip(room, each)),
            ((len(COEFFICIENTS), fresh * ROWS, depth), F32),
            spread,
            *more,
            ((shares,) + slab[0], F32),
        ],
        "edges",
    )(*corners, here, start, stored, tall_medium, coef, then, part, fwd, med)
    pieces = [own_share]
    for m in reversed(range(1, shares)):
        pairs = [(i, i ^ m) for i in range(shares)]
        pieces.append(lax.ppermute(sent[m - 1], "ev", pairs))
    mid, after = call(
        functools.partial(second_kernel, events),
        [flat, flat],
        [pltpu.VMEM] * 8,
        name="second",
    )(now, med, cells, force, tall_medium, coef, then, edge)
    shear, density = call(
        functools.partial(finish_kernel, shares, 1.0 / (events * shares)),
        [((tile, depth // shares), F32)] * 2,
        [pltpu.VMEM] * shares,
        name="finish",
    )(*pieces)
    shape = adjoint_now.shape
    grad = (width_x, width_y, depth // shares)
    return mid.reshape(shape), after.reshape(shape), shear.reshape(grad), density.reshape(grad)


def solution(mesh):
    in_specs = (
        P("ev", None, "gx", "gy", None),
        P("ev", None, "gx", "gy", None),
        P("ev", None, None, "gx", "gy", None),
        P(None, "gx", "gy", None),
        P("gx", "gy", None),
        P("ev", None, None, "gx", "gy", None),
    )
    out_specs = (
        P("ev", None, "gx", "gy", None),
        P("ev", None, "gx", "gy", None),
        P("gx", "gy", "ev"),
        P("gx", "gy", "ev"),
    )
    return jax.shard_map(body, mesh=mesh, in_specs=in_specs, out_specs=out_specs, check_vma=False)
```

```python
import functools
import itertools

import jax
import jax.numpy as jnp
from jax import lax
from jax.experimental import pallas as pl
from jax.experimental.pallas import tpu as pltpu
from jax.sharding import PartitionSpec as P

STEP_FACTOR = 0.01
F32, BF16 = jnp.float32, jnp.bfloat16
SHEAR, LAME, BUOY, INV = range(4)
ROWS = 16
VMEM_LIMIT = 40 * 1024 * 1024


def rounds_of(count):
    return "AB"[: max(0, min(2, count - 1))]


def swap(values, rounds, first_along_x=False, first_idle=False):
    names = ("ev", "gx", "gy")
    sizes = [lax.axis_size(a) for a in names]
    pairs = []
    for source in itertools.product(*map(range, sizes)):
        target = list(source)
        steps = {"gx": "A"}.items() if first_along_x and source[2] == 0 else rounds.items()
        for axis, name in steps:
            along = names.index(axis)
            target[along] += 1 if (source[along] % 2 == 0) == (name == "A") else -1
        idle = first_idle and source[2] == 0
        if idle or not all(0 <= t < size for t, size in zip(target, sizes)):
            target = [source[0] ^ 1, *source[1:]]
        flat = [(s[0] * sizes[1] + s[1]) * sizes[2] + s[2] for s in (source, target)]
        pairs.append(tuple(flat))
    return lax.ppermute(values, names, pairs)


def their_turn(x_rounds, y_rounds):
    return bool(x_rounds) and "B" in y_rounds


def is_first():
    return lax.axis_index("gy") == 0


def linked(axis, name):
    other = lax.axis_index(axis) + jnp.where(upward(axis, name), 1, -1)
    return jnp.logical_and(other >= 0, other < lax.axis_size(axis))


def upward(axis, name):
    even = lax.rem(lax.axis_index(axis), 2) == 0
    return even if name == "A" else jnp.logical_not(even)


def padded(count):
    return -(-count // 8) * 8


def face_parts(fields):
    parts = []
    for f in range(fields):
        for kind in ("field", "base"):
            parts += [(kind, f, 1, False)] + [(kind, f, 1, True)]
    parts += [("field", f, 2, False) for f in range(fields)]
    parts += [("wave", k, 1, False) for k in range(2 * fields)]
    for m in (SHEAR, LAME, INV):
        parts += [("medium", m, 1, False), ("medium", m, 2, False)]
    parts.append(("medium", BUOY, 1, False))
    return parts


def corner_layout(fields):
    layout, at = [], 0
    for ring_x in (1, 2):
        for ring_y in (1, 2):
            layout.append(("field", ring_x, ring_y, at))
            at += fields
            if ring_x == 1 and ring_y == 1:
                layout.append(("base", ring_x, ring_y, at))
                at += fields
            layout.append(("medium", ring_x, ring_y, at))
            at += 4
    return layout, -(-at // 16) * 16, -(-at // 16) * 16 + padded(fields) + 8


def take_corner(fields, corner, real, spread, put):
    layout, rows, _ = corner_layout(fields)
    if corner is not None:
        spread[pl.ds(0, rows), :] = jnp.where(real, corner[...].astype(F32), 0.0)
    for kind, ring_x, ring_y, first in layout:
        count = 8 if kind == "medium" else padded(fields)
        values = jnp.zeros((count, 128), F32)
        if corner is not None:
            values = spread[pl.ds(first, count), :]
        put(kind, ring_x, ring_y, values)


def force_field(cells, force_rows, width):
    depth = 128
    count = cells.shape[1]
    place = lax.broadcasted_iota(jnp.int32, (width, count), 0)
    mask = place == cells // depth
    level = lax.broadcasted_iota(jnp.int32, (depth, count), 0)
    hot = jnp.where(level == lax.rem(cells, depth), 1.0, 0.0).astype(BF16)
    left = jnp.concatenate([jnp.where(mask, row, 0.0) for row in force_rows], axis=0)
    total = None
    for _ in range(3):
        part = left.astype(BF16)
        left = left - part.astype(F32)
        term = lax.dot_general(part, hot, (((1,), (1,)), ((), ())), preferred_element_type=F32)
        total = term if total is None else total + term
    return total


def pack_kernel(events, x_rounds, y_rounds, *refs):
    fields = 3 * events
    now_in, prev_in, fwd_in, med_in, cells_in, force_in = refs[:6]
    now, fwd, med, cells, force, base = refs[6:12]
    messages, (prev, stored, spread, arrived) = refs[12:-4], refs[-4:]
    pairs = [(cells_in, cells), (force_in, force), (now_in, now), (prev_in, prev), (med_in, med)]
    for first, count in ((3, 6), (0, 3), (9, 3)):
        part = pl.ds(first, count)
        pairs.append((fwd_in.at[:, part], fwd.at[:, part]))
    copies = []
    for k, (source, target) in enumerate(pairs):
        if target.shape != source.shape:
            target = target.at[pl.ds(0, source.shape[0])]
        copies.append(pltpu.make_async_copy(source, target, arrived.at[k]))
    for copy in copies:
        copy.start()
    for copy in copies[:2]:
        copy.wait()
    rows = [force[e, 0, c, 0] for e in range(events) for c in range(3)]
    pushed = force_field(cells[0], rows, 64)
    for copy in copies[2:5]:
        copy.wait()
    scale = STEP_FACTOR * med[pl.ds(BUOY * 64, 64), :]
    for f in range(fields):
        spot = pl.ds(f * 64, 64)
        base[spot, :] = 2.0 * now[spot, :] - prev[spot, :] + scale * pushed[f * 64 : (f + 1) * 64]

    sources = {"field": now, "base": base, "wave": stored, "medium": med}

    parts = face_parts(fields)
    parts += parts[-1:] * (len(parts) % 2)

    def fill(message, pick, waves):
        for k in range(0, len(parts), 2):
            if waves != any(kind == "wave" for kind, *_ in parts[k : k + 2]):
                continue
            halves = []
            for kind, index, ring, remainder in parts[k : k + 2]:
                value = pick(sources[kind], index, ring)
                halves.append(value - value.astype(BF16).astype(F32) if remainder else value)
            message[k // 2] = jnp.concatenate(halves, axis=0).astype(BF16)

    def face(axis, name, ring):
        return jnp.where(upward(axis, name), 8 - ring, ring - 1)

    def pick_x(name):
        def pick(ref, index, ring):
            row = pl.multiple_of(face("gx", name, ring) * 8, 8)
            return ref[pl.ds(index * 64 + row, 8), :]

        return pick

    def pick_y(name):
        def pick(ref, index, ring):
            return ref[pl.ds(index * 64 + face("gy", name, ring), 8, stride=8), :]

        return pick

    def fill_faces(waves):
        for message, name in zip(messages, y_rounds):
            if name == "B" and their_turn(x_rounds, y_rounds):
                pl.when(is_first())(functools.partial(fill, message, pick_x("A"), waves))
                other = functools.partial(fill, message, pick_y(name), waves)
                pl.when(jnp.logical_not(is_first()))(other)
            else:
                fill(message, pick_y(name), waves)
        for message, name in zip(messages[len(y_rounds) :], x_rounds):
            fill(message, pick_x(name), waves)

    fill_faces(False)
    corners = iter(messages[len(y_rounds) + len(x_rounds) :])
    for name_x in x_rounds:
        for name_y in y_rounds:
            message = next(corners)
            layout, rows, _ = corner_layout(fields)
            for kind, ring_x, ring_y, first in layout:
                cell = face("gx", name_x, ring_x) * 8 + face("gy", name_y, ring_y)
                count = 8 if kind == "medium" else padded(fields)
                spread[pl.ds(first, count), :] = sources[kind][pl.ds(cell, count, stride=64), :]
            message[...] = spread[pl.ds(0, rows), :].astype(BF16)
    copies[5].wait()
    for f in range(fields):
        e, c = f // 3, f % 3
        for t in range(2):
            part = fwd[e, (t + 1) * 3 + c].astype(F32).reshape(64, 128)
            stored[pl.ds((f * 2 + t) * 64, 64), :] = part
    fill_faces(True)
    for copy in copies[6:]:
        copy.wait()


def masked(message, axis, name):
    if name == "A" and lax.axis_size(axis) % 2 == 0:
        return lambda index: message[index]
    real = linked(axis, name)
    return lambda index: jnp.where(real, message[index].astype(F32), 0.0).astype(BF16)


def shift_z(values, step):
    depth = values.shape[-1]
    lane = lax.broadcasted_iota(jnp.int32, values.shape, values.ndim - 1)
    moved = pltpu.roll(values, (-step) % depth, axis=values.ndim - 1)
    return jnp.where(lane == (depth - 1 if step > 0 else 0), 0.0, moved)


def shift_y(values, step):
    return pltpu.roll(values, (-step) % ROWS, axis=0)


def row_of(ref, index, row):
    return ref[index, pl.ds(row * ROWS, ROWS), :]


COEFFICIENTS = (
    ("own_x", "other_x", "own_y", "other_y", "own_z", "other_z", "cross", "cross_z")
    + ("own_y_down", "other_y_down", "own_z_down", "other_z_down")
)


def coefficients(medium, row, ahead=True):
    def both_of(row):
        return medium(LAME, row) + 2.0 * medium(SHEAR, row)

    shear, lame, inverse = (medium(m, row) for m in (SHEAR, LAME, INV))
    both = both_of(row)
    values = {}
    if ahead:
        values["own_x"] = 0.5 * (both + both_of(row + 1))
        values["other_x"] = 0.5 * (shear + medium(SHEAR, row + 1))
    for tail, step in (("", 1), ("_down", -1)):
        values["own_y" + tail] = 0.5 * (both + shift_y(both, step))
        values["other_y" + tail] = 0.5 * (shear + shift_y(shear, step))
        spacing = 0.25 * (inverse + shift_z(inverse, step))
        values["own_z" + tail] = spacing * (both + shift_z(both, step))
        values["other_z" + tail] = spacing * (shear + shift_z(shear, step))
    values["cross"] = 0.25 * (lame + shear)
    values["cross_z"] = values["cross"] * inverse
    return values


class Event:
    def __init__(self, value):
        self.value = functools.cache(value)
        self.y = functools.cache(lambda c, row, step: shift_y(self.value(c, row), step))
        self.z = functools.cache(lambda c, row, step: shift_z(self.value(c, row), step))

    def slopes(self, c, row):
        return (
            (self.value(c, row + 1) - self.value(c, row - 1))[:8],
            (self.y(c, row, 1) - self.y(c, row, -1))[:8],
            (self.z(c, row, 1) - self.z(c, row, -1))[:8],
        )

    def operator(self, faces, sign=None):
        value = self.value

        def signed(values):
            return values if sign is None else sign * values

        @functools.cache
        def slope(d, row):
            if d == 0:
                return signed(faces("cross", row) * (value(0, row + 1) - value(0, row - 1)))
            if d == 1:
                return faces("cross", row) * (self.y(1, row, 1) - self.y(1, row, -1))
            return faces("cross_z", row) * (self.z(2, row, 1) - self.z(2, row, -1))

        @functools.cache
        def flux_x(c, row):
            kind = "own_x" if c == 0 else "other_x"
            return faces(kind, row) * (value(c, row + 1) - value(c, row))

        def apply(row):
            results = []
            for c in range(3):
                here = value(c, row)
                total = flux_x(c, row) - flux_x(c, row - 1)
                kind = "own_y" if c == 1 else "other_y"
                total = total + (
                    faces(kind, row) * (self.y(c, row, 1) - here)
                    - faces(kind + "_down", row) * (here - self.y(c, row, -1))
                )
                kind = "own_z" if c == 2 else "other_z"
                upright = faces(kind, row) * (self.z(c, row, 1) - here) - faces(
                    kind + "_down", row
                ) * (here - self.z(c, row, -1))
                if c == 0:
                    total = total + signed(
                        (slope(1, row + 1) + slope(2, row + 1))
                        - (slope(1, row - 1) + slope(2, row - 1))
                    )
                elif c == 1:
                    mixed = slope(0, row) + slope(2, row)
                    total = total + (shift_y(mixed, 1) - shift_y(mixed, -1))
                else:
                    mixed = slope(0, row) + slope(1, row)
                    upright = upright + (shift_z(mixed, 1) - shift_z(mixed, -1))
                results.append(total + faces("inverse", row) * upright)
            return results

        return apply


def x_row(up, ring):
    return jnp.where(up, 9 + ring, 2 - ring)


def y_place(up, ring):
    return jnp.where(up, 7 + ring, ROWS - ring)


def tile_row(ref, index, row):
    return ref[pl.ds(index * 64 + (row - 2) * 8, 8), :]


def add_to(sums, key, value):
    sums[key] = sums[key] + value if key in sums else value


def inner_kernel(events, x_rounds, y_rounds, now, base, fwd, med, *refs):
    fields = 3 * events
    x_messages, refs = refs[: len(x_rounds)], refs[len(x_rounds) :]
    y_messages, refs = refs[: len(y_rounds)], refs[len(y_rounds) :]
    here, start, stored, medium, coef, then, part = refs[-7:]

    for f in range(fields):
        e, c = f // 3, f % 3
        for x in range(8):
            spot = pl.ds((x + 2) * ROWS, 8)
            here[f, spot, :] = now[pl.ds(f * 64 + x * 8, 8), :]
            start[f, spot, :] = base[pl.ds(f * 64 + x * 8, 8), :]
            for t in range(2):
                stored[2 * f + t, spot, :] = fwd[(e * 4 + t + 1) * 3 + c, x].astype(F32)
    for m in range(4):
        for x in range(8):
            medium[m, pl.ds((x + 2) * ROWS, 8), :] = med[pl.ds(m * 64 + x * 8, 8), :]

    targets = {"field": here, "base": start, "wave": stored, "medium": medium}
    parts = face_parts(fields)

    def place(tile, put):
        whole = functools.cache(lambda k: tile(k).astype(F32))
        for k, (kind, index, ring, remainder) in enumerate(parts):
            if remainder:
                continue
            value = whole(k // 2)[8 * (k % 2) :][:8]
            if parts[k + 1 : k + 2] == [(kind, index, ring, True)]:
                value = value + whole((k + 1) // 2)[8 * ((k + 1) % 2) :][:8]
            put(targets[kind], index, ring, value)

    def nothing(_):
        return jnp.zeros((16, 128), BF16)

    near = one_sided(x_rounds)
    if near:
        zeros = jnp.zeros((ROWS, 128), F32)
        for row in (0, 1, 10, 11):
            spot = pl.ds(row * ROWS, ROWS)
            for f in range(fields):
                here[f, spot, :] = zeros
                start[f, spot, :] = zeros
            for m in range(4):
                medium[m, spot, :] = zeros
        for row in (1, 10):
            for k in range(2 * fields):
                stored[k, pl.ds(row * ROWS, 8), :] = zeros[:8]
    for k, name in enumerate("A" if near else "AB"):
        up = upward("gx", name)

        def put_x(ref, index, ring, values, up=up):
            row = pl.multiple_of(x_row(up, ring) * ROWS, ROWS)
            ref[index, pl.ds(row, 8), :] = values

        if name == "A" and their_turn(x_rounds, y_rounds):
            for message, when in (
                (y_messages[1], is_first()),
                (x_messages[0], jnp.logical_not(is_first())),
            ):
                pl.when(when)(functools.partial(place, masked(message, "gx", name), put_x))
        else:
            place(masked(x_messages[k], "gx", name) if k < len(x_rounds) else nothing, put_x)
    for k, name in enumerate("AB"):
        up = upward("gy", name)

        def put_y(ref, index, ring, values, up=up):
            ref[index, pl.ds(2 * ROWS + y_place(up, ring), 8, stride=ROWS), :] = values

        place(masked(y_messages[k], "gy", name) if k < len(y_rounds) else nothing, put_y)

    for row in range(1, 11):
        values = coefficients(lambda m, r: row_of(medium, m, r), row, row < 10)
        for name, value in values.items():
            coef[COEFFICIENTS.index(name), pl.ds(row * ROWS, ROWS), :] = value

    def faces(name, row):
        if name == "inverse":
            return row_of(medium, INV, row)
        return row_of(coef, COEFFICIENTS.index(name), row)

    sums = {}
    for e in range(events):
        first = Event(lambda c, row, e=e: row_of(here, 3 * e + c, row))
        apply = first.operator(faces)
        waves = [
            Event(lambda c, row, e=e, t=t: row_of(stored, 2 * (3 * e + c) + t, row))
            for t in range(2)
        ]
        for row in range(2, 10):
            if near or 3 <= row <= 8:
                scale = STEP_FACTOR * row_of(medium, BUOY, row)
                for c, result in enumerate(apply(row)):
                    f = 3 * e + c
                    then[f, pl.ds(row * ROWS, ROWS), :] = row_of(start, f, row) + scale * result
            gather(sums, first, waves[0], fwd, e, 0, row)
        second = Event(lambda c, row, e=e: row_of(then, 3 * e + c, row))
        for row in range(4, 8):
            gather(sums, second, waves[1], fwd, e, 1, row)
    for row in range(2, 10):
        inverse = tile_row(med, INV, row)
        shear = sums["lateral", row] + inverse * inverse * sums["upright", row]
        part[pl.ds((row - 2) * 8, 8), :] = -0.25 * shear
        part[pl.ds(64 + (row - 2) * 8, 8), :] = -sums["density", row]
    if near:
        mirror, sums = Mirror(), {}
        for f in range(fields):
            then[f, pl.ds(pl.multiple_of(mirror.row(1) * ROWS, ROWS), ROWS), :] = zeros
        for e in range(events):
            second = Event(lambda c, row, e=e: mirror.of(then, 3 * e + c, row))
            wave = Event(lambda c, row, e=e: mirror.of(stored, 2 * (3 * e + c) + 1, row))
            for row in (2, 3):
                gather(sums, second, wave, fwd, e, 1, row, mirror.row(row) - 2)
        for row in (2, 3):
            mirror.add(part, sums, med, row)


def gather(sums, field, wave, fwd, e, t, row, x=None):
    x = row - 2 if x is None else x
    for c in range(3):
        ax, ay, az = field.slopes(c, row)
        ux, uy, uz = wave.slopes(c, row)
        newer = fwd[(e * 4 + t) * 3 + c, x].astype(F32)
        older = fwd[(e * 4 + t + 2) * 3 + c, x].astype(F32)
        bend = newer - 2.0 * wave.value(c, row)[:8] + older
        add_to(sums, ("lateral", row), ax * ux + ay * uy)
        add_to(sums, ("upright", row), az * uz)
        add_to(sums, ("density", row), field.value(c, row)[:8] * bend)


def one_sided(x_rounds):
    return x_rounds == "A" and lax.axis_size("gx") == 2


class Mirror:
    def __init__(self):
        self.up = upward("gx", "A")
        self.sign = jnp.where(self.up, 1.0, -1.0)
        self.row = functools.cache(lambda r: jnp.where(self.up, r, 11 - r))

    def of(self, ref, index, row):
        start = pl.multiple_of(self.row(row) * ROWS, ROWS)
        return ref[index, pl.ds(start, ROWS), :]

    def tile(self, index, row):
        return pl.ds(pl.multiple_of(index * 64 + (self.row(row) - 2) * 8, 8), 8)

    def add(self, part, sums, med, row):
        inverse = med[self.tile(INV, row), :]
        more = sums["lateral", row] + inverse * inverse * sums["upright", row]
        for index, value in ((0, -0.25 * more), (1, -sums["density", row])):
            spot = self.tile(index, row)
            part[spot, :] = part[spot, :] + value


OUTER = (0, 1, 10, 11)
EDGES = (1, 2, 9, 10)


def edge_kernel(events, x_rounds, y_rounds, shares, *refs):
    fields = 3 * events
    count = len(x_rounds) * len(y_rounds)
    corners, refs = refs[:count], refs[count:]
    (here, start, stored, medium, coef, then, part, fwd, med), refs = refs[:9], refs[9:]
    edge, own_share, *sent = refs[: 1 + shares]
    outer, outer_start, outer_medium, outer_coef, spread, slabs = refs[1 + shares :]

    height = len(OUTER) * ROWS
    for k, row in enumerate(OUTER):
        for f in range(fields):
            spot = pl.ds(f * height + k * ROWS, ROWS)
            outer[spot, :] = row_of(here, f, row)
            if row in EDGES:
                outer_start[spot, :] = row_of(start, f, row)
        for m in range(4):
            outer_medium[pl.ds(m * height + k * ROWS, ROWS), :] = row_of(medium, m, row)
    for kx, name_x in enumerate("AB"):
        for ky, name_y in enumerate("AB"):
            corner = None
            if kx < len(x_rounds) and ky < len(y_rounds):
                corner = corners[kx * len(y_rounds) + ky]
            up_x, up_y = upward("gx", name_x), upward("gy", name_y)
            real = jnp.logical_and(linked("gx", name_x), linked("gy", name_y))

            def put(kind, ring_x, ring_y, values):
                place = jnp.where(up_x, 1 + ring_x, 2 - ring_x)
                spot = pl.ds(place * ROWS + y_place(up_y, ring_y), values.shape[0], stride=height)
                {"field": outer, "base": outer_start, "medium": outer_medium}[kind][spot, :] = values

            take_corner(fields, corner, real, spread, put)

    def outer_or(ref, full):
        def pick(index, row):
            if row in OUTER:
                return ref[pl.ds(index * height + OUTER.index(row) * ROWS, ROWS), :]
            return row_of(full, index, row)

        return pick

    field_row, start_row = outer_or(outer, here), outer_or(outer_start, start)
    medium_row = outer_or(outer_medium, medium)
    fresh = (0, 1, 9, 10, 11)
    for k, row in enumerate(fresh):
        for name, value in coefficients(medium_row, row, row < 11).items():
            outer_coef[COEFFICIENTS.index(name), pl.ds(k * ROWS, ROWS), :] = value

    def faces(name, row):
        if name == "inverse":
            return medium_row(INV, row)
        index = COEFFICIENTS.index(name)
        if row in fresh:
            return row_of(outer_coef, index, fresh.index(row))
        return row_of(coef, index, row)

    def then_row(f, row):
        if row in EDGES:
            return row_of(edge, f, EDGES.index(row))
        return row_of(then, f, row)

    sums = {}
    for e in range(events):
        apply = Event(lambda c, row, e=e: field_row(3 * e + c, row)).operator(faces)
        for k, row in enumerate(EDGES):
            scale = STEP_FACTOR * medium_row(BUOY, row)
            for c, result in enumerate(apply(row)):
                f = 3 * e + c
                edge[f, pl.ds(k * ROWS, ROWS), :] = start_row(f, row) + scale * result
        second = Event(lambda c, row, e=e: then_row(3 * e + c, row))
        wave = Event(lambda c, row, e=e: row_of(stored, 2 * (3 * e + c) + 1, row))
        for row in (2, 3, 8, 9):
            gather(sums, second, wave, fwd, e, 1, row)
    grads = [[], []]
    for row in range(2, 10):
        shear, density = tile_row(part, 0, row), tile_row(part, 1, row)
        if row in (2, 3, 8, 9):
            inverse = tile_row(med, INV, row)
            more = sums["lateral", row] + inverse * inverse * sums["upright", row]
            shear = shear - 0.25 * more
            density = density - sums["density", row]
        grads[0].append(shear)
        grads[1].append(density)
    cut(grads[0] + grads[1], shares, slabs, own_share, sent)


def cut(grads, shares, slabs, own_share, sent):
    piece = 128 // shares
    quarter = lax.broadcasted_iota(jnp.int32, (8, 128), 1) // piece
    per = len(grads) // shares
    for j in range(shares):
        for r in range(per):
            tile = None
            for g in range(shares):
                source = grads[r * shares + g]
                moved = pltpu.roll(source, ((g - j) * piece) % 128, axis=1) if g != j else source
                tile = moved if tile is None else jnp.where(quarter == g, moved, tile)
            slabs[j, pl.ds(r * 8, 8), :] = tile
    me = lax.axis_index("ev")
    own_share[...] = slabs[me]
    for m in range(1, shares):
        sent[m - 1][...] = slabs[me ^ m]


def near_kernel(events, x_rounds, y_rounds, shares, *refs):
    fields = 3 * events
    corners, refs = refs[: len(y_rounds)], refs[len(y_rounds) :]
    (here, start, stored, medium, coef, then, part, fwd, med), refs = refs[:9], refs[9:]
    edge, own_share, *sent = refs[: 1 + shares]
    outer, outer_start, outer_medium, outer_coef, spread, total, slabs = refs[1 + shares :]
    mirror = Mirror()

    height = 2 * ROWS
    for f in range(fields):
        outer_start[pl.ds(f * ROWS, ROWS), :] = mirror.of(start, f, 10)
    for k, row in enumerate((10, 11)):
        for f in range(fields):
            outer[pl.ds(f * height + k * ROWS, ROWS), :] = mirror.of(here, f, row)
        for m in range(4):
            outer_medium[pl.ds(m * height + k * ROWS, ROWS), :] = mirror.of(medium, m, row)
    for corner, name in zip(corners, y_rounds):
        up_y, real = upward("gy", name), linked("gy", name)

        def put(kind, ring_x, ring_y, values):
            place = y_place(up_y, ring_y)
            count = values.shape[0]
            if kind == "base":
                outer_start[pl.ds(place, count, stride=ROWS), :] = values
            else:
                target = outer if kind == "field" else outer_medium
                target[pl.ds((ring_x - 1) * ROWS + place, count, stride=height), :] = values

        take_corner(fields, corner, real, spread, put)

    def row_with(ref, full):
        def pick(index, row):
            if row >= 10:
                return ref[pl.ds(index * height + (row - 10) * ROWS, ROWS), :]
            return mirror.of(full, index, row)

        return pick

    field_row, medium_row = row_with(outer, here), row_with(outer_medium, medium)
    for k, row in enumerate((9, 10, 11)):
        for name, value in coefficients(medium_row, row, row < 11).items():
            if row > 9 or name in ("own_x", "other_x"):
                outer_coef[COEFFICIENTS.index(name), pl.ds(k * ROWS, ROWS), :] = value

    def faces(name, row):
        if name == "inverse":
            return medium_row(INV, row)
        index = COEFFICIENTS.index(name)
        along_x = name in ("own_x", "other_x")
        if row >= (9 if along_x else 10):
            return row_of(outer_coef, index, row - 9)
        first = jnp.where(mirror.up, row, 10 - row) if along_x else mirror.row(row)
        return coef[index, pl.ds(pl.multiple_of(first * ROWS, ROWS), ROWS), :]

    def slot(row):
        up, down = EDGES.index(row), EDGES.index(11 - row)
        return pl.ds(pl.multiple_of(jnp.where(mirror.up, up, down) * ROWS, ROWS), ROWS)

    def then_row(f, row):
        return edge[f, slot(row), :] if row > 8 else mirror.of(then, f, row)

    sums = {}
    for e in range(events):
        apply = Event(lambda c, row, e=e: field_row(3 * e + c, row)).operator(faces, mirror.sign)
        for row in (9, 10):
            scale = STEP_FACTOR * medium_row(BUOY, row)
            for c, result in enumerate(apply(row)):
                f = 3 * e + c
                first = outer_start[pl.ds(f * ROWS, ROWS), :] if row == 10 else mirror.of(start, f, 9)
                edge[f, slot(row), :] = first + scale * result
                edge[f, slot(11 - row), :] = mirror.of(then, f, 11 - row)
        second = Event(lambda c, row, e=e: then_row(3 * e + c, row))
        wave = Event(lambda c, row, e=e: mirror.of(stored, 2 * (3 * e + c) + 1, row))
        for row in (8, 9):
            gather(sums, second, wave, fwd, e, 1, row, mirror.row(row) - 2)
    total[...] = part[...]
    for row in (8, 9):
        mirror.add(total, sums, med, row)
    grads = [total[pl.ds(8 * k, 8), :] for k in range(16)]
    cut(grads, shares, slabs, own_share, sent)


def second_kernel(events, now, med, cells, force, medium, coef, then, edge, mid, after):
    rows = [force[e, 1, c, 0] for e in range(events) for c in range(3)]
    pushed = force_field(cells[0], rows, 64)

    def faces(name, row):
        if name == "inverse":
            return row_of(medium, INV, row)
        return row_of(coef, COEFFICIENTS.index(name), row)

    def then_row(f, row):
        if row in EDGES:
            return row_of(edge, f, EDGES.index(row))
        return row_of(then, f, row)

    for e in range(events):
        apply = Event(lambda c, row, e=e: then_row(3 * e + c, row)).operator(faces)
        for row in range(2, 10):
            scale = STEP_FACTOR * tile_row(med, BUOY, row)
            for c, result in enumerate(apply(row)):
                f = 3 * e + c
                first = f * 64 + (row - 2) * 8
                spot = pl.ds(first, 8)
                current = then_row(f, row)[:8]
                mid[spot, :] = current
                after[spot, :] = (
                    2.0 * current - now[spot, :] + scale * (result[:8] + pushed[first : first + 8])
                )


def finish_kernel(shares, scale, *refs):
    pieces, (shear, density) = refs[:shares], refs[shares:]
    total = pieces[0][...]
    for piece in pieces[1:]:
        total = total + piece[...]
    width = 128 // shares
    for v in range(16):
        g, r = v % shares, v // shares
        tile = total[r * 8 : (r + 1) * 8]
        if g:
            tile = pltpu.roll(tile, (-g * width) % 128, axis=1)
        out = shear if v < 8 else density
        out[pl.ds((v % 8) * 8, 8), :] = tile[:, :width] * scale


def call(kernel, outs, ins, scratch=(), name=None, cost=1000, out_memory=pltpu.VMEM, pinned=False):
    return pl.pallas_call(
        kernel,
        out_shape=[pltpu.VMEM(s, d) if pinned else jax.ShapeDtypeStruct(s, d) for s, d in outs],
        in_specs=[pl.BlockSpec(memory_space=m) for m in ins],
        out_specs=[pl.BlockSpec(memory_space=out_memory)] * len(outs),
        scratch_shapes=[s if not isinstance(s, tuple) else pltpu.VMEM(*s) for s in scratch],
        compiler_params=pltpu.CompilerParams(vmem_limit_bytes=VMEM_LIMIT),
        cost_estimate=pl.CostEstimate(
            flops=cost * 1024, bytes_accessed=cost * 1024, transcendentals=0
        ),
        name=name,
    )


def wait_for(before, messages):
    arrays = [*before, *messages]
    return call(
        lambda *refs: None,
        [((8, 128), F32)],
        [pl.ANY] * len(arrays),
        name="arrival",
        out_memory=pl.ANY,
        cost=8000,
    )(*arrays)


def body(adjoint_now, adjoint_prev, forward, medium, drm_cells, drm_force):
    events, _, width_x, width_y, depth = adjoint_now.shape
    fields = 3 * events
    tile = width_x * width_y
    shares = lax.axis_size("ev")
    x_rounds, y_rounds = rounds_of(lax.axis_size("gx")), rounds_of(lax.axis_size("gy"))
    flat = ((fields * tile, depth), F32)
    tall = 12 * ROWS

    face = (((len(face_parts(fields)) + 1) // 2, 16, depth), BF16)
    wide_fields = padded(fields)
    _, corner_rows, spread_rows = corner_layout(fields)
    corner, spread = ((corner_rows, depth), BF16), ((spread_rows, depth), F32)
    roomy = (((wide_fields + 1) * tile, depth), F32)
    inputs = [
        adjoint_now.reshape(flat[0]),
        adjoint_prev.reshape(flat[0]),
        forward.reshape(events, 12, width_x, width_y, depth),
        medium.reshape(4 * tile, depth),
        drm_cells,
        drm_force,
    ]
    now, fwd, med, cells, force, base, *messages = call(
        functools.partial(pack_kernel, events, x_rounds, y_rounds),
        [roomy, (inputs[2].shape, BF16), ((9 * tile, depth), F32)]
        + [(a.shape, a.dtype) for a in inputs[4:]]
        + [roomy]
        + [face] * (len(y_rounds) + len(x_rounds))
        + [corner] * (len(x_rounds) * len(y_rounds)),
        [pltpu.HBM] * len(inputs),
        [
            flat,
            (((2 * fields + 1) * tile, depth), F32),
            spread,
            pltpu.SemaphoreType.DMA((8,)),
        ],
        "pack",
        cost=8000,
        pinned=True,
    )(*(pltpu.with_memory_space_constraint(a, pltpu.HBM) for a in inputs))
    kinds = [{"gy": r} for r in y_rounds] + [{"gx": r} for r in x_rounds]
    kinds += [{"gx": x, "gy": y} for x in x_rounds for y in y_rounds]
    fwd = fwd.reshape(events * 12, width_x, width_y, depth)
    turn = their_turn(x_rounds, y_rounds)
    received = [
        swap(message, kind, turn and kind == {"gy": "B"}, turn and kind == {"gx": "A"})
        for message, kind in zip(messages, kinds)
    ]
    y_messages, rest = received[: len(y_rounds)], received[len(y_rounds) :]
    x_messages, corners = rest[: len(x_rounds)], rest[len(x_rounds) :]
    order = [y_messages[1], y_messages[0]] if turn else [*x_messages[:1], *y_messages[:1]]
    arrival = ()
    for message in order:
        arrival = wait_for(arrival, [message])

    wide = ((fields, tall, depth), F32)
    here, start, stored, tall_medium, coef, then, part = call(
        functools.partial(inner_kernel, events, x_rounds, y_rounds),
        [
            wide,
            wide,
            ((2 * fields, tall, depth), F32),
            ((4, tall, depth), F32),
            ((len(COEFFICIENTS), tall, depth), F32),
            wide,
            ((2 * tile, depth), F32),
        ],
        [pltpu.VMEM] * (4 + len(x_messages) + len(y_messages)) + [pl.ANY] * len(arrival),
        name="inner",
        cost=3000,
    )(now, base, fwd, med, *x_messages, *y_messages, *arrival)
    slab = ((16 // shares * 8, depth), F32)
    outer = ((fields, len(OUTER) * ROWS, depth), F32)
    if one_sided(x_rounds):
        edge_step, each, fresh, more = near_kernel, (2, 1, 2), 3, [((2 * tile, depth), F32)]
    else:
        edge_step, each, fresh, more = edge_kernel, (len(OUTER),) * 3, 5, []
    room = [wide_fields + 1, wide_fields + 1, 9]
    edge, own_share, *sent = call(
        functools.partial(edge_step, events, x_rounds, y_rounds, shares),
        [outer] + [slab] * shares,
        [pltpu.VMEM] * (9 + len(corners)),
        [
            *(((count * rows * ROWS, depth), F32) for count, rows in zip(room, each)),
            ((len(COEFFICIENTS), fresh * ROWS, depth), F32),
            spread,
            *more,
            ((shares,) + slab[0], F32),
        ],
        "edges",
    )(*corners, here, start, stored, tall_medium, coef, then, part, fwd, med)
    pieces = [own_share]
    for m in reversed(range(1, shares)):
        pairs = [(i, i ^ m) for i in range(shares)]
        pieces.append(lax.ppermute(sent[m - 1], "ev", pairs))
    mid, after = call(
        functools.partial(second_kernel, events),
        [flat, flat],
        [pltpu.VMEM] * 8,
        name="second",
    )(now, med, cells, force, tall_medium, coef, then, edge)
    shear, density = call(
        functools.partial(finish_kernel, shares, 1.0 / (events * shares)),
        [((tile, depth // shares), F32)] * 2,
        [pltpu.VMEM] * shares,
        name="finish",
    )(*pieces)
    shape = adjoint_now.shape
    grad = (width_x, width_y, depth // shares)
    return mid.reshape(shape), after.reshape(shape), shear.reshape(grad), density.reshape(grad)


def solution(mesh):
    in_specs = (
        P("ev", None, "gx", "gy", None),
        P("ev", None, "gx", "gy", None),
        P("ev", None, None, "gx", "gy", None),
        P(None, "gx", "gy", None),
        P("gx", "gy", None),
        P("ev", None, None, "gx", "gy", None),
    )
    out_specs = (
        P("ev", None, "gx", "gy", None),
        P("ev", None, "gx", "gy", None),
        P("gx", "gy", "ev"),
        P("gx", "gy", "ev"),
    )
    return jax.shard_map(body, mesh=mesh, in_specs=in_specs, out_specs=out_specs, check_vma=False)
```

```python
import functools
import itertools

import jax
import jax.numpy as jnp
from jax import lax
from jax.experimental import pallas as pl
from jax.experimental.pallas import tpu as pltpu
from jax.sharding import PartitionSpec as P

STEP_FACTOR = 0.01
F32, BF16 = jnp.float32, jnp.bfloat16
SHEAR, LAME, BUOY, INV = range(4)
ROWS = 16
VMEM_LIMIT = 40 * 1024 * 1024


def rounds_of(count):
    return "AB"[: max(0, min(2, count - 1))]


def swap(values, rounds, first_along_x=False, first_idle=False):
    names = ("ev", "gx", "gy")
    sizes = [lax.axis_size(a) for a in names]
    pairs = []
    for source in itertools.product(*map(range, sizes)):
        target = list(source)
        steps = {"gx": "A"}.items() if first_along_x and source[2] == 0 else rounds.items()
        for axis, name in steps:
            along = names.index(axis)
            target[along] += 1 if (source[along] % 2 == 0) == (name == "A") else -1
        idle = first_idle and source[2] == 0
        if idle or not all(0 <= t < size for t, size in zip(target, sizes)):
            target = [source[0] ^ 1, *source[1:]]
        flat = [(s[0] * sizes[1] + s[1]) * sizes[2] + s[2] for s in (source, target)]
        pairs.append(tuple(flat))
    return lax.ppermute(values, names, pairs)


def their_turn(x_rounds, y_rounds):
    return bool(x_rounds) and "B" in y_rounds


def is_first():
    return lax.axis_index("gy") == 0


def linked(axis, name):
    other = lax.axis_index(axis) + jnp.where(upward(axis, name), 1, -1)
    return jnp.logical_and(other >= 0, other < lax.axis_size(axis))


def upward(axis, name):
    even = lax.rem(lax.axis_index(axis), 2) == 0
    return even if name == "A" else jnp.logical_not(even)


def padded(count):
    return -(-count // 8) * 8


def face_parts(fields):
    parts = []
    for f in range(fields):
        for kind in ("field", "base"):
            parts += [(kind, f, 1, False)] + [(kind, f, 1, True)]
    parts += [("field", f, 2, False) for f in range(fields)]
    parts += [("wave", k, 1, False) for k in range(2 * fields)]
    for m in (SHEAR, LAME, INV):
        parts += [("medium", m, 1, False), ("medium", m, 2, False)]
    parts.append(("medium", BUOY, 1, False))
    return parts


def corner_layout(fields):
    layout, at = [], 0
    for ring_x in (1, 2):
        for ring_y in (1, 2):
            layout.append(("field", ring_x, ring_y, at))
            at += fields
            if ring_x == 1 and ring_y == 1:
                layout.append(("base", ring_x, ring_y, at))
                at += fields
            layout.append(("medium", ring_x, ring_y, at))
            at += 4
    return layout, -(-at // 16) * 16, -(-at // 16) * 16 + padded(fields) + 8


def take_corner(fields, corner, real, spread, put):
    layout, rows, _ = corner_layout(fields)
    if corner is not None:
        spread[pl.ds(0, rows), :] = jnp.where(real, corner[...].astype(F32), 0.0)
    for kind, ring_x, ring_y, first in layout:
        count = 8 if kind == "medium" else padded(fields)
        values = jnp.zeros((count, 128), F32)
        if corner is not None:
            values = spread[pl.ds(first, count), :]
        put(kind, ring_x, ring_y, values)


def force_field(cells, force_rows, width):
    depth = 128
    count = cells.shape[1]
    place = lax.broadcasted_iota(jnp.int32, (width, count), 0)
    mask = place == cells // depth
    level = lax.broadcasted_iota(jnp.int32, (depth, count), 0)
    hot = jnp.where(level == lax.rem(cells, depth), 1.0, 0.0).astype(BF16)
    left = jnp.concatenate([jnp.where(mask, row, 0.0) for row in force_rows], axis=0)
    total = None
    for _ in range(3):
        part = left.astype(BF16)
        left = left - part.astype(F32)
        term = lax.dot_general(part, hot, (((1,), (1,)), ((), ())), preferred_element_type=F32)
        total = term if total is None else total + term
    return total


def pack_kernel(events, x_rounds, y_rounds, *refs):
    fields = 3 * events
    now_in, prev_in, fwd_in, med_in, cells_in, force_in = refs[:6]
    now, fwd, med, cells, force, base = refs[6:12]
    messages, (prev, stored, spread, arrived) = refs[12:-4], refs[-4:]
    pairs = [(cells_in, cells), (force_in, force), (now_in, now), (prev_in, prev), (med_in, med)]
    for first, count in ((3, 6), (0, 3), (9, 3)):
        part = pl.ds(first, count)
        pairs.append((fwd_in.at[:, part], fwd.at[:, part]))
    copies = []
    for k, (source, target) in enumerate(pairs):
        if target.shape != source.shape:
            target = target.at[pl.ds(0, source.shape[0])]
        copies.append(pltpu.make_async_copy(source, target, arrived.at[k]))
    for copy in copies:
        copy.start()
    for copy in copies[:2]:
        copy.wait()
    rows = [force[e, 0, c, 0] for e in range(events) for c in range(3)]
    pushed = force_field(cells[0], rows, 64)
    for copy in copies[2:5]:
        copy.wait()
    scale = STEP_FACTOR * med[pl.ds(BUOY * 64, 64), :]
    for f in range(fields):
        spot = pl.ds(f * 64, 64)
        base[spot, :] = 2.0 * now[spot, :] - prev[spot, :] + scale * pushed[f * 64 : (f + 1) * 64]

    sources = {"field": now, "base": base, "wave": stored, "medium": med}

    parts = face_parts(fields)
    parts += parts[-1:] * (len(parts) % 2)

    def fill(message, pick, waves):
        for k in range(0, len(parts), 2):
            if waves != any(kind == "wave" for kind, *_ in parts[k : k + 2]):
                continue
            halves = []
            for kind, index, ring, remainder in parts[k : k + 2]:
                value = pick(sources[kind], index, ring)
                halves.append(value - value.astype(BF16).astype(F32) if remainder else value)
            message[k // 2] = jnp.concatenate(halves, axis=0).astype(BF16)

    def face(axis, name, ring):
        return jnp.where(upward(axis, name), 8 - ring, ring - 1)

    def pick_x(name):
        def pick(ref, index, ring):
            row = pl.multiple_of(face("gx", name, ring) * 8, 8)
            return ref[pl.ds(index * 64 + row, 8), :]

        return pick

    def pick_y(name):
        def pick(ref, index, ring):
            return ref[pl.ds(index * 64 + face("gy", name, ring), 8, stride=8), :]

        return pick

    def fill_faces(waves):
        for message, name in zip(messages, y_rounds):
            if name == "B" and their_turn(x_rounds, y_rounds):
                pl.when(is_first())(functools.partial(fill, message, pick_x("A"), waves))
                other = functools.partial(fill, message, pick_y(name), waves)
                pl.when(jnp.logical_not(is_first()))(other)
            else:
                fill(message, pick_y(name), waves)
        for message, name in zip(messages[len(y_rounds) :], x_rounds):
            fill(message, pick_x(name), waves)

    fill_faces(False)
    corners = iter(messages[len(y_rounds) + len(x_rounds) :])
    for name_x in x_rounds:
        for name_y in y_rounds:
            message = next(corners)
            layout, rows, _ = corner_layout(fields)
            for kind, ring_x, ring_y, first in layout:
                cell = face("gx", name_x, ring_x) * 8 + face("gy", name_y, ring_y)
                count = 8 if kind == "medium" else padded(fields)
                spread[pl.ds(first, count), :] = sources[kind][pl.ds(cell, count, stride=64), :]
            message[...] = spread[pl.ds(0, rows), :].astype(BF16)
    copies[5].wait()
    for f in range(fields):
        e, c = f // 3, f % 3
        for t in range(2):
            part = fwd[e, (t + 1) * 3 + c].astype(F32).reshape(64, 128)
            stored[pl.ds((f * 2 + t) * 64, 64), :] = part
    fill_faces(True)
    for copy in copies[6:]:
        copy.wait()


def masked(message, axis, name):
    if name == "A" and lax.axis_size(axis) % 2 == 0:
        return lambda index: message[index]
    real = linked(axis, name)
    return lambda index: jnp.where(real, message[index].astype(F32), 0.0).astype(BF16)


def shift_z(values, step):
    depth = values.shape[-1]
    lane = lax.broadcasted_iota(jnp.int32, values.shape, values.ndim - 1)
    moved = pltpu.roll(values, (-step) % depth, axis=values.ndim - 1)
    return jnp.where(lane == (depth - 1 if step > 0 else 0), 0.0, moved)


def shift_y(values, step):
    return pltpu.roll(values, (-step) % ROWS, axis=0)


def row_of(ref, index, row):
    return ref[index, pl.ds(row * ROWS, ROWS), :]


COEFFICIENTS = (
    ("own_x", "other_x", "own_y", "other_y", "own_z", "other_z", "cross", "cross_z")
    + ("own_y_down", "other_y_down", "own_z_down", "other_z_down")
)


def coefficients(medium, row, ahead=True):
    def both_of(row):
        return medium(LAME, row) + 2.0 * medium(SHEAR, row)

    shear, lame, inverse = (medium(m, row) for m in (SHEAR, LAME, INV))
    both = both_of(row)
    values = {}
    if ahead:
        values["own_x"] = 0.5 * (both + both_of(row + 1))
        values["other_x"] = 0.5 * (shear + medium(SHEAR, row + 1))
    for tail, step in (("", 1), ("_down", -1)):
        values["own_y" + tail] = 0.5 * (both + shift_y(both, step))
        values["other_y" + tail] = 0.5 * (shear + shift_y(shear, step))
        spacing = 0.25 * (inverse + shift_z(inverse, step))
        values["own_z" + tail] = spacing * (both + shift_z(both, step))
        values["other_z" + tail] = spacing * (shear + shift_z(shear, step))
    values["cross"] = 0.25 * (lame + shear)
    values["cross_z"] = values["cross"] * inverse
    return values


class Event:
    def __init__(self, value):
        self.value = functools.cache(value)
        self.y = functools.cache(lambda c, row, step: shift_y(self.value(c, row), step))
        self.z = functools.cache(lambda c, row, step: shift_z(self.value(c, row), step))

    def slopes(self, c, row):
        return (
            (self.value(c, row + 1) - self.value(c, row - 1))[:8],
            (self.y(c, row, 1) - self.y(c, row, -1))[:8],
            (self.z(c, row, 1) - self.z(c, row, -1))[:8],
        )

    def operator(self, faces, sign=None):
        value = self.value

        def signed(values):
            return values if sign is None else sign * values

        @functools.cache
        def slope(d, row):
            if d == 0:
                return signed(faces("cross", row) * (value(0, row + 1) - value(0, row - 1)))
            if d == 1:
                return faces("cross", row) * (self.y(1, row, 1) - self.y(1, row, -1))
            return faces("cross_z", row) * (self.z(2, row, 1) - self.z(2, row, -1))

        @functools.cache
        def flux_x(c, row):
            kind = "own_x" if c == 0 else "other_x"
            return faces(kind, row) * (value(c, row + 1) - value(c, row))

        def apply(row):
            results = []
            for c in range(3):
                here = value(c, row)
                total = flux_x(c, row) - flux_x(c, row - 1)
                kind = "own_y" if c == 1 else "other_y"
                total = total + (
                    faces(kind, row) * (self.y(c, row, 1) - here)
                    - faces(kind + "_down", row) * (here - self.y(c, row, -1))
                )
                kind = "own_z" if c == 2 else "other_z"
                upright = faces(kind, row) * (self.z(c, row, 1) - here) - faces(
                    kind + "_down", row
                ) * (here - self.z(c, row, -1))
                if c == 0:
                    total = total + signed(
                        (slope(1, row + 1) + slope(2, row + 1))
                        - (slope(1, row - 1) + slope(2, row - 1))
                    )
                elif c == 1:
                    mixed = slope(0, row) + slope(2, row)
                    total = total + (shift_y(mixed, 1) - shift_y(mixed, -1))
                else:
                    mixed = slope(0, row) + slope(1, row)
                    upright = upright + (shift_z(mixed, 1) - shift_z(mixed, -1))
                results.append(total + faces("inverse", row) * upright)
            return results

        return apply


def x_row(up, ring):
    return jnp.where(up, 9 + ring, 2 - ring)


def y_place(up, ring):
    return jnp.where(up, 7 + ring, ROWS - ring)


def tile_row(ref, index, row):
    return ref[pl.ds(index * 64 + (row - 2) * 8, 8), :]


def add_to(sums, key, value):
    sums[key] = sums[key] + value if key in sums else value


def inner_kernel(events, x_rounds, y_rounds, shares, now, base, fwd, med, *refs):
    fields = 3 * events
    x_messages, refs = refs[: len(x_rounds)], refs[len(x_rounds) :]
    y_messages, refs = refs[: len(y_rounds)], refs[len(y_rounds) :]
    near = one_sided(x_rounds)
    if near:
        here, start, medium, coef, then, slabs, slopes, stored, part = refs[-9:]
    else:
        here, start, stored, medium, coef, then, part = refs[-7:]

    for f in range(fields):
        e, c = f // 3, f % 3
        for x in range(8):
            spot = pl.ds((x + 2) * ROWS, 8)
            here[f, spot, :] = now[pl.ds(f * 64 + x * 8, 8), :]
            start[f, spot, :] = base[pl.ds(f * 64 + x * 8, 8), :]
            for t in range(2):
                stored[2 * f + t, spot, :] = fwd[(e * 4 + t + 1) * 3 + c, x].astype(F32)
    for m in range(4):
        for x in range(8):
            medium[m, pl.ds((x + 2) * ROWS, 8), :] = med[pl.ds(m * 64 + x * 8, 8), :]

    targets = {"field": here, "base": start, "wave": stored, "medium": medium}
    parts = face_parts(fields)

    def place(tile, put):
        whole = functools.cache(lambda k: tile(k).astype(F32))
        for k, (kind, index, ring, remainder) in enumerate(parts):
            if remainder:
                continue
            value = whole(k // 2)[8 * (k % 2) :][:8]
            if parts[k + 1 : k + 2] == [(kind, index, ring, True)]:
                value = value + whole((k + 1) // 2)[8 * ((k + 1) % 2) :][:8]
            put(targets[kind], index, ring, value)

    def nothing(_):
        return jnp.zeros((16, 128), BF16)

    if near:
        zeros = jnp.zeros((ROWS, 128), F32)
        for row in (0, 1, 10, 11):
            spot = pl.ds(row * ROWS, ROWS)
            for f in range(fields):
                here[f, spot, :] = zeros
                start[f, spot, :] = zeros
            for m in range(4):
                medium[m, spot, :] = zeros
        for row in (1, 10):
            for k in range(2 * fields):
                stored[k, pl.ds(row * ROWS, 8), :] = zeros[:8]
    for k, name in enumerate("A" if near else "AB"):
        up = upward("gx", name)

        def put_x(ref, index, ring, values, up=up):
            row = pl.multiple_of(x_row(up, ring) * ROWS, ROWS)
            ref[index, pl.ds(row, 8), :] = values

        if name == "A" and their_turn(x_rounds, y_rounds):
            for message, when in (
                (y_messages[1], is_first()),
                (x_messages[0], jnp.logical_not(is_first())),
            ):
                pl.when(when)(functools.partial(place, masked(message, "gx", name), put_x))
        else:
            place(masked(x_messages[k], "gx", name) if k < len(x_rounds) else nothing, put_x)
    for k, name in enumerate("AB"):
        up = upward("gy", name)

        def put_y(ref, index, ring, values, up=up):
            ref[index, pl.ds(2 * ROWS + y_place(up, ring), 8, stride=ROWS), :] = values

        place(masked(y_messages[k], "gy", name) if k < len(y_rounds) else nothing, put_y)

    for row in range(1, 11):
        values = coefficients(lambda m, r: row_of(medium, m, r), row, row < 10)
        for name, value in values.items():
            coef[COEFFICIENTS.index(name), pl.ds(row * ROWS, ROWS), :] = value

    def faces(name, row):
        if name == "inverse":
            return row_of(medium, INV, row)
        return row_of(coef, COEFFICIENTS.index(name), row)

    sums = {}
    for e in range(events):
        first = Event(lambda c, row, e=e: row_of(here, 3 * e + c, row))
        apply = first.operator(faces)
        waves = [
            Event(lambda c, row, e=e, t=t: row_of(stored, 2 * (3 * e + c) + t, row))
            for t in range(2)
        ]
        for row in range(2, 10):
            if near or 3 <= row <= 8:
                scale = STEP_FACTOR * row_of(medium, BUOY, row)
                for c, result in enumerate(apply(row)):
                    f = 3 * e + c
                    then[f, pl.ds(row * ROWS, ROWS), :] = row_of(start, f, row) + scale * result
            gather(sums, first, waves[0], fwd, e, 0, row)
        second = Event(lambda c, row, e=e: row_of(then, 3 * e + c, row))
        for row in range(4, 8):
            gather(sums, second, waves[1], fwd, e, 1, row)
    for row in range(2, 10):
        inverse = tile_row(med, INV, row)
        shear = sums["lateral", row] + inverse * inverse * sums["upright", row]
        part[pl.ds((row - 2) * 8, 8), :] = -0.25 * shear
        part[pl.ds(64 + (row - 2) * 8, 8), :] = -sums["density", row]
    if near:
        mirror, sums = Mirror(), {}
        for f in range(fields):
            then[f, pl.ds(pl.multiple_of(mirror.row(1) * ROWS, ROWS), ROWS), :] = zeros
        for e in range(events):
            second = Event(lambda c, row, e=e: mirror.of(then, 3 * e + c, row))
            wave = Event(lambda c, row, e=e: mirror.of(stored, 2 * (3 * e + c) + 1, row))
            for row in (2, 3):
                gather(sums, second, wave, fwd, e, 1, row, mirror.row(row) - 2)
            for row in (8, 9):
                for c in range(3):
                    terms = (*wave.slopes(c, row), bend_of(wave, fwd, e, 1, c, row, mirror.row(row) - 2))
                    for k, term in enumerate(terms):
                        slopes[slope_place(events, e, c, row, k), :] = term
        for row in (2, 3):
            mirror.add(part, sums, med, row)
        cut([part[pl.ds(8 * k, 8), :] for k in range(16)], shares, slabs)


def bend_of(wave, fwd, e, t, c, row, x):
    newer = fwd[(e * 4 + t) * 3 + c, x].astype(F32)
    older = fwd[(e * 4 + t + 2) * 3 + c, x].astype(F32)
    return newer - 2.0 * wave.value(c, row)[:8] + older


def slope_place(events, e, c, row, k):
    return pl.ds((((row - 8) * events + e) * 3 + c) * 32 + k * 8, 8)


def gather(sums, field, wave, fwd, e, t, row, x=None):
    x = row - 2 if x is None else x
    for c in range(3):
        terms = (*wave.slopes(c, row), bend_of(wave, fwd, e, t, c, row, x))
        gather_terms(sums, field, terms, c, row)


def gather_terms(sums, field, terms, c, row):
    ax, ay, az = field.slopes(c, row)
    ux, uy, uz, bend = terms
    add_to(sums, ("lateral", row), ax * ux + ay * uy)
    add_to(sums, ("upright", row), az * uz)
    add_to(sums, ("density", row), field.value(c, row)[:8] * bend)


def one_sided(x_rounds):
    return x_rounds == "A" and lax.axis_size("gx") == 2


class Mirror:
    def __init__(self):
        self.up = upward("gx", "A")
        self.sign = jnp.where(self.up, 1.0, -1.0)
        self.row = functools.cache(lambda r: jnp.where(self.up, r, 11 - r))

    def of(self, ref, index, row):
        start = pl.multiple_of(self.row(row) * ROWS, ROWS)
        return ref[index, pl.ds(start, ROWS), :]

    def tile(self, index, row):
        return pl.ds(pl.multiple_of(index * 64 + (self.row(row) - 2) * 8, 8), 8)

    def terms(self, sums, med, row):
        inverse = med[self.tile(INV, row), :]
        more = sums["lateral", row] + inverse * inverse * sums["upright", row]
        return -0.25 * more, -sums["density", row]

    def add(self, part, sums, med, row):
        for index, value in enumerate(self.terms(sums, med, row)):
            spot = self.tile(index, row)
            part[spot, :] = part[spot, :] + value


OUTER = (0, 1, 10, 11)
EDGES = (1, 2, 9, 10)


def edge_kernel(events, x_rounds, y_rounds, shares, *refs):
    fields = 3 * events
    count = len(x_rounds) * len(y_rounds)
    corners, refs = refs[:count], refs[count:]
    (here, start, stored, medium, coef, then, part, fwd, med), refs = refs[:9], refs[9:]
    edge, own_share, *sent = refs[: 1 + shares]
    outer, outer_start, outer_medium, outer_coef, spread, slabs = refs[1 + shares :]

    height = len(OUTER) * ROWS
    for k, row in enumerate(OUTER):
        for f in range(fields):
            spot = pl.ds(f * height + k * ROWS, ROWS)
            outer[spot, :] = row_of(here, f, row)
            if row in EDGES:
                outer_start[spot, :] = row_of(start, f, row)
        for m in range(4):
            outer_medium[pl.ds(m * height + k * ROWS, ROWS), :] = row_of(medium, m, row)
    for kx, name_x in enumerate("AB"):
        for ky, name_y in enumerate("AB"):
            corner = None
            if kx < len(x_rounds) and ky < len(y_rounds):
                corner = corners[kx * len(y_rounds) + ky]
            up_x, up_y = upward("gx", name_x), upward("gy", name_y)
            real = jnp.logical_and(linked("gx", name_x), linked("gy", name_y))

            def put(kind, ring_x, ring_y, values):
                place = jnp.where(up_x, 1 + ring_x, 2 - ring_x)
                spot = pl.ds(place * ROWS + y_place(up_y, ring_y), values.shape[0], stride=height)
                {"field": outer, "base": outer_start, "medium": outer_medium}[kind][spot, :] = values

            take_corner(fields, corner, real, spread, put)

    def outer_or(ref, full):
        def pick(index, row):
            if row in OUTER:
                return ref[pl.ds(index * height + OUTER.index(row) * ROWS, ROWS), :]
            return row_of(full, index, row)

        return pick

    field_row, start_row = outer_or(outer, here), outer_or(outer_start, start)
    medium_row = outer_or(outer_medium, medium)
    fresh = (0, 1, 9, 10, 11)
    for k, row in enumerate(fresh):
        for name, value in coefficients(medium_row, row, row < 11).items():
            outer_coef[COEFFICIENTS.index(name), pl.ds(k * ROWS, ROWS), :] = value

    def faces(name, row):
        if name == "inverse":
            return medium_row(INV, row)
        index = COEFFICIENTS.index(name)
        if row in fresh:
            return row_of(outer_coef, index, fresh.index(row))
        return row_of(coef, index, row)

    def then_row(f, row):
        if row in EDGES:
            return row_of(edge, f, EDGES.index(row))
        return row_of(then, f, row)

    sums = {}
    for e in range(events):
        apply = Event(lambda c, row, e=e: field_row(3 * e + c, row)).operator(faces)
        for k, row in enumerate(EDGES):
            scale = STEP_FACTOR * medium_row(BUOY, row)
            for c, result in enumerate(apply(row)):
                f = 3 * e + c
                edge[f, pl.ds(k * ROWS, ROWS), :] = start_row(f, row) + scale * result
        second = Event(lambda c, row, e=e: then_row(3 * e + c, row))
        wave = Event(lambda c, row, e=e: row_of(stored, 2 * (3 * e + c) + 1, row))
        for row in (2, 3, 8, 9):
            gather(sums, second, wave, fwd, e, 1, row)
    grads = [[], []]
    for row in range(2, 10):
        shear, density = tile_row(part, 0, row), tile_row(part, 1, row)
        if row in (2, 3, 8, 9):
            inverse = tile_row(med, INV, row)
            more = sums["lateral", row] + inverse * inverse * sums["upright", row]
            shear = shear - 0.25 * more
            density = density - sums["density", row]
        grads[0].append(shear)
        grads[1].append(density)
    cut(grads[0] + grads[1], shares, slabs)
    deal(shares, slabs, own_share, sent)


def cut(grads, shares, slabs):
    piece = 128 // shares
    quarter = lax.broadcasted_iota(jnp.int32, (8, 128), 1) // piece
    per = len(grads) // shares
    for j in range(shares):
        for r in range(per):
            tile = None
            for g in range(shares):
                source = grads[r * shares + g]
                moved = pltpu.roll(source, ((g - j) * piece) % 128, axis=1) if g != j else source
                tile = moved if tile is None else jnp.where(quarter == g, moved, tile)
            slabs[j, pl.ds(r * 8, 8), :] = tile


def deal(shares, slabs, own_share, sent):
    me = lax.axis_index("ev")
    own_share[...] = slabs[me]
    for m in range(1, shares):
        sent[m - 1][...] = slabs[me ^ m]


def near_kernel(events, x_rounds, y_rounds, shares, *refs):
    fields = 3 * events
    corners, refs = refs[: len(y_rounds)], refs[len(y_rounds) :]
    (here, start, medium, coef, then, ready, slopes, med), refs = refs[:8], refs[8:]
    edge, own_share, *sent = refs[: 1 + shares]
    outer, outer_start, outer_medium, outer_coef, spread, slabs = refs[1 + shares :]
    mirror = Mirror()

    height = 2 * ROWS
    for f in range(fields):
        outer_start[pl.ds(f * ROWS, ROWS), :] = mirror.of(start, f, 10)
    for k, row in enumerate((10, 11)):
        for f in range(fields):
            outer[pl.ds(f * height + k * ROWS, ROWS), :] = mirror.of(here, f, row)
        for m in range(4):
            outer_medium[pl.ds(m * height + k * ROWS, ROWS), :] = mirror.of(medium, m, row)
    for corner, name in zip(corners, y_rounds):
        up_y, real = upward("gy", name), linked("gy", name)

        def put(kind, ring_x, ring_y, values):
            place = y_place(up_y, ring_y)
            count = values.shape[0]
            if kind == "base":
                outer_start[pl.ds(place, count, stride=ROWS), :] = values
            else:
                target = outer if kind == "field" else outer_medium
                target[pl.ds((ring_x - 1) * ROWS + place, count, stride=height), :] = values

        take_corner(fields, corner, real, spread, put)

    def row_with(ref, full):
        def pick(index, row):
            if row >= 10:
                return ref[pl.ds(index * height + (row - 10) * ROWS, ROWS), :]
            return mirror.of(full, index, row)

        return pick

    field_row, medium_row = row_with(outer, here), row_with(outer_medium, medium)
    for k, row in enumerate((9, 10, 11)):
        for name, value in coefficients(medium_row, row, row < 11).items():
            if row > 9 or name in ("own_x", "other_x"):
                outer_coef[COEFFICIENTS.index(name), pl.ds(k * ROWS, ROWS), :] = value

    def faces(name, row):
        if name == "inverse":
            return medium_row(INV, row)
        index = COEFFICIENTS.index(name)
        along_x = name in ("own_x", "other_x")
        if row >= (9 if along_x else 10):
            return row_of(outer_coef, index, row - 9)
        first = jnp.where(mirror.up, row, 10 - row) if along_x else mirror.row(row)
        return coef[index, pl.ds(pl.multiple_of(first * ROWS, ROWS), ROWS), :]

    def slot(row):
        up, down = EDGES.index(row), EDGES.index(11 - row)
        return pl.ds(pl.multiple_of(jnp.where(mirror.up, up, down) * ROWS, ROWS), ROWS)

    def then_row(f, row):
        return edge[f, slot(row), :] if row > 8 else mirror.of(then, f, row)

    sums = {}
    for e in range(events):
        apply = Event(lambda c, row, e=e: field_row(3 * e + c, row)).operator(faces, mirror.sign)
        for row in (9, 10):
            scale = STEP_FACTOR * medium_row(BUOY, row)
            for c, result in enumerate(apply(row)):
                f = 3 * e + c
                first = outer_start[pl.ds(f * ROWS, ROWS), :] if row == 10 else mirror.of(start, f, 9)
                edge[f, slot(row), :] = first + scale * result
                edge[f, slot(11 - row), :] = mirror.of(then, f, 11 - row)
        second = Event(lambda c, row, e=e: then_row(3 * e + c, row))
        for row in (8, 9):
            for c in range(3):
                terms = [slopes[slope_place(events, e, c, row, k), :] for k in range(4)]
                gather_terms(sums, second, terms, c, row)
    piece = 128 // shares
    quarter = lax.broadcasted_iota(jnp.int32, (8, 128), 1) // piece
    slabs[...] = ready[...]
    rows = {row: mirror.terms(sums, med, row) for row in (8, 9)}
    for index in range(2):
        tile = index * (8 // shares) + (mirror.row(9) - 2) // shares
        spot = pl.ds(pl.multiple_of(tile * 8, 8), 8)
        for j in range(shares):
            values = slabs[j, spot, :]
            for row in (8, 9):
                g = lax.rem(mirror.row(row) - 2, shares)
                moved = pltpu.roll(rows[row][index], lax.rem((g - j + shares) * piece, 128), axis=1)
                values = values + jnp.where(quarter == g, moved, 0.0)
            slabs[j, spot, :] = values
    deal(shares, slabs, own_share, sent)


def second_kernel(events, now, med, cells, force, medium, coef, then, edge, mid, after):
    rows = [force[e, 1, c, 0] for e in range(events) for c in range(3)]
    pushed = force_field(cells[0], rows, 64)

    def faces(name, row):
        if name == "inverse":
            return row_of(medium, INV, row)
        return row_of(coef, COEFFICIENTS.index(name), row)

    def then_row(f, row):
        if row in EDGES:
            return row_of(edge, f, EDGES.index(row))
        return row_of(then, f, row)

    for e in range(events):
        apply = Event(lambda c, row, e=e: then_row(3 * e + c, row)).operator(faces)
        for row in range(2, 10):
            scale = STEP_FACTOR * tile_row(med, BUOY, row)
            for c, result in enumerate(apply(row)):
                f = 3 * e + c
                first = f * 64 + (row - 2) * 8
                spot = pl.ds(first, 8)
                current = then_row(f, row)[:8]
                mid[spot, :] = current
                after[spot, :] = (
                    2.0 * current - now[spot, :] + scale * (result[:8] + pushed[first : first + 8])
                )


def finish_kernel(shares, scale, *refs):
    pieces, (shear, density) = refs[:shares], refs[shares:]
    total = pieces[0][...]
    for piece in pieces[1:]:
        total = total + piece[...]
    width = 128 // shares
    for v in range(16):
        g, r = v % shares, v // shares
        tile = total[r * 8 : (r + 1) * 8]
        if g:
            tile = pltpu.roll(tile, (-g * width) % 128, axis=1)
        out = shear if v < 8 else density
        out[pl.ds((v % 8) * 8, 8), :] = tile[:, :width] * scale


def call(kernel, outs, ins, scratch=(), name=None, cost=1000, out_memory=pltpu.VMEM, pinned=False):
    return pl.pallas_call(
        kernel,
        out_shape=[pltpu.VMEM(s, d) if pinned else jax.ShapeDtypeStruct(s, d) for s, d in outs],
        in_specs=[pl.BlockSpec(memory_space=m) for m in ins],
        out_specs=[pl.BlockSpec(memory_space=out_memory)] * len(outs),
        scratch_shapes=[s if not isinstance(s, tuple) else pltpu.VMEM(*s) for s in scratch],
        compiler_params=pltpu.CompilerParams(vmem_limit_bytes=VMEM_LIMIT),
        cost_estimate=pl.CostEstimate(
            flops=cost * 1024, bytes_accessed=cost * 1024, transcendentals=0
        ),
        name=name,
    )


def wait_for(before, messages):
    arrays = [*before, *messages]
    return call(
        lambda *refs: None,
        [((8, 128), F32)],
        [pl.ANY] * len(arrays),
        name="arrival",
        out_memory=pl.ANY,
        cost=8000,
    )(*arrays)


def body(adjoint_now, adjoint_prev, forward, medium, drm_cells, drm_force):
    events, _, width_x, width_y, depth = adjoint_now.shape
    fields = 3 * events
    tile = width_x * width_y
    shares = lax.axis_size("ev")
    x_rounds, y_rounds = rounds_of(lax.axis_size("gx")), rounds_of(lax.axis_size("gy"))
    flat = ((fields * tile, depth), F32)
    tall = 12 * ROWS

    face = (((len(face_parts(fields)) + 1) // 2, 16, depth), BF16)
    wide_fields = padded(fields)
    _, corner_rows, spread_rows = corner_layout(fields)
    corner, spread = ((corner_rows, depth), BF16), ((spread_rows, depth), F32)
    roomy = (((wide_fields + 1) * tile, depth), F32)
    inputs = [
        adjoint_now.reshape(flat[0]),
        adjoint_prev.reshape(flat[0]),
        forward.reshape(events, 12, width_x, width_y, depth),
        medium.reshape(4 * tile, depth),
        drm_cells,
        drm_force,
    ]
    now, fwd, med, cells, force, base, *messages = call(
        functools.partial(pack_kernel, events, x_rounds, y_rounds),
        [roomy, (inputs[2].shape, BF16), ((9 * tile, depth), F32)]
        + [(a.shape, a.dtype) for a in inputs[4:]]
        + [roomy]
        + [face] * (len(y_rounds) + len(x_rounds))
        + [corner] * (len(x_rounds) * len(y_rounds)),
        [pltpu.HBM] * len(inputs),
        [
            flat,
            (((2 * fields + 1) * tile, depth), F32),
            spread,
            pltpu.SemaphoreType.DMA((8,)),
        ],
        "pack",
        cost=8000,
        pinned=True,
    )(*(pltpu.with_memory_space_constraint(a, pltpu.HBM) for a in inputs))
    kinds = [{"gy": r} for r in y_rounds] + [{"gx": r} for r in x_rounds]
    kinds += [{"gx": x, "gy": y} for x in x_rounds for y in y_rounds]
    fwd = fwd.reshape(events * 12, width_x, width_y, depth)
    turn = their_turn(x_rounds, y_rounds)
    received = [
        swap(message, kind, turn and kind == {"gy": "B"}, turn and kind == {"gx": "A"})
        for message, kind in zip(messages, kinds)
    ]
    y_messages, rest = received[: len(y_rounds)], received[len(y_rounds) :]
    x_messages, corners = rest[: len(x_rounds)], rest[len(x_rounds) :]
    order = [y_messages[1], y_messages[0]] if turn else [*x_messages[:1], *y_messages[:1]]
    arrival = ()
    for message in order:
        arrival = wait_for(arrival, [message])

    wide = ((fields, tall, depth), F32)
    slab = ((16 // shares * 8, depth), F32)
    whole, near = ((2 * tile, depth), F32), one_sided(x_rounds)
    waves = ((2 * fields, tall, depth), F32)
    results = call(
        functools.partial(inner_kernel, events, x_rounds, y_rounds, shares),
        [wide, wide]
        + ([] if near else [waves])
        + [((4, tall, depth), F32), ((len(COEFFICIENTS), tall, depth), F32), wide]
        + ([((shares,) + slab[0], F32), ((fields * 64, depth), F32)] if near else [whole]),
        [pltpu.VMEM] * (4 + len(x_messages) + len(y_messages)) + [pl.ANY] * len(arrival),
        [waves, whole] if near else (),
        name="inner",
        cost=3000,
    )(now, base, fwd, med, *x_messages, *y_messages, *arrival)
    outer = ((fields, len(OUTER) * ROWS, depth), F32)
    if near:
        edge_step, each, fresh, operands = near_kernel, (2, 1, 2), 3, [*results, med]
        _, _, tall_medium, coef, then, *_ = results
    else:
        edge_step, each, fresh, operands = edge_kernel, (len(OUTER),) * 3, 5, [*results, fwd, med]
        _, _, _, tall_medium, coef, then, _ = results
    room = [wide_fields + 1, wide_fields + 1, 9]
    edge, own_share, *sent = call(
        functools.partial(edge_step, events, x_rounds, y_rounds, shares),
        [outer] + [slab] * shares,
        [pltpu.VMEM] * (len(operands) + len(corners)),
        [
            *(((count * rows * ROWS, depth), F32) for count, rows in zip(room, each)),
            ((len(COEFFICIENTS), fresh * ROWS, depth), F32),
            spread,
            ((shares,) + slab[0], F32),
        ],
        "edges",
    )(*corners, *operands)
    pieces = [own_share]
    for m in reversed(range(1, shares)):
        pairs = [(i, i ^ m) for i in range(shares)]
        pieces.append(lax.ppermute(sent[m - 1], "ev", pairs))
    mid, after = call(
        functools.partial(second_kernel, events),
        [flat, flat],
        [pltpu.VMEM] * 8,
        name="second",
    )(now, med, cells, force, tall_medium, coef, then, edge)
    shear, density = call(
        functools.partial(finish_kernel, shares, 1.0 / (events * shares)),
        [((tile, depth // shares), F32)] * 2,
        [pltpu.VMEM] * shares,
        name="finish",
    )(*pieces)
    shape = adjoint_now.shape
    grad = (width_x, width_y, depth // shares)
    return mid.reshape(shape), after.reshape(shape), shear.reshape(grad), density.reshape(grad)


def solution(mesh):
    in_specs = (
        P("ev", None, "gx", "gy", None),
        P("ev", None, "gx", "gy", None),
        P("ev", None, None, "gx", "gy", None),
        P(None, "gx", "gy", None),
        P("gx", "gy", None),
        P("ev", None, None, "gx", "gy", None),
    )
    out_specs = (
        P("ev", None, "gx", "gy", None),
        P("ev", None, "gx", "gy", None),
        P("gx", "gy", "ev"),
        P("gx", "gy", "ev"),
    )
    return jax.shard_map(body, mesh=mesh, in_specs=in_specs, out_specs=out_specs, check_vma=False)
```

```python
import functools
import itertools

import jax
import jax.numpy as jnp
from jax import lax
from jax.experimental import pallas as pl
from jax.experimental.pallas import tpu as pltpu
from jax.sharding import PartitionSpec as P

STEP_FACTOR = 0.01
F32, BF16 = jnp.float32, jnp.bfloat16
SHEAR, LAME, BUOY, INV = range(4)
ROWS = 16
VMEM_LIMIT = 40 * 1024 * 1024


def rounds_of(count):
    return "AB"[: max(0, min(2, count - 1))]


def swap(values, rounds, first_along_x=False, first_idle=False):
    names = ("ev", "gx", "gy")
    sizes = [lax.axis_size(a) for a in names]
    pairs = []
    for source in itertools.product(*map(range, sizes)):
        target = list(source)
        steps = {"gx": "A"}.items() if first_along_x and source[2] == 0 else rounds.items()
        for axis, name in steps:
            along = names.index(axis)
            target[along] += 1 if (source[along] % 2 == 0) == (name == "A") else -1
        idle = first_idle and source[2] == 0
        if idle or not all(0 <= t < size for t, size in zip(target, sizes)):
            target = [source[0] ^ 1, *source[1:]]
        flat = [(s[0] * sizes[1] + s[1]) * sizes[2] + s[2] for s in (source, target)]
        pairs.append(tuple(flat))
    return lax.ppermute(values, names, pairs)


def their_turn(x_rounds, y_rounds):
    return bool(x_rounds) and "B" in y_rounds


def is_first():
    return lax.axis_index("gy") == 0


def linked(axis, name):
    other = lax.axis_index(axis) + jnp.where(upward(axis, name), 1, -1)
    return jnp.logical_and(other >= 0, other < lax.axis_size(axis))


def upward(axis, name):
    even = lax.rem(lax.axis_index(axis), 2) == 0
    return even if name == "A" else jnp.logical_not(even)


def padded(count):
    return -(-count // 8) * 8


def face_parts(fields):
    parts = []
    for f in range(fields):
        for kind in ("field", "base"):
            parts += [(kind, f, 1, False)] + [(kind, f, 1, True)]
    parts += [("field", f, 2, False) for f in range(fields)]
    parts += [("wave", k, 1, False) for k in range(2 * fields)]
    for m in (SHEAR, LAME, INV):
        parts += [("medium", m, 1, False), ("medium", m, 2, False)]
    parts.append(("medium", BUOY, 1, False))
    return parts


def corner_layout(fields):
    layout, at = [], 0
    for ring_x in (1, 2):
        for ring_y in (1, 2):
            layout.append(("field", ring_x, ring_y, at))
            at += fields
            if ring_x == 1 and ring_y == 1:
                layout.append(("base", ring_x, ring_y, at))
                at += fields
            layout.append(("medium", ring_x, ring_y, at))
            at += 4
    return layout, -(-at // 16) * 16, -(-at // 16) * 16 + padded(fields) + 8


def take_corner(fields, corner, real, spread, put):
    layout, rows, _ = corner_layout(fields)
    if corner is not None:
        spread[pl.ds(0, rows), :] = jnp.where(real, corner[...].astype(F32), 0.0)
    for kind, ring_x, ring_y, first in layout:
        count = 8 if kind == "medium" else padded(fields)
        values = jnp.zeros((count, 128), F32)
        if corner is not None:
            values = spread[pl.ds(first, count), :]
        put(kind, ring_x, ring_y, values)


def force_field(cells, force_rows, width):
    depth = 128
    count = cells.shape[1]
    place = lax.broadcasted_iota(jnp.int32, (width, count), 0)
    mask = place == cells // depth
    level = lax.broadcasted_iota(jnp.int32, (depth, count), 0)
    hot = jnp.where(level == lax.rem(cells, depth), 1.0, 0.0).astype(BF16)
    left = jnp.concatenate([jnp.where(mask, row, 0.0) for row in force_rows], axis=0)
    total = None
    for _ in range(3):
        part = left.astype(BF16)
        left = left - part.astype(F32)
        term = lax.dot_general(part, hot, (((1,), (1,)), ((), ())), preferred_element_type=F32)
        total = term if total is None else total + term
    return total


def pack_kernel(events, x_rounds, y_rounds, *refs):
    fields = 3 * events
    now_in, prev_in, fwd_in, med_in, cells_in, force_in = refs[:6]
    now, fwd, med, cells, force, base = refs[6:12]
    messages, (prev, stored, spread, arrived) = refs[12:-4], refs[-4:]
    pairs = [(cells_in, cells), (force_in, force), (now_in, now), (prev_in, prev), (med_in, med)]
    for first, count in ((3, 6), (0, 3), (9, 3)):
        part = pl.ds(first, count)
        pairs.append((fwd_in.at[:, part], fwd.at[:, part]))
    copies = []
    for k, (source, target) in enumerate(pairs):
        if target.shape != source.shape:
            target = target.at[pl.ds(0, source.shape[0])]
        copies.append(pltpu.make_async_copy(source, target, arrived.at[k]))
    for copy in copies:
        copy.start()
    for copy in copies[:2]:
        copy.wait()
    rows = [force[e, 0, c, 0] for e in range(events) for c in range(3)]
    pushed = force_field(cells[0], rows, 64)
    for copy in copies[2:5]:
        copy.wait()
    scale = STEP_FACTOR * med[pl.ds(BUOY * 64, 64), :]
    for f in range(fields):
        spot = pl.ds(f * 64, 64)
        base[spot, :] = 2.0 * now[spot, :] - prev[spot, :] + scale * pushed[f * 64 : (f + 1) * 64]

    sources = {"field": now, "base": base, "wave": stored, "medium": med}

    parts = face_parts(fields)
    parts += parts[-1:] * (len(parts) % 2)

    def fill(message, pick, waves):
        for k in range(0, len(parts), 2):
            if waves != any(kind == "wave" for kind, *_ in parts[k : k + 2]):
                continue
            halves = []
            for kind, index, ring, remainder in parts[k : k + 2]:
                value = pick(sources[kind], index, ring)
                halves.append(value - value.astype(BF16).astype(F32) if remainder else value)
            message[k // 2] = jnp.concatenate(halves, axis=0).astype(BF16)

    def face(axis, name, ring):
        return jnp.where(upward(axis, name), 8 - ring, ring - 1)

    def pick_x(name):
        def pick(ref, index, ring):
            row = pl.multiple_of(face("gx", name, ring) * 8, 8)
            return ref[pl.ds(index * 64 + row, 8), :]

        return pick

    def pick_y(name):
        def pick(ref, index, ring):
            return ref[pl.ds(index * 64 + face("gy", name, ring), 8, stride=8), :]

        return pick

    def fill_faces(waves):
        for message, name in zip(messages, y_rounds):
            if name == "B" and their_turn(x_rounds, y_rounds):
                pl.when(is_first())(functools.partial(fill, message, pick_x("A"), waves))
                other = functools.partial(fill, message, pick_y(name), waves)
                pl.when(jnp.logical_not(is_first()))(other)
            else:
                fill(message, pick_y(name), waves)
        for message, name in zip(messages[len(y_rounds) :], x_rounds):
            fill(message, pick_x(name), waves)

    fill_faces(False)
    corners = iter(messages[len(y_rounds) + len(x_rounds) :])
    for name_x in x_rounds:
        for name_y in y_rounds:
            message = next(corners)
            layout, rows, _ = corner_layout(fields)
            for kind, ring_x, ring_y, first in layout:
                cell = face("gx", name_x, ring_x) * 8 + face("gy", name_y, ring_y)
                count = 8 if kind == "medium" else padded(fields)
                spread[pl.ds(first, count), :] = sources[kind][pl.ds(cell, count, stride=64), :]
            message[...] = spread[pl.ds(0, rows), :].astype(BF16)
    copies[5].wait()
    for f in range(fields):
        e, c = f // 3, f % 3
        for t in range(2):
            part = fwd[e, (t + 1) * 3 + c].astype(F32).reshape(64, 128)
            stored[pl.ds((f * 2 + t) * 64, 64), :] = part
    fill_faces(True)
    for copy in copies[6:]:
        copy.wait()


def masked(message, axis, name):
    if name == "A" and lax.axis_size(axis) % 2 == 0:
        return lambda index: message[index]
    real = linked(axis, name)
    return lambda index: jnp.where(real, message[index].astype(F32), 0.0).astype(BF16)


def shift_z(values, step):
    depth = values.shape[-1]
    lane = lax.broadcasted_iota(jnp.int32, values.shape, values.ndim - 1)
    moved = pltpu.roll(values, (-step) % depth, axis=values.ndim - 1)
    return jnp.where(lane == (depth - 1 if step > 0 else 0), 0.0, moved)


def shift_y(values, step):
    return pltpu.roll(values, (-step) % ROWS, axis=0)


def row_of(ref, index, row):
    return ref[index, pl.ds(row * ROWS, ROWS), :]


COEFFICIENTS = (
    ("own_x", "other_x", "own_y", "other_y", "own_z", "other_z", "cross", "cross_z")
    + ("own_y_down", "other_y_down", "own_z_down", "other_z_down")
)


def coefficients(medium, row, ahead=True):
    def both_of(row):
        return medium(LAME, row) + 2.0 * medium(SHEAR, row)

    shear, lame, inverse = (medium(m, row) for m in (SHEAR, LAME, INV))
    both = both_of(row)
    values = {}
    if ahead:
        values["own_x"] = 0.5 * (both + both_of(row + 1))
        values["other_x"] = 0.5 * (shear + medium(SHEAR, row + 1))
    for tail, step in (("", 1), ("_down", -1)):
        values["own_y" + tail] = 0.5 * (both + shift_y(both, step))
        values["other_y" + tail] = 0.5 * (shear + shift_y(shear, step))
        spacing = 0.25 * (inverse + shift_z(inverse, step))
        values["own_z" + tail] = spacing * (both + shift_z(both, step))
        values["other_z" + tail] = spacing * (shear + shift_z(shear, step))
    values["cross"] = 0.25 * (lame + shear)
    values["cross_z"] = values["cross"] * inverse
    return values


class Event:
    def __init__(self, value):
        self.value = functools.cache(value)
        self.y = functools.cache(lambda c, row, step: shift_y(self.value(c, row), step))
        self.z = functools.cache(lambda c, row, step: shift_z(self.value(c, row), step))

    def slopes(self, c, row):
        return (
            (self.value(c, row + 1) - self.value(c, row - 1))[:8],
            (self.y(c, row, 1) - self.y(c, row, -1))[:8],
            (self.z(c, row, 1) - self.z(c, row, -1))[:8],
        )

    def operator(self, faces, sign=None):
        value = self.value

        def signed(values):
            return values if sign is None else sign * values

        @functools.cache
        def slope(d, row):
            if d == 0:
                return signed(faces("cross", row) * (value(0, row + 1) - value(0, row - 1)))
            if d == 1:
                return faces("cross", row) * (self.y(1, row, 1) - self.y(1, row, -1))
            return faces("cross_z", row) * (self.z(2, row, 1) - self.z(2, row, -1))

        @functools.cache
        def flux_x(c, row):
            kind = "own_x" if c == 0 else "other_x"
            return faces(kind, row) * (value(c, row + 1) - value(c, row))

        def apply(row):
            results = []
            for c in range(3):
                here = value(c, row)
                total = flux_x(c, row) - flux_x(c, row - 1)
                kind = "own_y" if c == 1 else "other_y"
                total = total + (
                    faces(kind, row) * (self.y(c, row, 1) - here)
                    - faces(kind + "_down", row) * (here - self.y(c, row, -1))
                )
                kind = "own_z" if c == 2 else "other_z"
                upright = faces(kind, row) * (self.z(c, row, 1) - here) - faces(
                    kind + "_down", row
                ) * (here - self.z(c, row, -1))
                if c == 0:
                    total = total + signed(
                        (slope(1, row + 1) + slope(2, row + 1))
                        - (slope(1, row - 1) + slope(2, row - 1))
                    )
                elif c == 1:
                    mixed = slope(0, row) + slope(2, row)
                    total = total + (shift_y(mixed, 1) - shift_y(mixed, -1))
                else:
                    mixed = slope(0, row) + slope(1, row)
                    upright = upright + (shift_z(mixed, 1) - shift_z(mixed, -1))
                results.append(total + faces("inverse", row) * upright)
            return results

        return apply


def x_row(up, ring):
    return jnp.where(up, 9 + ring, 2 - ring)


def y_place(up, ring):
    return jnp.where(up, 7 + ring, ROWS - ring)


def tile_row(ref, index, row):
    return ref[pl.ds(index * 64 + (row - 2) * 8, 8), :]


def add_to(sums, key, value):
    sums[key] = sums[key] + value if key in sums else value


def inner_kernel(events, x_rounds, y_rounds, shares, now, base, fwd, med, *refs):
    fields = 3 * events
    x_messages, refs = refs[: len(x_rounds)], refs[len(x_rounds) :]
    y_messages, refs = refs[: len(y_rounds)], refs[len(y_rounds) :]
    near = one_sided(x_rounds)
    if near:
        here, start, medium, coef, then, slabs, slopes, stored, part = refs[-9:]
    else:
        here, start, stored, medium, coef, then, part = refs[-7:]

    for f in range(fields):
        e, c = f // 3, f % 3
        for x in range(8):
            spot = pl.ds((x + 2) * ROWS, 8)
            here[f, spot, :] = now[pl.ds(f * 64 + x * 8, 8), :]
            start[f, spot, :] = base[pl.ds(f * 64 + x * 8, 8), :]
            for t in range(2):
                stored[2 * f + t, spot, :] = fwd[(e * 4 + t + 1) * 3 + c, x].astype(F32)
    for m in range(4):
        for x in range(8):
            medium[m, pl.ds((x + 2) * ROWS, 8), :] = med[pl.ds(m * 64 + x * 8, 8), :]

    targets = {"field": here, "base": start, "wave": stored, "medium": medium}
    parts = face_parts(fields)

    def place(tile, put):
        whole = functools.cache(lambda k: tile(k).astype(F32))
        for k, (kind, index, ring, remainder) in enumerate(parts):
            if remainder:
                continue
            value = whole(k // 2)[8 * (k % 2) :][:8]
            if parts[k + 1 : k + 2] == [(kind, index, ring, True)]:
                value = value + whole((k + 1) // 2)[8 * ((k + 1) % 2) :][:8]
            put(targets[kind], index, ring, value)

    def nothing(_):
        return jnp.zeros((16, 128), BF16)

    if near:
        zeros = jnp.zeros((ROWS, 128), F32)
        for row in (0, 1, 10, 11):
            spot = pl.ds(row * ROWS, ROWS)
            for f in range(fields):
                here[f, spot, :] = zeros
                start[f, spot, :] = zeros
            for m in range(4):
                medium[m, spot, :] = zeros
        for row in (1, 10):
            for k in range(2 * fields):
                stored[k, pl.ds(row * ROWS, 8), :] = zeros[:8]
    for k, name in enumerate("A" if near else "AB"):
        up = upward("gx", name)

        def put_x(ref, index, ring, values, up=up):
            row = pl.multiple_of(x_row(up, ring) * ROWS, ROWS)
            ref[index, pl.ds(row, 8), :] = values

        if name == "A" and their_turn(x_rounds, y_rounds):
            for message, when in (
                (y_messages[1], is_first()),
                (x_messages[0], jnp.logical_not(is_first())),
            ):
                pl.when(when)(functools.partial(place, masked(message, "gx", name), put_x))
        else:
            place(masked(x_messages[k], "gx", name) if k < len(x_rounds) else nothing, put_x)
    for k, name in enumerate("AB"):
        up = upward("gy", name)

        def put_y(ref, index, ring, values, up=up):
            ref[index, pl.ds(2 * ROWS + y_place(up, ring), 8, stride=ROWS), :] = values

        place(masked(y_messages[k], "gy", name) if k < len(y_rounds) else nothing, put_y)

    for row in range(1, 11):
        values = coefficients(lambda m, r: row_of(medium, m, r), row, row < 10)
        for name, value in values.items():
            if 1 < row < 10 or name in ("own_x", "other_x", "cross", "cross_z"):
                coef[COEFFICIENTS.index(name), pl.ds(row * ROWS, ROWS), :] = value

    def faces(name, row):
        if name == "inverse":
            return row_of(medium, INV, row)
        return row_of(coef, COEFFICIENTS.index(name), row)

    sums = {}
    for e in range(events):
        first = Event(lambda c, row, e=e: row_of(here, 3 * e + c, row))
        apply = first.operator(faces)
        waves = [
            Event(lambda c, row, e=e, t=t: row_of(stored, 2 * (3 * e + c) + t, row))
            for t in range(2)
        ]
        for row in range(2, 10):
            if near or 3 <= row <= 8:
                scale = STEP_FACTOR * row_of(medium, BUOY, row)
                for c, result in enumerate(apply(row)):
                    f = 3 * e + c
                    then[f, pl.ds(row * ROWS, ROWS), :] = row_of(start, f, row) + scale * result
            gather(sums, first, waves[0], fwd, e, 0, row)
        second = Event(lambda c, row, e=e: row_of(then, 3 * e + c, row))
        for row in range(4, 8):
            gather(sums, second, waves[1], fwd, e, 1, row)
    for row in range(2, 10):
        inverse = tile_row(med, INV, row)
        shear = sums["lateral", row] + inverse * inverse * sums["upright", row]
        part[pl.ds((row - 2) * 8, 8), :] = -0.25 * shear
        part[pl.ds(64 + (row - 2) * 8, 8), :] = -sums["density", row]
    if near:
        mirror, sums = Mirror(), {}
        for f in range(fields):
            then[f, pl.ds(pl.multiple_of(mirror.row(1) * ROWS, ROWS), ROWS), :] = zeros
        for e in range(events):
            second = Event(lambda c, row, e=e: mirror.of(then, 3 * e + c, row))
            wave = Event(lambda c, row, e=e: mirror.of(stored, 2 * (3 * e + c) + 1, row))
            for row in (2, 3):
                gather(sums, second, wave, fwd, e, 1, row, mirror.row(row) - 2)
            for row in (8, 9):
                for c in range(3):
                    terms = (*wave.slopes(c, row), bend_of(wave, fwd, e, 1, c, row, mirror.row(row) - 2))
                    for k, term in enumerate(terms):
                        slopes[slope_place(events, e, c, row, k), :] = term
        for row in (2, 3):
            mirror.add(part, sums, med, row)
        cut([part[pl.ds(8 * k, 8), :] for k in range(16)], shares, slabs)


def bend_of(wave, fwd, e, t, c, row, x):
    newer = fwd[(e * 4 + t) * 3 + c, x].astype(F32)
    older = fwd[(e * 4 + t + 2) * 3 + c, x].astype(F32)
    return newer - 2.0 * wave.value(c, row)[:8] + older


def slope_place(events, e, c, row, k):
    return pl.ds((((row - 8) * events + e) * 3 + c) * 32 + k * 8, 8)


def gather(sums, field, wave, fwd, e, t, row, x=None):
    x = row - 2 if x is None else x
    for c in range(3):
        terms = (*wave.slopes(c, row), bend_of(wave, fwd, e, t, c, row, x))
        gather_terms(sums, field, terms, c, row)


def gather_terms(sums, field, terms, c, row):
    ax, ay, az = field.slopes(c, row)
    ux, uy, uz, bend = terms
    add_to(sums, ("lateral", row), ax * ux + ay * uy)
    add_to(sums, ("upright", row), az * uz)
    add_to(sums, ("density", row), field.value(c, row)[:8] * bend)


def one_sided(x_rounds):
    return x_rounds == "A" and lax.axis_size("gx") == 2


class Mirror:
    def __init__(self):
        self.up = upward("gx", "A")
        self.sign = jnp.where(self.up, 1.0, -1.0)
        self.row = functools.cache(lambda r: jnp.where(self.up, r, 11 - r))

    def of(self, ref, index, row):
        start = pl.multiple_of(self.row(row) * ROWS, ROWS)
        return ref[index, pl.ds(start, ROWS), :]

    def tile(self, index, row):
        return pl.ds(pl.multiple_of(index * 64 + (self.row(row) - 2) * 8, 8), 8)

    def terms(self, sums, med, row):
        inverse = med[self.tile(INV, row), :]
        more = sums["lateral", row] + inverse * inverse * sums["upright", row]
        return -0.25 * more, -sums["density", row]

    def add(self, part, sums, med, row):
        for index, value in enumerate(self.terms(sums, med, row)):
            spot = self.tile(index, row)
            part[spot, :] = part[spot, :] + value


OUTER = (0, 1, 10, 11)
EDGES = (1, 2, 9, 10)


def edge_kernel(events, x_rounds, y_rounds, shares, *refs):
    fields = 3 * events
    count = len(x_rounds) * len(y_rounds)
    corners, refs = refs[:count], refs[count:]
    (here, start, stored, medium, coef, then, part, fwd, med), refs = refs[:9], refs[9:]
    edge, own_share, *sent = refs[: 1 + shares]
    outer, outer_start, outer_medium, outer_coef, spread, slabs = refs[1 + shares :]

    height = len(OUTER) * ROWS
    for k, row in enumerate(OUTER):
        for f in range(fields):
            spot = pl.ds(f * height + k * ROWS, ROWS)
            outer[spot, :] = row_of(here, f, row)
            if row in EDGES:
                outer_start[spot, :] = row_of(start, f, row)
        for m in range(4):
            outer_medium[pl.ds(m * height + k * ROWS, ROWS), :] = row_of(medium, m, row)
    for kx, name_x in enumerate("AB"):
        for ky, name_y in enumerate("AB"):
            corner = None
            if kx < len(x_rounds) and ky < len(y_rounds):
                corner = corners[kx * len(y_rounds) + ky]
            up_x, up_y = upward("gx", name_x), upward("gy", name_y)
            real = jnp.logical_and(linked("gx", name_x), linked("gy", name_y))

            def put(kind, ring_x, ring_y, values):
                place = jnp.where(up_x, 1 + ring_x, 2 - ring_x)
                spot = pl.ds(place * ROWS + y_place(up_y, ring_y), values.shape[0], stride=height)
                {"field": outer, "base": outer_start, "medium": outer_medium}[kind][spot, :] = values

            take_corner(fields, corner, real, spread, put)

    def outer_or(ref, full):
        def pick(index, row):
            if row in OUTER:
                return ref[pl.ds(index * height + OUTER.index(row) * ROWS, ROWS), :]
            return row_of(full, index, row)

        return pick

    field_row, start_row = outer_or(outer, here), outer_or(outer_start, start)
    medium_row = outer_or(outer_medium, medium)
    fresh = (0, 1, 9, 10, 11)
    for k, row in enumerate(fresh):
        for name, value in coefficients(medium_row, row, row < 11).items():
            outer_coef[COEFFICIENTS.index(name), pl.ds(k * ROWS, ROWS), :] = value

    def faces(name, row):
        if name == "inverse":
            return medium_row(INV, row)
        index = COEFFICIENTS.index(name)
        if row in fresh:
            return row_of(outer_coef, index, fresh.index(row))
        return row_of(coef, index, row)

    def then_row(f, row):
        if row in EDGES:
            return row_of(edge, f, EDGES.index(row))
        return row_of(then, f, row)

    sums = {}
    for e in range(events):
        apply = Event(lambda c, row, e=e: field_row(3 * e + c, row)).operator(faces)
        for k, row in enumerate(EDGES):
            scale = STEP_FACTOR * medium_row(BUOY, row)
            for c, result in enumerate(apply(row)):
                f = 3 * e + c
                edge[f, pl.ds(k * ROWS, ROWS), :] = start_row(f, row) + scale * result
        second = Event(lambda c, row, e=e: then_row(3 * e + c, row))
        wave = Event(lambda c, row, e=e: row_of(stored, 2 * (3 * e + c) + 1, row))
        for row in (2, 3, 8, 9):
            gather(sums, second, wave, fwd, e, 1, row)
    grads = [[], []]
    for row in range(2, 10):
        shear, density = tile_row(part, 0, row), tile_row(part, 1, row)
        if row in (2, 3, 8, 9):
            inverse = tile_row(med, INV, row)
            more = sums["lateral", row] + inverse * inverse * sums["upright", row]
            shear = shear - 0.25 * more
            density = density - sums["density", row]
        grads[0].append(shear)
        grads[1].append(density)
    cut(grads[0] + grads[1], shares, slabs)
    deal(shares, slabs, own_share, sent)


def cut(grads, shares, slabs):
    piece = 128 // shares
    quarter = lax.broadcasted_iota(jnp.int32, (8, 128), 1) // piece
    per = len(grads) // shares
    for j in range(shares):
        for r in range(per):
            tile = None
            for g in range(shares):
                source = grads[r * shares + g]
                moved = pltpu.roll(source, ((g - j) * piece) % 128, axis=1) if g != j else source
                tile = moved if tile is None else jnp.where(quarter == g, moved, tile)
            slabs[j, pl.ds(r * 8, 8), :] = tile


def deal(shares, slabs, own_share, sent):
    me = lax.axis_index("ev")
    own_share[...] = slabs[me]
    for m in range(1, shares):
        sent[m - 1][...] = slabs[me ^ m]


def near_kernel(events, x_rounds, y_rounds, shares, *refs):
    fields = 3 * events
    corners, refs = refs[: len(y_rounds)], refs[len(y_rounds) :]
    (here, start, medium, coef, then, ready, slopes, med), refs = refs[:8], refs[8:]
    edge, own_share, *sent = refs[: 1 + shares]
    outer, outer_start, outer_medium, outer_coef, spread, slabs = refs[1 + shares :]
    mirror = Mirror()

    height = 2 * ROWS
    for f in range(fields):
        outer_start[pl.ds(f * ROWS, ROWS), :] = mirror.of(start, f, 10)
    for k, row in enumerate((10, 11)):
        for f in range(fields):
            outer[pl.ds(f * height + k * ROWS, ROWS), :] = mirror.of(here, f, row)
        for m in range(4):
            outer_medium[pl.ds(m * height + k * ROWS, ROWS), :] = mirror.of(medium, m, row)
    for corner, name in zip(corners, y_rounds):
        up_y, real = upward("gy", name), linked("gy", name)

        def put(kind, ring_x, ring_y, values):
            place = y_place(up_y, ring_y)
            count = values.shape[0]
            if kind == "base":
                outer_start[pl.ds(place, count, stride=ROWS), :] = values
            else:
                target = outer if kind == "field" else outer_medium
                target[pl.ds((ring_x - 1) * ROWS + place, count, stride=height), :] = values

        take_corner(fields, corner, real, spread, put)

    def row_with(ref, full):
        def pick(index, row):
            if row >= 10:
                return ref[pl.ds(index * height + (row - 10) * ROWS, ROWS), :]
            return mirror.of(full, index, row)

        return pick

    field_row, medium_row = row_with(outer, here), row_with(outer_medium, medium)
    for k, row in enumerate((9, 10, 11)):
        for name, value in coefficients(medium_row, row, row < 11).items():
            if row == 10 or name in (("own_x", "other_x") if row == 9 else ("cross", "cross_z")):
                outer_coef[COEFFICIENTS.index(name), pl.ds(k * ROWS, ROWS), :] = value

    def faces(name, row):
        if name == "inverse":
            return medium_row(INV, row)
        index = COEFFICIENTS.index(name)
        along_x = name in ("own_x", "other_x")
        if row >= (9 if along_x else 10):
            return row_of(outer_coef, index, row - 9)
        first = jnp.where(mirror.up, row, 10 - row) if along_x else mirror.row(row)
        return coef[index, pl.ds(pl.multiple_of(first * ROWS, ROWS), ROWS), :]

    def slot(row):
        up, down = EDGES.index(row), EDGES.index(11 - row)
        return pl.ds(pl.multiple_of(jnp.where(mirror.up, up, down) * ROWS, ROWS), ROWS)

    def then_row(f, row):
        return edge[f, slot(row), :] if row > 8 else mirror.of(then, f, row)

    sums = {}
    for e in range(events):
        apply = Event(lambda c, row, e=e: field_row(3 * e + c, row)).operator(faces, mirror.sign)
        for row in (9, 10):
            scale = STEP_FACTOR * medium_row(BUOY, row)
            for c, result in enumerate(apply(row)):
                f = 3 * e + c
                first = outer_start[pl.ds(f * ROWS, ROWS), :] if row == 10 else mirror.of(start, f, 9)
                edge[f, slot(row), :] = first + scale * result
                edge[f, slot(11 - row), :] = mirror.of(then, f, 11 - row)
        second = Event(lambda c, row, e=e: then_row(3 * e + c, row))
        for row in (8, 9):
            for c in range(3):
                terms = [slopes[slope_place(events, e, c, row, k), :] for k in range(4)]
                gather_terms(sums, second, terms, c, row)
    piece = 128 // shares
    quarter = lax.broadcasted_iota(jnp.int32, (8, 128), 1) // piece
    slabs[...] = ready[...]
    rows = {row: mirror.terms(sums, med, row) for row in (8, 9)}
    for index in range(2):
        tile = index * (8 // shares) + (mirror.row(9) - 2) // shares
        spot = pl.ds(pl.multiple_of(tile * 8, 8), 8)
        for j in range(shares):
            values = slabs[j, spot, :]
            for row in (8, 9):
                g = lax.rem(mirror.row(row) - 2, shares)
                moved = pltpu.roll(rows[row][index], lax.rem((g - j + shares) * piece, 128), axis=1)
                values = values + jnp.where(quarter == g, moved, 0.0)
            slabs[j, spot, :] = values
    deal(shares, slabs, own_share, sent)


def second_kernel(events, now, med, cells, force, medium, coef, then, edge, mid, after):
    rows = [force[e, 1, c, 0] for e in range(events) for c in range(3)]
    pushed = force_field(cells[0], rows, 64)

    def faces(name, row):
        if name == "inverse":
            return row_of(medium, INV, row)
        return row_of(coef, COEFFICIENTS.index(name), row)

    def then_row(f, row):
        if row in EDGES:
            return row_of(edge, f, EDGES.index(row))
        return row_of(then, f, row)

    for e in range(events):
        apply = Event(lambda c, row, e=e: then_row(3 * e + c, row)).operator(faces)
        for row in range(2, 10):
            scale = STEP_FACTOR * tile_row(med, BUOY, row)
            for c, result in enumerate(apply(row)):
                f = 3 * e + c
                first = f * 64 + (row - 2) * 8
                spot = pl.ds(first, 8)
                current = then_row(f, row)[:8]
                mid[spot, :] = current
                after[spot, :] = (
                    2.0 * current - now[spot, :] + scale * (result[:8] + pushed[first : first + 8])
                )


def finish_kernel(shares, scale, *refs):
    pieces, (shear, density) = refs[:shares], refs[shares:]
    total = pieces[0][...]
    for piece in pieces[1:]:
        total = total + piece[...]
    width = 128 // shares
    for v in range(16):
        g, r = v % shares, v // shares
        tile = total[r * 8 : (r + 1) * 8]
        if g:
            tile = pltpu.roll(tile, (-g * width) % 128, axis=1)
        out = shear if v < 8 else density
        out[pl.ds((v % 8) * 8, 8), :] = tile[:, :width] * scale


def call(kernel, outs, ins, scratch=(), name=None, cost=1000, out_memory=pltpu.VMEM, pinned=False):
    return pl.pallas_call(
        kernel,
        out_shape=[pltpu.VMEM(s, d) if pinned else jax.ShapeDtypeStruct(s, d) for s, d in outs],
        in_specs=[pl.BlockSpec(memory_space=m) for m in ins],
        out_specs=[pl.BlockSpec(memory_space=out_memory)] * len(outs),
        scratch_shapes=[s if not isinstance(s, tuple) else pltpu.VMEM(*s) for s in scratch],
        compiler_params=pltpu.CompilerParams(vmem_limit_bytes=VMEM_LIMIT),
        cost_estimate=pl.CostEstimate(
            flops=cost * 1024, bytes_accessed=cost * 1024, transcendentals=0
        ),
        name=name,
    )


def wait_for(before, messages):
    arrays = [*before, *messages]
    return call(
        lambda *refs: None,
        [((8, 128), F32)],
        [pl.ANY] * len(arrays),
        name="arrival",
        out_memory=pl.ANY,
        cost=8000,
    )(*arrays)


def body(adjoint_now, adjoint_prev, forward, medium, drm_cells, drm_force):
    events, _, width_x, width_y, depth = adjoint_now.shape
    fields = 3 * events
    tile = width_x * width_y
    shares = lax.axis_size("ev")
    x_rounds, y_rounds = rounds_of(lax.axis_size("gx")), rounds_of(lax.axis_size("gy"))
    flat = ((fields * tile, depth), F32)
    tall = 12 * ROWS

    face = (((len(face_parts(fields)) + 1) // 2, 16, depth), BF16)
    wide_fields = padded(fields)
    _, corner_rows, spread_rows = corner_layout(fields)
    corner, spread = ((corner_rows, depth), BF16), ((spread_rows, depth), F32)
    roomy = (((wide_fields + 1) * tile, depth), F32)
    inputs = [
        adjoint_now.reshape(flat[0]),
        adjoint_prev.reshape(flat[0]),
        forward.reshape(events, 12, width_x, width_y, depth),
        medium.reshape(4 * tile, depth),
        drm_cells,
        drm_force,
    ]
    now, fwd, med, cells, force, base, *messages = call(
        functools.partial(pack_kernel, events, x_rounds, y_rounds),
        [roomy, (inputs[2].shape, BF16), ((9 * tile, depth), F32)]
        + [(a.shape, a.dtype) for a in inputs[4:]]
        + [roomy]
        + [face] * (len(y_rounds) + len(x_rounds))
        + [corner] * (len(x_rounds) * len(y_rounds)),
        [pltpu.HBM] * len(inputs),
        [
            flat,
            (((2 * fields + 1) * tile, depth), F32),
            spread,
            pltpu.SemaphoreType.DMA((8,)),
        ],
        "pack",
        cost=8000,
        pinned=True,
    )(*(pltpu.with_memory_space_constraint(a, pltpu.HBM) for a in inputs))
    kinds = [{"gy": r} for r in y_rounds] + [{"gx": r} for r in x_rounds]
    kinds += [{"gx": x, "gy": y} for x in x_rounds for y in y_rounds]
    fwd = fwd.reshape(events * 12, width_x, width_y, depth)
    turn = their_turn(x_rounds, y_rounds)
    received = [
        swap(message, kind, turn and kind == {"gy": "B"}, turn and kind == {"gx": "A"})
        for message, kind in zip(messages, kinds)
    ]
    y_messages, rest = received[: len(y_rounds)], received[len(y_rounds) :]
    x_messages, corners = rest[: len(x_rounds)], rest[len(x_rounds) :]
    order = [y_messages[1], y_messages[0]] if turn else [*x_messages[:1], *y_messages[:1]]
    arrival = ()
    for message in order:
        arrival = wait_for(arrival, [message])

    wide = ((fields, tall, depth), F32)
    slab = ((16 // shares * 8, depth), F32)
    whole, near = ((2 * tile, depth), F32), one_sided(x_rounds)
    waves = ((2 * fields, tall, depth), F32)
    results = call(
        functools.partial(inner_kernel, events, x_rounds, y_rounds, shares),
        [wide, wide]
        + ([] if near else [waves])
        + [((4, tall, depth), F32), ((len(COEFFICIENTS), tall, depth), F32), wide]
        + ([((shares,) + slab[0], F32), ((fields * 64, depth), F32)] if near else [whole]),
        [pltpu.VMEM] * (4 + len(x_messages) + len(y_messages)) + [pl.ANY] * len(arrival),
        [waves, whole] if near else (),
        name="inner",
        cost=3000,
    )(now, base, fwd, med, *x_messages, *y_messages, *arrival)
    outer = ((fields, len(OUTER) * ROWS, depth), F32)
    if near:
        edge_step, each, fresh, operands = near_kernel, (2, 1, 2), 3, [*results, med]
        _, _, tall_medium, coef, then, *_ = results
    else:
        edge_step, each, fresh, operands = edge_kernel, (len(OUTER),) * 3, 5, [*results, fwd, med]
        _, _, _, tall_medium, coef, then, _ = results
    room = [wide_fields + 1, wide_fields + 1, 9]
    edge, own_share, *sent = call(
        functools.partial(edge_step, events, x_rounds, y_rounds, shares),
        [outer] + [slab] * shares,
        [pltpu.VMEM] * (len(operands) + len(corners)),
        [
            *(((count * rows * ROWS, depth), F32) for count, rows in zip(room, each)),
            ((len(COEFFICIENTS), fresh * ROWS, depth), F32),
            spread,
            ((shares,) + slab[0], F32),
        ],
        "edges",
    )(*corners, *operands)
    pieces = [own_share]
    for m in reversed(range(1, shares)):
        pairs = [(i, i ^ m) for i in range(shares)]
        pieces.append(lax.ppermute(sent[m - 1], "ev", pairs))
    mid, after = call(
        functools.partial(second_kernel, events),
        [flat, flat],
        [pltpu.VMEM] * 8,
        name="second",
    )(now, med, cells, force, tall_medium, coef, then, edge)
    shear, density = call(
        functools.partial(finish_kernel, shares, 1.0 / (events * shares)),
        [((tile, depth // shares), F32)] * 2,
        [pltpu.VMEM] * shares,
        name="finish",
    )(*pieces)
    shape = adjoint_now.shape
    grad = (width_x, width_y, depth // shares)
    return mid.reshape(shape), after.reshape(shape), shear.reshape(grad), density.reshape(grad)


def solution(mesh):
    in_specs = (
        P("ev", None, "gx", "gy", None),
        P("ev", None, "gx", "gy", None),
        P("ev", None, None, "gx", "gy", None),
        P(None, "gx", "gy", None),
        P("gx", "gy", None),
        P("ev", None, None, "gx", "gy", None),
    )
    out_specs = (
        P("ev", None, "gx", "gy", None),
        P("ev", None, "gx", "gy", None),
        P("gx", "gy", "ev"),
        P("gx", "gy", "ev"),
    )
    return jax.shard_map(body, mesh=mesh, in_specs=in_specs, out_specs=out_specs, check_vma=False)
```
